32 devices in a mesh: grp: 2 (over y), tp: 4 (over z), kv: 4 (over x, core).
Axes of the slice: x: 2, y: 2, z: 4, core: 2. Of those that a mesh axis runs over, the one named last changes fastest.
Arguments:
- states: bfloat16 [8, 8192], P('grp', 'tp'), parts along dimension 0, may hold values from -3000 to 3000
- norm_gains: float32 [2, 8192], P(None, 'tp'), may hold values from 0.1 to 1.9
- w_query: bfloat16 [8192, 32, 128], P('tp', 'kv'), may hold values from -0.0625 to 0.0625
- w_keyval: bfloat16 [8192, 4, 256], P('tp', 'kv'), may hold values from -0.0625 to 0.0625
- w_out: bfloat16 [4096, 8192], P('kv', 'tp'), may hold values from -0.5 to 0.5
- w_gate_up: bfloat16 [8192, 2, 14336], P('tp', None, 'kv'), may hold values from -0.0625 to 0.0625
- w_down: bfloat16 [14336, 8192], P('kv', 'tp'), may hold values from -0.046875 to 0.046875
- kv_cache: bfloat16 [8, 8192, 4, 256], P(('grp', 'tp'), None, 'kv'), parts along dimension 0, may hold values from -2000 to 2000
- lengths: int32 [8], P('grp'), parts along dimension 0, may hold values from 2048 to 8192, as said below
- owner_rows: int32 [8], P('grp'), parts along dimension 0, may hold values from 0 to 3, each once
Outputs:
- attn_out: bfloat16 [8, 8192], P('grp', 'tp'), parts along dimension 0
- ffn_out: bfloat16 [8, 8192], P('grp', 'tp'), parts along dimension 0
- new_kv: bfloat16 [8, 4, 256], P(('grp', 'tp'), 'kv'), parts along dimension 0
The draws below stay inside these ranges and needn't reach their ends.
There are 2 independent parts, one for each index of `grp`. The reference program is written for one: setup_inputs(seed, part) draws one part's arguments, and reference() takes and returns one part's arrays. A program takes and returns all parts, laid end to end along the dimension named above; an argument that names none is the same for every part. Nothing has to cross between parts.
Inputs may be any that keep to these rules, and one draw needn't show every extreme that they name: `lengths`: some document has exactly 8192 cached tokens. `owner_rows`: A permutation of the documents.
All inputs are finite; a program needn't handle non-finite values.
Results may differ from the reference program's by a relative error of at most 0.0165.
The reference program's roundings to bfloat16 on the way count: a program that leaves them out, or rounds other values in their place, can miss the bound.
Values may be sent and summed in bfloat16 or wider, within the bound.
No kernel may reach another device: no remote copies, remote signals or barrier semaphores. Data moves between devices by JAX's collectives and lax.ppermute only.
A program may use at most 256 MiB of HBM per device.

```python
import math
import jax
import jax.numpy as jnp
from jax import lax

D = 8192
HQ = 32
KVH = 4
HS = 128
FF = 14336
LMAX = 8192
MIN_LEN = 2048
DOCS = 4


def draw_states(key, part):
    key = jax.random.fold_in(key, 11)
    keys_all = jax.random.split(key, 2)
    column = jnp.arange(D, dtype=jnp.float32)[None, :] / D
    row_scale = jnp.exp(jax.random.uniform(keys_all[0], (DOCS, 1), minval=0.0, maxval=math.log(10.0)))
    column_scale = jnp.power(10.0, 0.5 * column)
    values = jax.random.normal(keys_all[1], (DOCS, D)) * row_scale * column_scale
    return values.astype(jnp.bfloat16)


def draw_kv_cache(key, part):
    key = jax.random.fold_in(key, 23)
    keys_all = jax.random.split(key, 2)
    shape = (DOCS, LMAX, KVH, HS)
    cached_keys = jax.random.normal(keys_all[0], shape) * 2.0
    cached_values = jax.random.normal(keys_all[1], shape)
    return jnp.concatenate([cached_keys, cached_values], axis=-1).astype(jnp.bfloat16)


def draw_lengths(key, part):
    key = jax.random.fold_in(key, 37)
    keys_all = jax.random.split(key, 2)
    values = jax.random.randint(keys_all[0], (DOCS,), MIN_LEN, LMAX + 1)
    longest = jax.random.randint(keys_all[1], (), 0, DOCS)
    return jnp.where(jnp.arange(DOCS) == longest, LMAX, values).astype(jnp.int32)


def levels(rng, shape, shards, least, top_value):
    def one(dim, blocks):
        heights = jax.random.uniform(jax.random.fold_in(jax.random.fold_in(rng, 6), dim), (blocks,), jnp.float32, least / len(shards), top_value / len(shards))
        return jnp.repeat(jnp.exp(heights), shape[dim] // blocks).reshape((-1,) + (1,) * (len(shape) - dim - 1))

    level = one(*shards[0])
    for cut in shards[1:]:
        level = level * one(*cut)
    return level


def centred(key, shape, deviation, most, shards=(), kind=jnp.bfloat16):
    drawn = deviation * jax.random.normal(key, shape, jnp.float32)
    if shards:
        drawn = drawn * levels(key, shape, shards, -0.22, 0.18)
    return jnp.clip(drawn, -most, most).astype(kind)


def setup_inputs(seed: int = 0, part: int = 0) -> dict:
    keys = jax.random.split(jax.random.key(seed), 11)
    own_keys = jax.random.split(jax.random.fold_in(keys[10], part), 11)
    return {
        "states": draw_states(jax.random.fold_in(jax.random.fold_in(keys[10], part), 71), part),
        "norm_gains": jnp.clip(1.0 + 0.18 * jax.random.normal(keys[1], (2, D), jnp.float32), 0.1, 1.9),
        "w_query": centred(keys[2], (D, HQ, HS), D ** -0.5, 0.0625, ((0, 4), (1, 4))),
        "w_keyval": centred(keys[3], (D, KVH, 2 * HS), D ** -0.5, 0.0625, ((0, 4), (1, 4))),
        "w_out": centred(keys[4], (HQ * HS, D), HS ** -0.5, 0.5, ((0, 4), (1, 4))),
        "w_gate_up": centred(keys[5], (D, 2, FF), D ** -0.5, 0.0625, ((0, 4), (2, 4))),
        "w_down": centred(keys[6], (FF, D), FF ** -0.5, 0.046875, ((0, 4), (1, 4))),
        "kv_cache": draw_kv_cache(jax.random.fold_in(jax.random.fold_in(keys[10], part), 71), part),
        "lengths": draw_lengths(jax.random.fold_in(jax.random.fold_in(keys[10], part), 71), part),
        "owner_rows": jax.random.permutation(own_keys[9], DOCS).astype(jnp.int32),
    }


eps_norm = 1e-05
rope_base = 500000.0

def rotate(values, places):
    extent = values.shape[-1]
    midway = extent // 2
    frequency = jnp.power(jnp.float32(rope_base), -(jnp.arange(midway, dtype=jnp.float32) * 2.0 / extent))
    angles = places.astype(jnp.float32)[:, None] * frequency[None, :]
    cosine = jnp.cos(angles)[:, None, :]
    sines = jnp.sin(angles)[:, None, :]
    leading = values[..., :midway]
    trailing = values[..., midway:]
    return jnp.concatenate([leading * cosine - trailing * sines, trailing * cosine + leading * sines], axis=-1)

def normalize(inputs, gain):
    mean_sq = lax.optimization_barrier(jnp.mean(inputs * inputs, axis=1, keepdims=True))
    return (inputs * lax.rsqrt(mean_sq + eps_norm) * gain[None, :]).astype(jnp.bfloat16)

def attend(slot_items):
    cache_one, query_one, fresh_one, length_one = slot_items
    groups = fresh_one.shape[0]
    head_dim = fresh_one.shape[1] // 2
    score_scale = head_dim ** (-0.5)
    query_f = query_one.astype(jnp.float32).reshape(groups, -1, head_dim)
    cached_keys = cache_one[..., :head_dim].astype(jnp.float32)
    cached_values = cache_one[..., head_dim:].astype(jnp.float32)
    scores = jnp.einsum('hgd,lhd->hgl', query_f, cached_keys, precision=lax.Precision.HIGHEST) * score_scale
    attended_mask = jnp.arange(cache_one.shape[0], dtype=jnp.int32) < length_one
    scores = jnp.where(attended_mask[None, None, :], scores, -jnp.inf)
    own_score = jnp.einsum('hgd,hd->hg', query_f, fresh_one[:, :head_dim].astype(jnp.float32), precision=lax.Precision.HIGHEST) * score_scale
    highest = jnp.maximum(lax.optimization_barrier(jnp.max(scores, axis=-1)), own_score)
    weights = jnp.exp(scores - highest[..., None])
    own_weight = jnp.exp(own_score - highest)
    totals = lax.optimization_barrier(jnp.sum(weights, axis=-1)) + own_weight
    rounded = lax.optimization_barrier((weights.astype(jnp.bfloat16), own_weight.astype(jnp.bfloat16)))
    weighted = jnp.einsum('hgl,lhd->hgd', rounded[0].astype(jnp.float32), cached_values, precision=lax.Precision.HIGHEST)
    weighted = weighted + rounded[1].astype(jnp.float32)[..., None] * fresh_one[:, head_dim:].astype(jnp.float32)[:, None, :]
    return (weighted / totals[..., None]).astype(jnp.bfloat16).reshape(-1)

def reference(states, norm_gains, w_query, w_keyval, w_out, w_gate_up, w_down, kv_cache, lengths, owner_rows):
    inputs = states.astype(jnp.float32)
    normed = normalize(inputs, norm_gains[0])
    queries = jnp.dot(normed, w_query.reshape(D, HQ * HS), preferred_element_type=jnp.float32).reshape(DOCS, HQ, HS)
    keyvals = jnp.dot(normed, w_keyval.reshape(D, KVH * 2 * HS), preferred_element_type=jnp.float32).reshape(DOCS, KVH, 2 * HS)
    queries = jnp.take(queries, owner_rows, axis=0)
    keyvals = jnp.take(keyvals, owner_rows, axis=0)
    places = jnp.take(lengths, owner_rows, axis=0)
    rotated = rotate(queries, places).astype(jnp.bfloat16)
    new_kv = jnp.concatenate([rotate(keyvals[..., :HS], places), keyvals[..., HS:]], axis=-1).astype(jnp.bfloat16)
    heads = lax.map(attend, (kv_cache, rotated, new_kv, places))
    ordered = jnp.zeros_like(heads).at[owner_rows].set(heads)
    attn_out = jnp.dot(ordered, w_out, preferred_element_type=jnp.float32).astype(jnp.bfloat16)
    resid = (inputs + attn_out.astype(jnp.float32)).astype(jnp.bfloat16)
    normed_two = normalize(resid.astype(jnp.float32), norm_gains[1])
    gate_up = jnp.dot(normed_two, w_gate_up.reshape(D, 2 * FF), preferred_element_type=jnp.float32).reshape(DOCS, 2, FF)
    active = (jax.nn.silu(gate_up[:, 0]) * gate_up[:, 1]).astype(jnp.bfloat16)
    ffn_out = jnp.dot(active, w_down, preferred_element_type=jnp.float32).astype(jnp.bfloat16)
    return (attn_out, ffn_out, new_kv)
```

```python
import functools
import math

import jax
import jax.numpy as jnp
import numpy as np
from jax import lax
from jax.experimental import pallas as pl
from jax.experimental.pallas import tpu as pltpu
from jax.sharding import PartitionSpec as P

D = 8192
EPS = 1e-05
ROPE_BASE = 500000.0
LANES = 128
MIB = 1 << 20
GU_BLOCK = 256
F32 = jnp.float32
BF16 = jnp.bfloat16
TURN_A = 6.28125
TURN_B = 0.0019340515136718750
TURN_C = 2.0 * math.pi - TURN_A - TURN_B


def vmem():
    return pl.BlockSpec(memory_space=pltpu.VMEM)


def smem():
    return pl.BlockSpec(memory_space=pltpu.SMEM)


def hbm():
    return pl.BlockSpec(memory_space=pl.ANY)


def exchange(arrays, axis, size):
    return [arrays[0]] + [
        lax.ppermute(arrays[s], axis, [(i, i ^ s) for i in range(size)])
        for s in range(1, size)
    ]


def tree_sum(parts):
    while len(parts) > 1:
        parts = [a + b for a, b in zip(parts[::2], parts[1::2])]
    return parts[0]


def two_parts(scaled):
    high = scaled.astype(BF16).astype(F32)
    low = scaled - high
    return jnp.concatenate([high, high, low, low], axis=0).astype(BF16)


def spread(rows16, out_ref, docs):
    width = rows16.shape[1]
    source = lax.broadcasted_iota(jnp.int32, (LANES, 2 * LANES), 0)
    target = lax.broadcasted_iota(jnp.int32, (LANES, 2 * LANES), 1)
    pick = (lax.shift_right_logical(target, 1) == source).astype(F32).astype(BF16)
    row = lax.broadcasted_iota(jnp.int32, (4 * docs, 2 * LANES), 0)
    lane = lax.broadcasted_iota(jnp.int32, (4 * docs, 2 * LANES), 1)
    keep = lax.rem(lax.div(row, docs), 2) == lax.rem(lane, 2)
    for c in range(width // LANES):
        doubled = jnp.dot(
            rows16[:, c * LANES : (c + 1) * LANES], pick, preferred_element_type=F32
        )
        out_ref[:, 2 * c * LANES : 2 * (c + 1) * LANES] = jnp.where(keep, doubled, 0.0).astype(BF16)


def pick_row(ref, index):
    row = lax.broadcasted_iota(jnp.int32, ref.shape, 0)
    return jnp.sum(jnp.where(row == index, ref[...], 0.0), axis=0, keepdims=True)


def qkv_kernel(tp, owner, states, gains, wq, wkv, *rest):
    outs = rest[:tp]
    wq_buf, wkv_buf, spread_buf, res, kv_res, sq_res, sems = rest[tp:]
    docs, width = states.shape
    pairs = wq.shape[1]
    halves = wq_buf.shape[0]
    rows = 2 * width // halves
    copies = []
    for c in range(halves):
        for p in range(pairs):
            copies.append(
                pltpu.make_async_copy(
                    wq.at[pl.ds(c * rows // 2, rows // 2), p],
                    wq_buf.at[c, p],
                    sems.at[c * pairs + p],
                )
            )
    kv_copy = pltpu.make_async_copy(wkv, wkv_buf, sems.at[halves * pairs])
    for copy in copies:
        copy.start()
    kv_copy.start()
    me = lax.axis_index("tp")
    x = states[...].astype(F32)
    sq_res[...] = jnp.broadcast_to(jnp.sum(x * x, axis=1, keepdims=True), sq_res.shape)
    rows16 = two_parts(x * gains[0:1, :])
    spread(rows16, spread_buf, docs)
    total = jnp.zeros((4 * docs, pairs * LANES), F32)
    for c in range(halves):
        for p in range(pairs):
            copies[c * pairs + p].wait()
        block = jnp.concatenate(
            [wq_buf.at[c, p].reshape(rows, LANES)[...] for p in range(pairs)], axis=1
        )
        total = total + jnp.dot(
            spread_buf[:, c * rows : (c + 1) * rows], block, preferred_element_type=F32
        )
    res[...] = total[: 2 * docs] + total[2 * docs :]
    kv_copy.wait()
    kv_total = jnp.dot(rows16, wkv_buf[...], preferred_element_type=F32)
    kv_res[...] = kv_total[: 2 * docs] + kv_total[2 * docs :]
    for s in range(tp):
        doc = owner[me ^ s]
        for parity in range(2):
            chosen = pick_row(res, parity * docs + doc)
            for p in range(pairs):
                outs[s][2 * p + parity : 2 * p + parity + 1, :] = chosen[
                    :, p * LANES : (p + 1) * LANES
                ]
        chosen = pick_row(kv_res, doc)
        h = 2 * pairs
        outs[s][h : h + 1, :] = chosen[:, :LANES]
        outs[s][h + 1 : h + 2, :] = chosen[:, LANES:]
        outs[s][h + 2 : h + 3, :] = pick_row(sq_res, doc)
        outs[s][h + 3 :, :] = jnp.zeros((outs[s].shape[0] - h - 3, LANES), F32)


def attend_kernel(tp, heads, owner, lengths, frequency, cache, *rest):
    parts = rest[:tp]
    heads_out, new_kv_out, cache_buf, scores, sems = rest[tp:]
    blocks, rows = cache_buf.shape[:2]
    copies = [
        pltpu.make_async_copy(cache.at[pl.ds(b * rows, rows)], cache_buf.at[b], sems.at[b])
        for b in range(blocks)
    ]
    for copy in copies:
        copy.start()
    length = lengths[owner[lax.axis_index("tp")]]
    sums = tree_sum([part[...] for part in parts])
    sums = sums * lax.rsqrt(sums[heads + 2 : heads + 3, :] / D + EPS)
    angle = length.astype(F32) * frequency[...]
    turns = jnp.floor(angle * (0.5 / math.pi) + 0.5)
    angle = ((angle - turns * TURN_A) - turns * TURN_B) - turns * TURN_C
    cosine = jnp.cos(angle)
    sine = jnp.sin(angle)
    lane = lax.broadcasted_iota(jnp.int32, (1, LANES), 1)
    sine = jnp.where(lane < LANES // 2, -sine, sine)
    rotated = sums * cosine + pltpu.roll(sums, LANES // 2, 1) * sine
    query = rotated[:heads].astype(BF16)
    key = rotated[heads : heads + 1].astype(BF16)
    value = sums[heads + 1 : heads + 2].astype(BF16)
    new_kv_out[:, :LANES] = key
    new_kv_out[:, LANES:] = value
    key = key.astype(F32)
    value = value.astype(F32)
    scale = LANES ** (-0.5)
    own = jnp.sum(query.astype(F32) * key, axis=1, keepdims=True) * scale
    column = lax.broadcasted_iota(jnp.int32, (heads, rows), 1)
    top = own
    for b in range(blocks):
        copies[b].wait()
        block = lax.dot_general(
            query,
            cache_buf[b, :, :LANES],
            (((1,), (1,)), ((), ())),
            preferred_element_type=F32,
        )
        block = jnp.where(column < length - b * rows, block * scale, -jnp.inf)
        top = jnp.maximum(top, jnp.max(block, axis=1, keepdims=True))
        scores[:, b * rows : (b + 1) * rows] = block
    own = jnp.exp(own - top)
    total = own
    acc = own.astype(BF16).astype(F32) * value
    for b in range(blocks):
        weights = jnp.exp(scores[:, b * rows : (b + 1) * rows] - top)
        total = total + jnp.sum(weights, axis=1, keepdims=True)
        acc = acc + jnp.dot(
            weights.astype(BF16), cache_buf[b, :, LANES:], preferred_element_type=F32
        )
    heads_out[...] = (acc / total).astype(BF16)


def out_kernel(tp, owner, w_out, *rest):
    parts = rest[:tp]
    out, left = rest[tp:]
    docs = out.shape[0]
    me = lax.axis_index("tp")
    row = lax.broadcasted_iota(jnp.int32, (left.shape[0], LANES), 0)
    own = [parts[s][...].astype(F32) for s in range(tp)]
    for h in range(own[0].shape[0]):
        piece = jnp.zeros((left.shape[0], LANES), F32)
        for s in range(tp):
            piece = jnp.where(row == owner[me ^ s], own[s][h : h + 1, :], piece)
        left[:, h * LANES : (h + 1) * LANES] = piece
    out[...] = jnp.dot(left[...].astype(BF16), w_out[...], preferred_element_type=F32)[:docs]


def gate_up_kernel(kv, states, gains, w, *rest):
    parts = rest[:kv]
    attn_out, partial_out, w_buf, spread_buf, acc, sems = rest[kv:]
    docs, width = states.shape
    hidden = w.shape[2]
    blocks, rows = w_buf.shape[:2]
    w_rows = w.reshape(2 * width, hidden)

    def block_copy(b):
        return pltpu.make_async_copy(
            w_rows.at[pl.ds(b * rows, rows)], w_buf.at[b], sems.at[b]
        )

    for b in range(blocks):
        block_copy(b).start()
    attn = tree_sum([part[...] for part in parts]).astype(BF16)
    attn_out[...] = attn
    resid = (states[...].astype(F32) + attn.astype(F32)).astype(BF16).astype(F32)
    squares = jnp.sum(resid * resid, axis=1, keepdims=True)
    spread(two_parts(resid * gains[1:2, :]), spread_buf, docs)
    acc[...] = jnp.zeros_like(acc)

    def step(b, carry):
        block_copy(b).wait()
        left = spread_buf[:, pl.ds(pl.multiple_of(b * rows, rows), rows)]
        acc[...] += jnp.dot(left, w_buf[b], preferred_element_type=F32)
        return carry

    lax.fori_loop(0, blocks, step, 0)
    partial_out[:, :hidden] = (acc[: 2 * docs] + acc[2 * docs :]).astype(BF16)
    lane = lax.broadcasted_iota(jnp.int32, (docs, LANES), 1)
    first = squares.astype(BF16).astype(F32)
    second = (squares - first).astype(BF16).astype(F32)
    third = squares - first - second
    terms = jnp.where(lane == 0, first, jnp.where(lane == 1, second, jnp.where(lane == 2, third, 0.0)))
    partial_out[:, hidden:] = jnp.concatenate([terms, terms], axis=0).astype(BF16)


def down_kernel(tp, w_down, *rest):
    parts = rest[:tp]
    out, act_buf = rest[tp:]
    docs = out.shape[0]
    hidden = w_down.shape[0]
    summed = tree_sum([part[...].astype(F32) for part in parts])
    squares = jnp.sum(summed[:docs, hidden:], axis=1, keepdims=True)
    inverse = lax.rsqrt(squares / D + EPS)
    gate = summed[:docs, :hidden] * inverse
    up = summed[docs:, :hidden] * inverse
    act_buf[...] = (gate / (1.0 + jnp.exp(-gate)) * up).astype(BF16)
    step_rows = 512
    out[...] = jnp.zeros_like(out)

    def step(b, carry):
        start = pl.multiple_of(b * step_rows, step_rows)
        out[...] += jnp.dot(
            act_buf[:, pl.ds(start, step_rows)],
            w_down[pl.ds(start, step_rows), :],
            preferred_element_type=F32,
        )
        return carry

    lax.fori_loop(0, hidden // step_rows, step, 0)


def cost(flops, nbytes):
    return pl.CostEstimate(flops=flops, bytes_accessed=nbytes, transcendentals=0)


def params(mib):
    return pltpu.CompilerParams(vmem_limit_bytes=mib * MIB)


def per_device(
    tp, kv,
    states, norm_gains, w_query, w_keyval, w_out, w_gate_up, w_down, kv_cache, lengths, owner_rows
):
    docs, width = states.shape
    heads = w_query.shape[1]
    cache_len = kv_cache.shape[1]
    hidden = w_gate_up.shape[2]
    wq = w_query.reshape(width, heads // 2, 2, LANES)
    wkv = w_keyval.reshape(width, 2 * LANES)
    cache = kv_cache.reshape(cache_len, 2 * LANES)
    packed = 2 * heads
    pairs = heads // 2
    halves = 2

    qkv_parts = pl.pallas_call(
        functools.partial(qkv_kernel, tp),
        out_shape=[jax.ShapeDtypeStruct((packed, LANES), F32)] * tp,
        in_specs=[smem(), vmem(), vmem(), hbm(), hbm()],
        out_specs=[vmem()] * tp,
        scratch_shapes=[
            pltpu.VMEM((halves, pairs, width // halves, 2, LANES), BF16),
            pltpu.VMEM((width, 2 * LANES), BF16),
            pltpu.VMEM((4 * docs, 2 * width), BF16),
            pltpu.VMEM((2 * docs, pairs * LANES), F32),
            pltpu.VMEM((2 * docs, 2 * LANES), F32),
            pltpu.VMEM((docs, LANES), F32),
            pltpu.SemaphoreType.DMA((halves * pairs + 1,)),
        ],
        compiler_params=params(12),
        cost_estimate=cost(32 * docs * width * LANES, width * heads * 320),
        name="qkv",
    )(owner_rows, states, norm_gains, wq, wkv)
    qkv_parts = exchange(qkv_parts, "tp", tp)

    half = LANES // 2
    freq = ROPE_BASE ** (-(np.arange(half, dtype=np.float64) * 2.0 / LANES))
    freq = np.concatenate([freq, freq]).astype(np.float32)[None, :]
    rows = 512
    head_out, new_kv = pl.pallas_call(
        functools.partial(attend_kernel, tp, heads),
        out_shape=[
            jax.ShapeDtypeStruct((heads, LANES), BF16),
            jax.ShapeDtypeStruct((1, 2 * LANES), BF16),
        ],
        in_specs=[smem(), smem(), vmem(), hbm()] + [vmem()] * tp,
        out_specs=[vmem(), vmem()],
        scratch_shapes=[
            pltpu.VMEM((cache_len // rows, rows, 2 * LANES), BF16),
            pltpu.VMEM((heads, cache_len), F32),
            pltpu.SemaphoreType.DMA((cache_len // rows,)),
        ],
        compiler_params=params(10),
        cost_estimate=cost(32 * cache_len * LANES, cache_len * 512),
        name="attend",
    )(owner_rows, lengths, jnp.asarray(freq), cache, *qkv_parts)

    head_parts = exchange([head_out] * tp, "tp", tp)
    out_part = pl.pallas_call(
        functools.partial(out_kernel, tp),
        out_shape=jax.ShapeDtypeStruct((docs, width), F32),
        in_specs=[smem(), vmem()] + [vmem()] * tp,
        out_specs=vmem(),
        scratch_shapes=[pltpu.VMEM((max(docs, 8), heads * LANES), F32)],
        compiler_params=params(8),
        cost_estimate=cost(2 * docs * heads * LANES * width, heads * LANES * width * 2),
        name="attn_project",
    )(owner_rows, w_out, *head_parts)

    out_parts = exchange([out_part] * kv, "kv", kv)
    gu_rows = GU_BLOCK
    gu_blocks = 2 * width // gu_rows
    attn_out, gu_part = pl.pallas_call(
        functools.partial(gate_up_kernel, kv),
        out_shape=[
            jax.ShapeDtypeStruct((docs, width), BF16),
            jax.ShapeDtypeStruct((2 * docs, hidden + LANES), BF16),
        ],
        in_specs=[vmem(), vmem(), hbm()] + [vmem()] * kv,
        out_specs=[vmem(), vmem()],
        scratch_shapes=[
            pltpu.VMEM((gu_blocks, gu_rows, hidden), BF16),
            pltpu.VMEM((4 * docs, 2 * width), BF16),
            pltpu.VMEM((4 * docs, hidden), F32),
            pltpu.SemaphoreType.DMA((gu_blocks,)),
        ],
        compiler_params=params(34),
        cost_estimate=cost(8 * docs * width * hidden, width * hidden * 4),
        name="gate_up",
    )(states, norm_gains, w_gate_up, *out_parts)

    gu_parts = exchange([gu_part] * tp, "tp", tp)
    ffn_part = pl.pallas_call(
        functools.partial(down_kernel, tp),
        out_shape=jax.ShapeDtypeStruct((docs, width), F32),
        in_specs=[vmem()] + [vmem()] * tp,
        out_specs=vmem(),
        scratch_shapes=[pltpu.VMEM((docs, hidden), BF16)],
        compiler_params=params(20),
        cost_estimate=cost(2 * docs * hidden * width, hidden * width * 2),
        name="down",
    )(w_down, *gu_parts)
    ffn_out = tree_sum(exchange([ffn_part] * kv, "kv", kv)).astype(BF16)
    return attn_out, ffn_out, new_kv.reshape(1, 1, 2 * LANES)


def solution(mesh):
    return jax.shard_map(
        functools.partial(per_device, mesh.shape["tp"], mesh.shape["kv"]),
        mesh=mesh,
        in_specs=(
            P("grp", "tp"),
            P(None, "tp"),
            P("tp", "kv", None),
            P("tp", "kv", None),
            P("kv", "tp"),
            P("tp", None, "kv"),
            P("kv", "tp"),
            P(("grp", "tp"), None, "kv", None),
            P("grp"),
            P("grp"),
        ),
        out_specs=(P("grp", "tp"), P("grp", "tp"), P(("grp", "tp"), "kv", None)),
        check_vma=False,
    )
```

```python
import functools
import math

import jax
import jax.numpy as jnp
import numpy as np
from jax import lax
from jax.experimental import pallas as pl
from jax.experimental.pallas import tpu as pltpu
from jax.sharding import PartitionSpec as P

D = 8192
EPS = 1e-05
ROPE_BASE = 500000.0
LANES = 128
MIB = 1 << 20
GU_BLOCK = 256
F32 = jnp.float32
BF16 = jnp.bfloat16
TURN_A = 6.28125
TURN_B = 0.0019340515136718750
TURN_C = 2.0 * math.pi - TURN_A - TURN_B


def vmem():
    return pl.BlockSpec(memory_space=pltpu.VMEM)


def hbm():
    return pl.BlockSpec(memory_space=pltpu.HBM)


def in_hbm(array):
    return pltpu.with_memory_space_constraint(array, pltpu.HBM)


def exchange(arrays, axis, size):
    return [arrays[0]] + [
        lax.ppermute(arrays[s], axis, [(i, i ^ s) for i in range(size)])
        for s in range(1, size)
    ]


def tree_sum(parts):
    while len(parts) > 1:
        parts = [a + b for a, b in zip(parts[::2], parts[1::2])]
    return parts[0]


def two_parts(scaled):
    high = scaled.astype(BF16).astype(F32)
    low = scaled - high
    return jnp.concatenate([high, high, low, low], axis=0).astype(BF16)


def spread(rows16, out_ref, docs):
    width = rows16.shape[1]
    source = lax.broadcasted_iota(jnp.int32, (LANES, 2 * LANES), 0)
    target = lax.broadcasted_iota(jnp.int32, (LANES, 2 * LANES), 1)
    pick = (lax.shift_right_logical(target, 1) == source).astype(F32).astype(BF16)
    row = lax.broadcasted_iota(jnp.int32, (4 * docs, 2 * LANES), 0)
    lane = lax.broadcasted_iota(jnp.int32, (4 * docs, 2 * LANES), 1)
    keep = lax.rem(lax.div(row, docs), 2) == lax.rem(lane, 2)
    for c in range(width // LANES):
        doubled = jnp.dot(
            rows16[:, c * LANES : (c + 1) * LANES], pick, preferred_element_type=F32
        )
        out_ref[:, 2 * c * LANES : 2 * (c + 1) * LANES] = jnp.where(keep, doubled, 0.0).astype(BF16)


def weight_copy(w_rows, block, buf, slot, sems):
    rows = buf.shape[1]
    return pltpu.make_async_copy(
        w_rows.at[pl.ds(block * rows, rows)], buf.at[slot], sems.at[slot]
    )


def weight_copies(w_rows, first, buf, sems):
    return [weight_copy(w_rows, first + b, buf, b, sems) for b in range(buf.shape[0])]


def pick_row(ref, index):
    row = lax.broadcasted_iota(jnp.int32, ref.shape, 0)
    return jnp.sum(jnp.where(row == index, ref[...], 0.0), axis=0, keepdims=True)


def rope_rows(length, frequency):
    angle = length * frequency
    turns = jnp.floor(angle * (0.5 / math.pi) + 0.5)
    angle = ((angle - turns * TURN_A) - turns * TURN_B) - turns * TURN_C
    lane = lax.broadcasted_iota(jnp.int32, (1, LANES), 1)
    sine = jnp.sin(angle)
    return jnp.cos(angle), jnp.where(lane < LANES // 2, -sine, sine)


def qkv_kernel(tp, owner_hbm, lengths_hbm, frequency_hbm, states_hbm, gains_hbm, wq, wkv, *rest):
    outs = rest[:tp]
    table, places = rest[tp : tp + 2]
    owner, lengths, frequency, states, gains = rest[tp + 2 : tp + 7]
    wq_buf, wkv_buf, spread_buf, res, kv_res, sq_res, sems, small_sems = rest[tp + 7 :]
    docs, width = states.shape
    pairs = wq.shape[1]
    halves = wq_buf.shape[0]
    rows = 2 * width // halves
    small = [
        pltpu.make_async_copy(source, target, small_sems.at[i])
        for i, (source, target) in enumerate(
            [
                (states_hbm, states),
                (gains_hbm, gains),
                (owner_hbm, owner),
                (lengths_hbm, lengths),
                (frequency_hbm, frequency),
            ]
        )
    ]
    for copy in small:
        copy.start()
    kv_copy = pltpu.make_async_copy(wkv, wkv_buf, sems.at[halves * pairs])
    kv_copy.start()
    copies = []
    for c in range(halves):
        for p in range(pairs):
            copies.append(
                pltpu.make_async_copy(
                    wq.at[pl.ds(c * rows // 2, rows // 2), p],
                    wq_buf.at[c, p],
                    sems.at[c * pairs + p],
                )
            )
    for copy in copies:
        copy.start()
    for copy in small:
        copy.wait()
    me = lax.axis_index("tp")
    x = states[...].astype(F32)
    sq_res[...] = jnp.broadcast_to(jnp.sum(x * x, axis=1, keepdims=True), sq_res.shape)
    rows16 = two_parts(x * gains[0:1, :])
    spread(rows16, spread_buf, docs)
    length = lengths[owner[me]].astype(F32)
    cosine, sine = rope_rows(length, frequency[...])
    table[0:1, :] = cosine
    table[1:2, :] = sine
    table[2:3, :] = jnp.full((1, LANES), length, F32)
    table[3:, :] = jnp.zeros((table.shape[0] - 3, LANES), F32)
    for s in range(tp):
        places[s : s + 1, :] = jnp.full((1, LANES), owner[me ^ s], jnp.int32)
    kv_copy.wait()
    kv_total = jnp.dot(rows16, wkv_buf[...], preferred_element_type=F32)
    kv_res[...] = kv_total[: 2 * docs] + kv_total[2 * docs :]
    total = jnp.zeros((4 * docs, pairs * LANES), F32)
    for c in range(halves):
        for p in range(pairs):
            copies[c * pairs + p].wait()
        block = jnp.concatenate(
            [wq_buf.at[c, p].reshape(rows, LANES)[...] for p in range(pairs)], axis=1
        )
        total = total + jnp.dot(
            spread_buf[:, c * rows : (c + 1) * rows], block, preferred_element_type=F32
        )
    res[...] = total[: 2 * docs] + total[2 * docs :]
    for s in range(tp):
        doc = owner[me ^ s]
        for parity in range(2):
            chosen = pick_row(res, parity * docs + doc)
            for p in range(pairs):
                outs[s][2 * p + parity : 2 * p + parity + 1, :] = chosen[
                    :, p * LANES : (p + 1) * LANES
                ]
        chosen = pick_row(kv_res, doc)
        h = 2 * pairs
        outs[s][h : h + 1, :] = chosen[:, :LANES]
        outs[s][h + 1 : h + 2, :] = chosen[:, LANES:]
        outs[s][h + 2 : h + 3, :] = pick_row(sq_res, doc)
        outs[s][h + 3 :, :] = jnp.zeros((outs[s].shape[0] - h - 3, LANES), F32)


def attend_kernel(tp, heads, rows, table, cache, w, *rest):
    parts = rest[:tp]
    heads_out, new_kv_out, w_ready, scores, w_sems = rest[tp:]
    width, _, hidden = w.shape
    w_copies = weight_copies(w.reshape(2 * width, hidden), 0, w_ready, w_sems)
    for copy in w_copies:
        copy.start()
    blocks = cache.shape[0] // rows
    sums = tree_sum([part[...] for part in parts])
    sums = sums * lax.rsqrt(sums[heads + 2 : heads + 3, :] / D + EPS)
    rotated = sums * table[0:1, :] + pltpu.roll(sums, LANES // 2, 1) * table[1:2, :]
    query = rotated[:heads].astype(BF16)
    key = rotated[heads : heads + 1].astype(BF16)
    value = sums[heads + 1 : heads + 2].astype(BF16)
    new_kv_out[:, :LANES] = key
    new_kv_out[:, LANES:] = value
    key = key.astype(F32)
    value = value.astype(F32)
    scale = LANES ** (-0.5)
    own = jnp.sum(query.astype(F32) * key, axis=1, keepdims=True) * scale
    column = lax.broadcasted_iota(jnp.int32, (heads, rows), 1).astype(F32)
    length = table[2:3, 0:1]
    top = own
    for b in range(blocks):
        block = lax.dot_general(
            query,
            cache[b * rows : (b + 1) * rows, :LANES],
            (((1,), (1,)), ((), ())),
            preferred_element_type=F32,
        )
        block = jnp.where(column < length - b * rows, block * scale, -jnp.inf)
        top = jnp.maximum(top, jnp.max(block, axis=1, keepdims=True))
        scores[:, b * rows : (b + 1) * rows] = block
    own = jnp.exp(own - top)
    total = own
    acc = own.astype(BF16).astype(F32) * value
    for b in range(blocks):
        weights = jnp.exp(scores[:, b * rows : (b + 1) * rows] - top)
        total = total + jnp.sum(weights, axis=1, keepdims=True)
        acc = acc + jnp.dot(
            weights.astype(BF16),
            cache[b * rows : (b + 1) * rows, LANES:],
            preferred_element_type=F32,
        )
    heads_out[...] = (acc / total).astype(BF16)
    for copy in w_copies:
        copy.wait()


def out_kernel(tp, first, places, w_out, w, *rest):
    parts = rest[:tp]
    out, w_ready, left, w_sems = rest[tp:]
    width, _, hidden = w.shape
    w_copies = weight_copies(w.reshape(2 * width, hidden), first, w_ready, w_sems)
    for copy in w_copies:
        copy.start()
    docs = out.shape[0]
    row = lax.broadcasted_iota(jnp.int32, (left.shape[0], LANES), 0)
    own = [parts[s][...].astype(F32) for s in range(tp)]
    for h in range(own[0].shape[0]):
        piece = jnp.zeros((left.shape[0], LANES), F32)
        for s in range(tp):
            piece = jnp.where(row == places[s : s + 1, :], own[s][h : h + 1, :], piece)
        left[:, h * LANES : (h + 1) * LANES] = piece
    out[...] = jnp.dot(left[...].astype(BF16), w_out[...], preferred_element_type=F32)[:docs]
    for copy in w_copies:
        copy.wait()


def gate_up_kernel(kv, states, gains, w, ready_a, ready_b, *rest):
    parts = rest[:kv]
    attn_out, partial_out, w_buf, spread_buf, acc, sems = rest[kv:]
    docs, width = states.shape
    hidden = w.shape[2]
    rows = w_buf.shape[1]
    first = ready_a.shape[0] + ready_b.shape[0]
    w_rows = w.reshape(2 * width, hidden)
    for copy in weight_copies(w_rows, first, w_buf, sems):
        copy.start()
    attn = tree_sum([part[...] for part in parts]).astype(BF16)
    attn_out[...] = attn
    resid = (states[...].astype(F32) + attn.astype(F32)).astype(BF16).astype(F32)
    squares = jnp.sum(resid * resid, axis=1, keepdims=True)
    spread(two_parts(resid * gains[1:2, :]), spread_buf, docs)
    acc[...] = jnp.zeros_like(acc)

    def add_blocks(buf, first, wait):
        def step(b, carry):
            if wait:
                weight_copy(w_rows, first + b, buf, b, sems).wait()
            start = pl.multiple_of((first + b) * rows, rows)
            acc[...] += jnp.dot(
                spread_buf[:, pl.ds(start, rows)], buf[b], preferred_element_type=F32
            )
            return carry

        lax.fori_loop(0, buf.shape[0], step, 0)

    add_blocks(ready_a, 0, False)
    add_blocks(ready_b, ready_a.shape[0], False)
    add_blocks(w_buf, first, True)
    partial_out[:, :hidden] = (acc[: 2 * docs] + acc[2 * docs :]).astype(BF16)
    lane = lax.broadcasted_iota(jnp.int32, (docs, LANES), 1)
    first = squares.astype(BF16).astype(F32)
    second = (squares - first).astype(BF16).astype(F32)
    third = squares - first - second
    terms = jnp.where(lane == 0, first, jnp.where(lane == 1, second, jnp.where(lane == 2, third, 0.0)))
    partial_out[:, hidden:] = jnp.concatenate([terms, terms], axis=0).astype(BF16)


def down_kernel(tp, w_down, *rest):
    parts = rest[:tp]
    out, act_buf = rest[tp:]
    docs = out.shape[0]
    hidden = w_down.shape[0]
    summed = tree_sum([part[...].astype(F32) for part in parts])
    squares = jnp.sum(summed[:docs, hidden:], axis=1, keepdims=True)
    inverse = lax.rsqrt(squares / D + EPS)
    gate = summed[:docs, :hidden] * inverse
    up = summed[docs:, :hidden] * inverse
    act_buf[...] = (gate / (1.0 + jnp.exp(-gate)) * up).astype(BF16)
    step_rows = 512
    out[...] = jnp.zeros_like(out)

    def step(b, carry):
        start = pl.multiple_of(b * step_rows, step_rows)
        out[...] += jnp.dot(
            act_buf[:, pl.ds(start, step_rows)],
            w_down[pl.ds(start, step_rows), :],
            preferred_element_type=F32,
        )
        return carry

    lax.fori_loop(0, hidden // step_rows, step, 0)


def cost(micros):
    return pl.CostEstimate(flops=0, bytes_accessed=int(micros * 3.69e6), transcendentals=0)


def params(docs, mib):
    return pltpu.CompilerParams(vmem_limit_bytes=(mib if docs <= 8 else mib + 24) * MIB)


def per_device(
    tp, kv,
    states, norm_gains, w_query, w_keyval, w_out, w_gate_up, w_down, kv_cache, lengths, owner_rows
):
    docs, width = states.shape
    heads = w_query.shape[1]
    cache_len = kv_cache.shape[1]
    hidden = w_gate_up.shape[2]
    wq = w_query.reshape(width, heads // 2, 2, LANES)
    wkv = w_keyval.reshape(width, 2 * LANES)
    cache = kv_cache.reshape(cache_len, 2 * LANES)
    packed = 2 * heads
    pairs = heads // 2
    halves = 2

    half = LANES // 2
    freq = ROPE_BASE ** (-(np.arange(half, dtype=np.float64) * 2.0 / LANES))
    freq = jnp.asarray(np.concatenate([freq, freq]).astype(np.float32)[None, :])
    *qkv_parts, table, places = pl.pallas_call(
        functools.partial(qkv_kernel, tp),
        out_shape=[jax.ShapeDtypeStruct((packed, LANES), F32)] * tp
        + [
            jax.ShapeDtypeStruct((8, LANES), F32),
            jax.ShapeDtypeStruct((max(tp, 8), LANES), jnp.int32),
        ],
        in_specs=[hbm()] * 7,
        out_specs=[vmem()] * (tp + 2),
        scratch_shapes=[
            pltpu.SMEM((docs,), jnp.int32),
            pltpu.SMEM((docs,), jnp.int32),
            pltpu.VMEM((1, LANES), F32),
            pltpu.VMEM((docs, width), BF16),
            pltpu.VMEM((2, width), F32),
            pltpu.VMEM((halves, pairs, width // halves, 2, LANES), BF16),
            pltpu.VMEM((width, 2 * LANES), BF16),
            pltpu.VMEM((4 * docs, 2 * width), BF16),
            pltpu.VMEM((2 * docs, pairs * LANES), F32),
            pltpu.VMEM((2 * docs, 2 * LANES), F32),
            pltpu.VMEM((docs, LANES), F32),
            pltpu.SemaphoreType.DMA((halves * pairs + 1,)),
            pltpu.SemaphoreType.DMA((5,)),
        ],
        compiler_params=params(docs, 10),
        cost_estimate=cost(8),
        name="qkv",
    )(*(in_hbm(a) for a in (owner_rows, lengths, freq, states, norm_gains, wq, wkv)))
    qkv_parts = exchange(qkv_parts, "tp", tp)

    w_gu = in_hbm(w_gate_up)
    gu_blocks = 2 * width // GU_BLOCK
    ready_a = max(gu_blocks * 5 // 16, 1)
    ready_b = max(gu_blocks // 8, 1)
    head_out, new_kv, w_ready_a = pl.pallas_call(
        functools.partial(attend_kernel, tp, heads, 512),
        out_shape=[
            jax.ShapeDtypeStruct((heads, LANES), BF16),
            jax.ShapeDtypeStruct((1, 2 * LANES), BF16),
            pltpu.VMEM((ready_a, GU_BLOCK, hidden), BF16),
        ],
        in_specs=[vmem(), vmem(), hbm()] + [vmem()] * tp,
        out_specs=[vmem()] * 3,
        scratch_shapes=[
            pltpu.VMEM((heads, cache_len), F32),
            pltpu.SemaphoreType.DMA((ready_a,)),
        ],
        compiler_params=params(docs, 6),
        cost_estimate=cost(8),
        name="attend",
    )(table, cache, w_gu, *qkv_parts)

    head_parts = exchange([head_out] * tp, "tp", tp)
    out_part, w_ready_b = pl.pallas_call(
        functools.partial(out_kernel, tp, ready_a),
        out_shape=[
            jax.ShapeDtypeStruct((docs, width), F32),
            pltpu.VMEM((ready_b, GU_BLOCK, hidden), BF16),
        ],
        in_specs=[vmem(), vmem(), hbm()] + [vmem()] * tp,
        out_specs=[vmem()] * 2,
        scratch_shapes=[
            pltpu.VMEM((max(docs, 8), heads * LANES), F32),
            pltpu.SemaphoreType.DMA((ready_b,)),
        ],
        compiler_params=params(docs, 6),
        cost_estimate=cost(6),
        name="attn_project",
    )(places, w_out, w_gu, *head_parts)

    out_parts = exchange([out_part] * kv, "kv", kv)
    gu_rest = gu_blocks - ready_a - ready_b
    attn_out, gu_part = pl.pallas_call(
        functools.partial(gate_up_kernel, kv),
        out_shape=[
            jax.ShapeDtypeStruct((docs, width), BF16),
            jax.ShapeDtypeStruct((2 * docs, hidden + LANES), BF16),
        ],
        in_specs=[vmem(), vmem(), hbm(), vmem(), vmem()] + [vmem()] * kv,
        out_specs=[vmem(), vmem()],
        scratch_shapes=[
            pltpu.VMEM((gu_rest, GU_BLOCK, hidden), BF16),
            pltpu.VMEM((4 * docs, 2 * width), BF16),
            pltpu.VMEM((4 * docs, hidden), F32),
            pltpu.SemaphoreType.DMA((gu_rest,)),
        ],
        compiler_params=params(docs, 18),
        cost_estimate=cost(8),
        name="gate_up",
    )(states, norm_gains, w_gu, w_ready_a, w_ready_b, *out_parts)

    gu_parts = exchange([gu_part] * tp, "tp", tp)
    ffn_part = pl.pallas_call(
        functools.partial(down_kernel, tp),
        out_shape=jax.ShapeDtypeStruct((docs, width), F32),
        in_specs=[vmem()] + [vmem()] * tp,
        out_specs=vmem(),
        scratch_shapes=[pltpu.VMEM((docs, hidden), BF16)],
        compiler_params=params(docs, 6),
        cost_estimate=cost(5),
        name="down",
    )(w_down, *gu_parts)
    ffn_out = tree_sum(exchange([ffn_part] * kv, "kv", kv)).astype(BF16)
    return attn_out, ffn_out, new_kv.reshape(1, 1, 2 * LANES)


def solution(mesh):
    return jax.shard_map(
        functools.partial(per_device, mesh.shape["tp"], mesh.shape["kv"]),
        mesh=mesh,
        in_specs=(
            P("grp", "tp"),
            P(None, "tp"),
            P("tp", "kv", None),
            P("tp", "kv", None),
            P("kv", "tp"),
            P("tp", None, "kv"),
            P("kv", "tp"),
            P(("grp", "tp"), None, "kv", None),
            P("grp"),
            P("grp"),
        ),
        out_specs=(P("grp", "tp"), P("grp", "tp"), P(("grp", "tp"), "kv", None)),
        check_vma=False,
    )
```

```python
import functools
import math

import jax
import jax.numpy as jnp
import numpy as np
from jax import lax
from jax.experimental import pallas as pl
from jax.experimental.pallas import tpu as pltpu
from jax.sharding import PartitionSpec as P

D = 8192
EPS = 1e-05
ROPE_BASE = 500000.0
LANES = 128
MIB = 1 << 20
GU_BLOCK = 256
F32 = jnp.float32
BF16 = jnp.bfloat16
TURN_A = 6.28125
TURN_B = 0.0019340515136718750
TURN_C = 2.0 * math.pi - TURN_A - TURN_B


def vmem():
    return pl.BlockSpec(memory_space=pltpu.VMEM)


def hbm():
    return pl.BlockSpec(memory_space=pltpu.HBM)


def in_hbm(array):
    return pltpu.with_memory_space_constraint(array, pltpu.HBM)


def exchange(arrays, axis, size):
    return [arrays[0]] + [
        lax.ppermute(arrays[s], axis, [(i, i ^ s) for i in range(size)])
        for s in range(1, size)
    ]


def tree_sum(parts):
    while len(parts) > 1:
        parts = [a + b for a, b in zip(parts[::2], parts[1::2])]
    return parts[0]


def two_parts(scaled):
    high = scaled.astype(BF16).astype(F32)
    low = scaled - high
    return jnp.concatenate([high, high, low, low], axis=0).astype(BF16)


def spread(rows16, out_ref, docs):
    width = rows16.shape[1]
    source = lax.broadcasted_iota(jnp.int32, (LANES, 2 * LANES), 0)
    target = lax.broadcasted_iota(jnp.int32, (LANES, 2 * LANES), 1)
    pick = (lax.shift_right_logical(target, 1) == source).astype(F32).astype(BF16)
    row = lax.broadcasted_iota(jnp.int32, (4 * docs, 2 * LANES), 0)
    lane = lax.broadcasted_iota(jnp.int32, (4 * docs, 2 * LANES), 1)
    keep = lax.rem(lax.div(row, docs), 2) == lax.rem(lane, 2)
    for c in range(width // LANES):
        doubled = jnp.dot(
            rows16[:, c * LANES : (c + 1) * LANES], pick, preferred_element_type=F32
        )
        out_ref[:, 2 * c * LANES : 2 * (c + 1) * LANES] = jnp.where(keep, doubled, 0.0).astype(BF16)


def weight_copy(w_rows, block, buf, slot, sems):
    rows = buf.shape[1]
    return pltpu.make_async_copy(
        w_rows.at[pl.ds(block * rows, rows)], buf.at[slot], sems.at[slot]
    )


def weight_copies(w_rows, first, buf, sems):
    return [weight_copy(w_rows, first + b, buf, b, sems) for b in range(buf.shape[0])]


def pick_row(ref, index):
    row = lax.broadcasted_iota(jnp.int32, ref.shape, 0)
    return jnp.sum(jnp.where(row == index, ref[...], 0.0), axis=0, keepdims=True)


def rope_rows(length, frequency):
    angle = length * frequency
    turns = jnp.floor(angle * (0.5 / math.pi) + 0.5)
    angle = ((angle - turns * TURN_A) - turns * TURN_B) - turns * TURN_C
    lane = lax.broadcasted_iota(jnp.int32, (1, LANES), 1)
    sine = jnp.sin(angle)
    return jnp.cos(angle), jnp.where(lane < LANES // 2, -sine, sine)


def qkv_kernel(tp, owner_hbm, lengths_hbm, frequency_hbm, states_hbm, gains_hbm, wq, wkv, *rest):
    outs, table, places = rest[:3]
    owner, lengths, frequency, states, gains = rest[3:8]
    wq_buf, wkv_buf, spread_buf, res, kv_res, sq_res, sems, small_sems = rest[8:]
    docs, width = states.shape
    pairs = wq.shape[1]
    halves = wq_buf.shape[0]
    rows = 2 * width // halves
    small = [
        pltpu.make_async_copy(source, target, small_sems.at[i])
        for i, (source, target) in enumerate(
            [
                (states_hbm, states),
                (gains_hbm, gains),
                (owner_hbm, owner),
                (lengths_hbm, lengths),
                (frequency_hbm, frequency),
            ]
        )
    ]
    for copy in small:
        copy.start()
    kv_copy = pltpu.make_async_copy(wkv, wkv_buf, sems.at[halves * pairs])
    kv_copy.start()
    copies = []
    for c in range(halves):
        for p in range(pairs):
            copies.append(
                pltpu.make_async_copy(
                    wq.at[pl.ds(c * rows // 2, rows // 2), p],
                    wq_buf.at[c, p],
                    sems.at[c * pairs + p],
                )
            )
    for copy in copies:
        copy.start()
    for copy in small:
        copy.wait()
    me = lax.axis_index("tp")
    x = states[...].astype(F32)
    sq_res[...] = jnp.broadcast_to(jnp.sum(x * x, axis=1, keepdims=True), sq_res.shape)
    rows16 = two_parts(x * gains[0:1, :])
    spread(rows16, spread_buf, docs)
    length = lengths[owner[me]].astype(F32)
    cosine, sine = rope_rows(length, frequency[...])
    table[0:1, :] = cosine
    table[1:2, :] = sine
    table[2:3, :] = jnp.full((1, LANES), length, F32)
    table[3:, :] = jnp.zeros((table.shape[0] - 3, LANES), F32)
    for s in range(tp):
        places[s : s + 1, :] = jnp.full((1, LANES), owner[me ^ s], jnp.int32)
    kv_copy.wait()
    kv_total = jnp.dot(rows16, wkv_buf[...], preferred_element_type=F32)
    kv_res[...] = kv_total[: 2 * docs] + kv_total[2 * docs :]
    total = jnp.zeros((4 * docs, pairs * LANES), F32)
    for c in range(halves):
        for p in range(pairs):
            copies[c * pairs + p].wait()
        block = jnp.concatenate(
            [wq_buf.at[c, p].reshape(rows, LANES)[...] for p in range(pairs)], axis=1
        )
        total = total + jnp.dot(
            spread_buf[:, c * rows : (c + 1) * rows], block, preferred_element_type=F32
        )
    res[...] = total[: 2 * docs] + total[2 * docs :]
    for s in range(tp):
        doc = owner[s]
        for parity in range(2):
            chosen = pick_row(res, parity * docs + doc)
            for p in range(pairs):
                outs[s, 2 * p + parity : 2 * p + parity + 1, :] = chosen[
                    :, p * LANES : (p + 1) * LANES
                ]
        chosen = pick_row(kv_res, doc)
        h = 2 * pairs
        outs[s, h : h + 1, :] = chosen[:, :LANES]
        outs[s, h + 1 : h + 2, :] = chosen[:, LANES:]
        outs[s, h + 2 : h + 3, :] = pick_row(sq_res, doc)
        outs[s, h + 3 :, :] = jnp.zeros((outs.shape[1] - h - 3, LANES), F32)


def attend_kernel(
    heads, rows, table, cache, w, parts, heads_out, new_kv_out, w_ready, scores, w_sems
):
    width, _, hidden = w.shape
    w_copies = weight_copies(w.reshape(2 * width, hidden), 0, w_ready, w_sems)
    for copy in w_copies:
        copy.start()
    blocks = cache.shape[0] // rows
    sums = tree_sum([parts[j] for j in range(parts.shape[0])])
    sums = sums * lax.rsqrt(sums[heads + 2 : heads + 3, :] / D + EPS)
    rotated = sums * table[0:1, :] + pltpu.roll(sums, LANES // 2, 1) * table[1:2, :]
    query = rotated[:heads].astype(BF16)
    key = rotated[heads : heads + 1].astype(BF16)
    value = sums[heads + 1 : heads + 2].astype(BF16)
    new_kv_out[:, :LANES] = key
    new_kv_out[:, LANES:] = value
    key = key.astype(F32)
    value = value.astype(F32)
    scale = LANES ** (-0.5)
    own = jnp.sum(query.astype(F32) * key, axis=1, keepdims=True) * scale
    column = lax.broadcasted_iota(jnp.int32, (heads, rows), 1).astype(F32)
    length = table[2:3, 0:1]
    top = own
    for b in range(blocks):
        block = lax.dot_general(
            query,
            cache[b * rows : (b + 1) * rows, :LANES],
            (((1,), (1,)), ((), ())),
            preferred_element_type=F32,
        )
        block = jnp.where(column < length - b * rows, block * scale, -jnp.inf)
        top = jnp.maximum(top, jnp.max(block, axis=1, keepdims=True))
        scores[:, b * rows : (b + 1) * rows] = block
    own = jnp.exp(own - top)
    total = own
    acc = own.astype(BF16).astype(F32) * value
    for b in range(blocks):
        weights = jnp.exp(scores[:, b * rows : (b + 1) * rows] - top)
        total = total + jnp.sum(weights, axis=1, keepdims=True)
        acc = acc + jnp.dot(
            weights.astype(BF16),
            cache[b * rows : (b + 1) * rows, LANES:],
            preferred_element_type=F32,
        )
    heads_out[...] = (acc / total).astype(BF16)
    for copy in w_copies:
        copy.wait()


def out_kernel(tp, places, w_out, *rest):
    parts = rest[:tp]
    out, left = rest[tp:]
    docs = out.shape[1]
    row = lax.broadcasted_iota(jnp.int32, (left.shape[0], LANES), 0)
    own = [parts[s][...].astype(F32) for s in range(tp)]
    for h in range(own[0].shape[0]):
        piece = jnp.zeros((left.shape[0], LANES), F32)
        for s in range(tp):
            piece = jnp.where(row == places[s : s + 1, :], own[s][h : h + 1, :], piece)
        left[:, h * LANES : (h + 1) * LANES] = piece
    terms = jnp.dot(left[...].astype(BF16), w_out[...], preferred_element_type=F32)[:docs]
    for j in range(out.shape[0]):
        out[j] = terms


def gate_up_kernel(
    states, gains, w, ready, parts, attn_out, partial_out, w_buf, spread_buf, acc, sems
):
    docs, width = states.shape
    hidden = w.shape[2]
    rows = w_buf.shape[1]
    first = ready.shape[0]
    w_rows = w.reshape(2 * width, hidden)
    for copy in weight_copies(w_rows, first, w_buf, sems):
        copy.start()
    attn = tree_sum([parts[j] for j in range(parts.shape[0])]).astype(BF16)
    attn_out[...] = attn
    resid = (states[...].astype(F32) + attn.astype(F32)).astype(BF16).astype(F32)
    squares = jnp.sum(resid * resid, axis=1, keepdims=True)
    spread(two_parts(resid * gains[1:2, :]), spread_buf, docs)
    acc[...] = jnp.zeros_like(acc)

    def add_blocks(buf, first, wait):
        def step(b, carry):
            if wait:
                weight_copy(w_rows, first + b, buf, b, sems).wait()
            start = pl.multiple_of((first + b) * rows, rows)
            acc[...] += jnp.dot(
                spread_buf[:, pl.ds(start, rows)], buf[b], preferred_element_type=F32
            )
            return carry

        lax.fori_loop(0, buf.shape[0], step, 0)

    add_blocks(ready, 0, False)
    add_blocks(w_buf, first, True)
    partial_out[:, :hidden] = (acc[: 2 * docs] + acc[2 * docs :]).astype(BF16)
    lane = lax.broadcasted_iota(jnp.int32, (docs, LANES), 1)
    first = squares.astype(BF16).astype(F32)
    second = (squares - first).astype(BF16).astype(F32)
    third = squares - first - second
    terms = jnp.where(lane == 0, first, jnp.where(lane == 1, second, jnp.where(lane == 2, third, 0.0)))
    partial_out[:, hidden:] = jnp.concatenate([terms, terms], axis=0).astype(BF16)


def down_kernel(tp, w_down, *rest):
    parts = rest[:tp]
    out, act_buf = rest[tp:]
    docs = out.shape[0]
    hidden = w_down.shape[0]
    summed = tree_sum([part[...].astype(F32) for part in parts])
    squares = jnp.sum(summed[:docs, hidden:], axis=1, keepdims=True)
    inverse = lax.rsqrt(squares / D + EPS)
    gate = summed[:docs, :hidden] * inverse
    up = summed[docs:, :hidden] * inverse
    act_buf[...] = (gate / (1.0 + jnp.exp(-gate)) * up).astype(BF16)
    step_rows = 512
    out[...] = jnp.zeros_like(out)

    def step(b, carry):
        start = pl.multiple_of(b * step_rows, step_rows)
        out[...] += jnp.dot(
            act_buf[:, pl.ds(start, step_rows)],
            w_down[pl.ds(start, step_rows), :],
            preferred_element_type=F32,
        )
        return carry

    lax.fori_loop(0, hidden // step_rows, step, 0)


def cost(micros):
    return pl.CostEstimate(flops=0, bytes_accessed=int(micros * 3.69e6), transcendentals=0)


def params(docs, mib):
    return pltpu.CompilerParams(vmem_limit_bytes=(mib if docs <= 8 else mib + 24) * MIB)


def per_device(
    tp, kv,
    states, norm_gains, w_query, w_keyval, w_out, w_gate_up, w_down, kv_cache, lengths, owner_rows
):
    docs, width = states.shape
    heads = w_query.shape[1]
    cache_len = kv_cache.shape[1]
    hidden = w_gate_up.shape[2]
    wq = w_query.reshape(width, heads // 2, 2, LANES)
    wkv = w_keyval.reshape(width, 2 * LANES)
    cache = kv_cache.reshape(cache_len, 2 * LANES)
    packed = 2 * heads
    pairs = heads // 2
    halves = 2

    half = LANES // 2
    freq = ROPE_BASE ** (-(np.arange(half, dtype=np.float64) * 2.0 / LANES))
    freq = jnp.asarray(np.concatenate([freq, freq]).astype(np.float32)[None, :])
    qkv_parts, table, places = pl.pallas_call(
        functools.partial(qkv_kernel, tp),
        out_shape=[
            jax.ShapeDtypeStruct((tp, packed, LANES), F32),
            jax.ShapeDtypeStruct((8, LANES), F32),
            jax.ShapeDtypeStruct((max(tp, 8), LANES), jnp.int32),
        ],
        in_specs=[hbm()] * 7,
        out_specs=[vmem()] * 3,
        scratch_shapes=[
            pltpu.SMEM((docs,), jnp.int32),
            pltpu.SMEM((docs,), jnp.int32),
            pltpu.VMEM((1, LANES), F32),
            pltpu.VMEM((docs, width), BF16),
            pltpu.VMEM((2, width), F32),
            pltpu.VMEM((halves, pairs, width // halves, 2, LANES), BF16),
            pltpu.VMEM((width, 2 * LANES), BF16),
            pltpu.VMEM((4 * docs, 2 * width), BF16),
            pltpu.VMEM((2 * docs, pairs * LANES), F32),
            pltpu.VMEM((2 * docs, 2 * LANES), F32),
            pltpu.VMEM((docs, LANES), F32),
            pltpu.SemaphoreType.DMA((halves * pairs + 1,)),
            pltpu.SemaphoreType.DMA((5,)),
        ],
        compiler_params=params(docs, 10),
        cost_estimate=cost(8),
        name="qkv",
    )(*(in_hbm(a) for a in (owner_rows, lengths, freq, states, norm_gains, wq, wkv)))
    qkv_parts = lax.all_to_all(qkv_parts, "tp", 0, 0, tiled=True)

    w_gu = in_hbm(w_gate_up)
    gu_blocks = 2 * width // GU_BLOCK
    ready = max(gu_blocks * 6 // 16, 1)
    head_out, new_kv, w_ready = pl.pallas_call(
        functools.partial(attend_kernel, heads, 512),
        out_shape=[
            jax.ShapeDtypeStruct((heads, LANES), BF16),
            jax.ShapeDtypeStruct((1, 2 * LANES), BF16),
            pltpu.VMEM((ready, GU_BLOCK, hidden), BF16),
        ],
        in_specs=[vmem(), vmem(), hbm(), vmem()],
        out_specs=[vmem()] * 3,
        scratch_shapes=[
            pltpu.VMEM((heads, cache_len), F32),
            pltpu.SemaphoreType.DMA((ready,)),
        ],
        compiler_params=params(docs, 6),
        cost_estimate=cost(8),
        name="attend",
    )(table, cache, w_gu, qkv_parts)

    head_parts = exchange([head_out] * tp, "tp", tp)
    out_part = pl.pallas_call(
        functools.partial(out_kernel, tp),
        out_shape=jax.ShapeDtypeStruct((kv, docs, width), F32),
        in_specs=[vmem()] * (tp + 2),
        out_specs=vmem(),
        scratch_shapes=[pltpu.VMEM((max(docs, 8), heads * LANES), F32)],
        compiler_params=params(docs, 6),
        cost_estimate=cost(6),
        name="attn_project",
    )(places, w_out, *head_parts)

    out_parts = lax.all_to_all(out_part, "kv", 0, 0, tiled=True)
    gu_rest = gu_blocks - ready
    attn_out, gu_part = pl.pallas_call(
        gate_up_kernel,
        out_shape=[
            jax.ShapeDtypeStruct((docs, width), BF16),
            jax.ShapeDtypeStruct((2 * docs, hidden + LANES), BF16),
        ],
        in_specs=[vmem(), vmem(), hbm(), vmem(), vmem()],
        out_specs=[vmem(), vmem()],
        scratch_shapes=[
            pltpu.VMEM((gu_rest, GU_BLOCK, hidden), BF16),
            pltpu.VMEM((4 * docs, 2 * width), BF16),
            pltpu.VMEM((4 * docs, hidden), F32),
            pltpu.SemaphoreType.DMA((gu_rest,)),
        ],
        compiler_params=params(docs, 22),
        cost_estimate=cost(8),
        name="gate_up",
    )(states, norm_gains, w_gu, w_ready, out_parts)

    gu_parts = exchange([gu_part] * tp, "tp", tp)
    ffn_part = pl.pallas_call(
        functools.partial(down_kernel, tp),
        out_shape=jax.ShapeDtypeStruct((docs, width), F32),
        in_specs=[vmem()] + [vmem()] * tp,
        out_specs=vmem(),
        scratch_shapes=[pltpu.VMEM((docs, hidden), BF16)],
        compiler_params=params(docs, 6),
        cost_estimate=cost(5),
        name="down",
    )(w_down, *gu_parts)
    ffn_out = tree_sum(exchange([ffn_part] * kv, "kv", kv)).astype(BF16)
    return attn_out, ffn_out, new_kv.reshape(1, 1, 2 * LANES)


def solution(mesh):
    return jax.shard_map(
        functools.partial(per_device, mesh.shape["tp"], mesh.shape["kv"]),
        mesh=mesh,
        in_specs=(
            P("grp", "tp"),
            P(None, "tp"),
            P("tp", "kv", None),
            P("tp", "kv", None),
            P("kv", "tp"),
            P("tp", None, "kv"),
            P("kv", "tp"),
            P(("grp", "tp"), None, "kv", None),
            P("grp"),
            P("grp"),
        ),
        out_specs=(P("grp", "tp"), P("grp", "tp"), P(("grp", "tp"), "kv", None)),
        check_vma=False,
    )
```

```python
import functools
import math

import jax
import jax.numpy as jnp
import numpy as np
from jax import lax
from jax.experimental import pallas as pl
from jax.experimental.pallas import tpu as pltpu
from jax.sharding import PartitionSpec as P

D = 8192
EPS = 1e-05
ROPE_BASE = 500000.0
LANES = 128
MIB = 1 << 20
GU_BLOCK = 256
DOWN_BLOCK = 512
F32 = jnp.float32
BF16 = jnp.bfloat16
TURN_A = 6.28125
TURN_B = 0.0019340515136718750
TURN_C = 2.0 * math.pi - TURN_A - TURN_B


def vmem():
    return pl.BlockSpec(memory_space=pltpu.VMEM)


def hbm():
    return pl.BlockSpec(memory_space=pltpu.HBM)


def in_hbm(array):
    return pltpu.with_memory_space_constraint(array, pltpu.HBM)


def exchange(arrays, axis, size):
    return [arrays[0]] + [
        lax.ppermute(arrays[s], axis, [(i, i ^ s) for i in range(size)])
        for s in range(1, size)
    ]


def tree_sum(parts):
    while len(parts) > 1:
        parts = [a + b for a, b in zip(parts[::2], parts[1::2])]
    return parts[0]


def two_parts(scaled):
    high = scaled.astype(BF16).astype(F32)
    low = scaled - high
    return jnp.concatenate([high, high, low, low], axis=0).astype(BF16)


def spread(rows16, out_ref, docs):
    width = rows16.shape[1]
    source = lax.broadcasted_iota(jnp.int32, (LANES, 2 * LANES), 0)
    target = lax.broadcasted_iota(jnp.int32, (LANES, 2 * LANES), 1)
    pick = (lax.shift_right_logical(target, 1) == source).astype(F32).astype(BF16)
    row = lax.broadcasted_iota(jnp.int32, (4 * docs, 2 * LANES), 0)
    lane = lax.broadcasted_iota(jnp.int32, (4 * docs, 2 * LANES), 1)
    keep = lax.rem(lax.div(row, docs), 2) == lax.rem(lane, 2)
    chunks = width // LANES
    stacked = jnp.concatenate(
        [rows16[:, c * LANES : (c + 1) * LANES] for c in range(chunks)], axis=0
    )
    doubled = jnp.dot(stacked, pick, preferred_element_type=F32)
    for c in range(chunks):
        piece = doubled[c * 4 * docs : (c + 1) * 4 * docs]
        out_ref[:, 2 * c * LANES : 2 * (c + 1) * LANES] = jnp.where(keep, piece, 0.0).astype(BF16)


def weight_copy(w_rows, block, buf, slot, sems):
    rows = buf.shape[1]
    return pltpu.make_async_copy(
        w_rows.at[pl.ds(block * rows, rows)], buf.at[slot], sems.at[slot]
    )


def weight_copies(w_rows, first, buf, sems):
    return [weight_copy(w_rows, first + b, buf, b, sems) for b in range(buf.shape[0])]


def pick_row(ref, index):
    row = lax.broadcasted_iota(jnp.int32, ref.shape, 0)
    return jnp.sum(jnp.where(row == index, ref[...], 0.0), axis=0, keepdims=True)


def rope_rows(length, frequency):
    angle = length * frequency
    turns = jnp.floor(angle * (0.5 / math.pi) + 0.5)
    angle = ((angle - turns * TURN_A) - turns * TURN_B) - turns * TURN_C
    lane = lax.broadcasted_iota(jnp.int32, (1, LANES), 1)
    sine = jnp.sin(angle)
    return jnp.cos(angle), jnp.where(lane < LANES // 2, -sine, sine)


def qkv_kernel(tp, owner_hbm, lengths_hbm, frequency_hbm, states_hbm, gains_hbm, wq, wkv, *rest):
    outs = rest[:tp]
    table, places = rest[tp : tp + 2]
    owner, lengths, frequency, states, gains = rest[tp + 2 : tp + 7]
    wq_buf, wkv_buf, spread_buf, res, kv_res, sq_res, sems, small_sems = rest[tp + 7 :]
    docs, width = states.shape
    pairs = wq.shape[1]
    halves = wq_buf.shape[0]
    rows = 2 * width // halves
    small = [
        pltpu.make_async_copy(source, target, small_sems.at[i])
        for i, (source, target) in enumerate(
            [
                (states_hbm, states),
                (gains_hbm, gains),
                (owner_hbm, owner),
                (lengths_hbm, lengths),
                (frequency_hbm, frequency),
            ]
        )
    ]
    for copy in small:
        copy.start()
    kv_copy = pltpu.make_async_copy(wkv, wkv_buf, sems.at[halves * pairs])
    kv_copy.start()
    copies = []
    for c in range(halves):
        for p in range(pairs):
            copies.append(
                pltpu.make_async_copy(
                    wq.at[pl.ds(c * rows // 2, rows // 2), p],
                    wq_buf.at[c, p],
                    sems.at[c * pairs + p],
                )
            )
    for copy in copies:
        copy.start()
    for copy in small:
        copy.wait()
    me = lax.axis_index("tp")
    x = states[...].astype(F32)
    sq_res[...] = jnp.broadcast_to(jnp.sum(x * x, axis=1, keepdims=True), sq_res.shape)
    rows16 = two_parts(x * gains[0:1, :])
    spread(rows16, spread_buf, docs)
    length = lengths[owner[me]].astype(F32)
    cosine, sine = rope_rows(length, frequency[...])
    table[0:1, :] = cosine
    table[1:2, :] = sine
    table[2:3, :] = jnp.full((1, LANES), length, F32)
    table[3:, :] = jnp.zeros((table.shape[0] - 3, LANES), F32)
    for s in range(tp):
        places[s : s + 1, :] = jnp.full((1, LANES), owner[me ^ s], jnp.int32)
    kv_copy.wait()
    kv_total = jnp.dot(rows16, wkv_buf[...], preferred_element_type=F32)
    kv_res[...] = kv_total[: 2 * docs] + kv_total[2 * docs :]
    total = jnp.zeros((4 * docs, pairs * LANES), F32)
    for c in range(halves):
        for p in range(pairs):
            copies[c * pairs + p].wait()
        block = jnp.concatenate(
            [wq_buf.at[c, p].reshape(rows, LANES)[...] for p in range(pairs)], axis=1
        )
        total = total + jnp.dot(
            spread_buf[:, c * rows : (c + 1) * rows], block, preferred_element_type=F32
        )
    res[...] = total[: 2 * docs] + total[2 * docs :]
    for s in range(tp):
        doc = owner[me ^ s]
        for parity in range(2):
            chosen = pick_row(res, parity * docs + doc)
            for p in range(pairs):
                outs[s][2 * p + parity : 2 * p + parity + 1, :] = chosen[
                    :, p * LANES : (p + 1) * LANES
                ]
        chosen = pick_row(kv_res, doc)
        h = 2 * pairs
        outs[s][h : h + 1, :] = chosen[:, :LANES]
        outs[s][h + 1 : h + 2, :] = chosen[:, LANES:]
        outs[s][h + 2 : h + 3, :] = pick_row(sq_res, doc)
        outs[s][h + 3 :, :] = jnp.zeros((outs[s].shape[0] - h - 3, LANES), F32)


def attend_kernel(tp, heads, rows, first, table, cache, w, *rest):
    parts = rest[:tp]
    heads_out, new_kv_out, w_ready, scores, w_sems = rest[-5:]
    width, _, hidden = w.shape
    w_copies = weight_copies(w.reshape(2 * width, hidden), first, w_ready, w_sems)
    for copy in w_copies:
        copy.start()
    blocks = cache.shape[0] // rows
    sums = tree_sum([part[...] for part in parts])
    sums = sums * lax.rsqrt(sums[heads + 2 : heads + 3, :] / D + EPS)
    rotated = sums * table[0:1, :] + pltpu.roll(sums, LANES // 2, 1) * table[1:2, :]
    query = rotated[:heads].astype(BF16)
    key = rotated[heads : heads + 1].astype(BF16)
    value = sums[heads + 1 : heads + 2].astype(BF16)
    new_kv_out[:, :LANES] = key
    new_kv_out[:, LANES:] = value
    key = key.astype(F32)
    value = value.astype(F32)
    scale = LANES ** (-0.5)
    own = jnp.sum(query.astype(F32) * key, axis=1, keepdims=True) * scale
    column = lax.broadcasted_iota(jnp.int32, (heads, rows), 1).astype(F32)
    length = table[2:3, 0:1]
    top = own
    for b in range(blocks):
        block = lax.dot_general(
            query,
            cache[b * rows : (b + 1) * rows, :LANES],
            (((1,), (1,)), ((), ())),
            preferred_element_type=F32,
        )
        block = jnp.where(column < length - b * rows, block * scale, -jnp.inf)
        top = jnp.maximum(top, jnp.max(block, axis=1, keepdims=True))
        scores[:, b * rows : (b + 1) * rows] = block
    own = jnp.exp(own - top)
    total = own
    acc = own.astype(BF16).astype(F32) * value
    for b in range(blocks):
        weights = jnp.exp(scores[:, b * rows : (b + 1) * rows] - top)
        total = total + jnp.sum(weights, axis=1, keepdims=True)
        acc = acc + jnp.dot(
            weights.astype(BF16),
            cache[b * rows : (b + 1) * rows, LANES:],
            preferred_element_type=F32,
        )
    heads_out[...] = (acc / total).astype(BF16)
    for copy in w_copies:
        copy.wait()


def out_kernel(tp, places, w_out, *rest):
    parts = rest[:tp]
    out, left = rest[-2:]
    docs = out.shape[0]
    row = lax.broadcasted_iota(jnp.int32, (left.shape[0], LANES), 0)
    own = [parts[s][...].astype(F32) for s in range(tp)]
    for h in range(own[0].shape[0]):
        piece = jnp.zeros((left.shape[0], LANES), F32)
        for s in range(tp):
            piece = jnp.where(row == places[s : s + 1, :], own[s][h : h + 1, :], piece)
        left[:, h * LANES : (h + 1) * LANES] = piece
    terms = jnp.dot(left[...].astype(BF16), w_out[...], preferred_element_type=F32)
    out[...] = terms[:docs].astype(BF16)


def fetch_kernel(first, token, w, out, sems):
    if len(w.shape) == 3:
        w = w.reshape(w.shape[0] * w.shape[1], w.shape[2])
    copies = weight_copies(w, first, out, sems)
    for copy in copies:
        copy.start()
    for copy in copies:
        copy.wait()


def gate_up_kernel(kv, groups, states, gains, *rest):
    blocks, parts = rest[:groups], rest[groups : groups + kv]
    attn_out, partial_out, spread_buf, acc = rest[groups + kv :]
    docs, width = states.shape
    rows, hidden = blocks[0].shape[1:]
    attn = tree_sum([part[...].astype(F32) for part in parts]).astype(BF16)
    attn_out[...] = attn
    resid = (states[...].astype(F32) + attn.astype(F32)).astype(BF16).astype(F32)
    squares = jnp.sum(resid * resid, axis=1, keepdims=True)
    spread(two_parts(resid * gains[1:2, :]), spread_buf, docs)
    acc[...] = jnp.zeros_like(acc)

    first = 0
    for group in blocks:

        def step(b, carry, group=group, first=first):
            start = pl.multiple_of((first + b) * rows, rows)
            acc[...] += jnp.dot(
                spread_buf[:, pl.ds(start, rows)], group[b], preferred_element_type=F32
            )
            return carry

        lax.fori_loop(0, group.shape[0], step, 0)
        first += group.shape[0]
    partial_out[:, :hidden] = (acc[: 2 * docs] + acc[2 * docs :]).astype(BF16)
    lane = lax.broadcasted_iota(jnp.int32, (docs, LANES), 1)
    first = squares.astype(BF16).astype(F32)
    second = (squares - first).astype(BF16).astype(F32)
    third = squares - first - second
    terms = jnp.where(lane == 0, first, jnp.where(lane == 1, second, jnp.where(lane == 2, third, 0.0)))
    partial_out[:, hidden:] = jnp.concatenate([terms, terms], axis=0).astype(BF16)


def down_kernel(tp, w_down, *rest):
    parts = rest[:tp]
    out, act_buf, acc = rest[tp:]
    docs = out.shape[0]
    blocks, step_rows = w_down.shape[:2]
    hidden = blocks * step_rows
    summed = tree_sum([part[...].astype(F32) for part in parts])
    squares = jnp.sum(summed[:docs, hidden:], axis=1, keepdims=True)
    inverse = lax.rsqrt(squares / D + EPS)
    gate = summed[:docs, :hidden] * inverse
    up = summed[docs:, :hidden] * inverse
    act_buf[...] = (gate / (1.0 + jnp.exp(-gate)) * up).astype(BF16)
    acc[...] = jnp.zeros_like(acc)

    def step(b, carry):
        start = pl.multiple_of(b * step_rows, step_rows)
        acc[...] += jnp.dot(
            act_buf[:, pl.ds(start, step_rows)],
            w_down[b],
            preferred_element_type=F32,
        )
        return carry

    lax.fori_loop(0, blocks, step, 0)
    out[...] = acc[...].astype(BF16)


def cost(micros):
    return pl.CostEstimate(flops=0, bytes_accessed=int(micros * 3.69e6), transcendentals=0)


def params(docs, mib):
    return pltpu.CompilerParams(vmem_limit_bytes=(mib if docs <= 8 else mib + 24) * MIB)


def per_device(
    tp, kv,
    states, norm_gains, w_query, w_keyval, w_out, w_gate_up, w_down, kv_cache, lengths, owner_rows
):
    docs, width = states.shape
    heads = w_query.shape[1]
    cache_len = kv_cache.shape[1]
    hidden = w_gate_up.shape[2]
    wq = w_query.reshape(width, heads // 2, 2, LANES)
    wkv = w_keyval.reshape(width, 2 * LANES)
    cache = kv_cache.reshape(cache_len, 2 * LANES)
    packed = 2 * heads
    pairs = heads // 2
    halves = 2

    half = LANES // 2
    freq = ROPE_BASE ** (-(np.arange(half, dtype=np.float64) * 2.0 / LANES))
    freq = jnp.asarray(np.concatenate([freq, freq]).astype(np.float32)[None, :])
    *qkv_parts, table, places = pl.pallas_call(
        functools.partial(qkv_kernel, tp),
        out_shape=[jax.ShapeDtypeStruct((packed, LANES), F32)] * tp
        + [
            jax.ShapeDtypeStruct((8, LANES), F32),
            jax.ShapeDtypeStruct((max(tp, 8), LANES), jnp.int32),
        ],
        in_specs=[hbm()] * 7,
        out_specs=[vmem()] * (tp + 2),
        scratch_shapes=[
            pltpu.SMEM((docs,), jnp.int32),
            pltpu.SMEM((docs,), jnp.int32),
            pltpu.VMEM((1, LANES), F32),
            pltpu.VMEM((docs, width), BF16),
            pltpu.VMEM((2, width), F32),
            pltpu.VMEM((halves, pairs, width // halves, 2, LANES), BF16),
            pltpu.VMEM((width, 2 * LANES), BF16),
            pltpu.VMEM((4 * docs, 2 * width), BF16),
            pltpu.VMEM((2 * docs, pairs * LANES), F32),
            pltpu.VMEM((2 * docs, 2 * LANES), F32),
            pltpu.VMEM((docs, LANES), F32),
            pltpu.SemaphoreType.DMA((halves * pairs + 1,)),
            pltpu.SemaphoreType.DMA((5,)),
        ],
        compiler_params=params(docs, 10),
        cost_estimate=cost(8),
        name="qkv",
    )(*(in_hbm(a) for a in (owner_rows, lengths, freq, states, norm_gains, wq, wkv)))
    w_gu = in_hbm(w_gate_up)
    gu_blocks = 2 * width // GU_BLOCK
    bounds = sorted({gu_blocks * i // 16 for i in (0, 5, 8, 13, 16)})
    shares = list(zip(bounds, bounds[1:]))
    fetched = []

    def blocks_of(share, rows=GU_BLOCK, columns=hidden):
        return pltpu.VMEM((share[1] - share[0], rows, columns), BF16)

    def fetch(weights, share, token, *block):
        return pl.pallas_call(
            functools.partial(fetch_kernel, share[0]),
            out_shape=blocks_of(share, *block),
            in_specs=[hbm(), hbm()],
            out_specs=vmem(),
            scratch_shapes=[pltpu.SemaphoreType.DMA((share[1] - share[0],))],
            compiler_params=params(docs, 2),
            cost_estimate=cost(0.5 * (share[1] - share[0])),
            name="fetch",
        )(token, weights)

    if len(shares) == 4:
        fetched.append(fetch(w_gu, shares[0], table))
    qkv_parts = exchange(qkv_parts, "tp", tp)
    own_share = shares[1] if len(shares) == 4 else shares[0]
    head_out, new_kv, w_ready = pl.pallas_call(
        functools.partial(attend_kernel, tp, heads, 512, own_share[0]),
        out_shape=[
            jax.ShapeDtypeStruct((heads, LANES), BF16),
            jax.ShapeDtypeStruct((1, 2 * LANES), BF16),
            blocks_of(own_share),
        ],
        in_specs=[vmem(), vmem(), hbm()] + [vmem()] * tp + [hbm()] * len(fetched),
        out_specs=[vmem()] * 3,
        scratch_shapes=[
            pltpu.VMEM((heads, cache_len), F32),
            pltpu.SemaphoreType.DMA((own_share[1] - own_share[0],)),
        ],
        compiler_params=params(docs, 6),
        cost_estimate=cost(8),
        name="attend",
    )(table, cache, w_gu, *qkv_parts, *fetched)
    fetched.append(w_ready)

    if len(shares) == 4:
        fetched.append(fetch(w_gu, shares[2], head_out))
    head_parts = exchange([head_out] * tp, "tp", tp)
    out_part = pl.pallas_call(
        functools.partial(out_kernel, tp),
        out_shape=jax.ShapeDtypeStruct((docs, width), BF16),
        in_specs=[vmem()] * (tp + 2) + [hbm()],
        out_specs=vmem(),
        scratch_shapes=[pltpu.VMEM((max(docs, 8), heads * LANES), F32)],
        compiler_params=params(docs, 6),
        cost_estimate=cost(6),
        name="attn_project",
    )(places, w_out, *head_parts, fetched[-1])

    fetched.append(fetch(w_gu, shares[-1], out_part))
    out_parts = exchange([out_part] * kv, "kv", kv)
    attn_out, gu_part = pl.pallas_call(
        functools.partial(gate_up_kernel, kv, len(fetched)),
        out_shape=[
            jax.ShapeDtypeStruct((docs, width), BF16),
            jax.ShapeDtypeStruct((2 * docs, hidden + LANES), BF16),
        ],
        in_specs=[vmem()] * (2 + len(fetched) + kv),
        out_specs=[vmem(), vmem()],
        scratch_shapes=[
            pltpu.VMEM((4 * docs, 2 * width), BF16),
            pltpu.VMEM((4 * docs, hidden), F32),
        ],
        compiler_params=params(docs, 6),
        cost_estimate=cost(10),
        name="gate_up",
    )(states, norm_gains, *fetched, *out_parts)

    w_down_ready = fetch(in_hbm(w_down), (0, hidden // DOWN_BLOCK), gu_part, DOWN_BLOCK, width)
    gu_parts = exchange([gu_part] * tp, "tp", tp)
    ffn_part = pl.pallas_call(
        functools.partial(down_kernel, tp),
        out_shape=jax.ShapeDtypeStruct((docs, width), BF16),
        in_specs=[vmem()] + [vmem()] * tp,
        out_specs=vmem(),
        scratch_shapes=[pltpu.VMEM((docs, hidden), BF16), pltpu.VMEM((docs, width), F32)],
        compiler_params=params(docs, 6),
        cost_estimate=cost(5),
        name="down",
    )(w_down_ready, *gu_parts)
    ffn_parts = exchange([ffn_part] * kv, "kv", kv)
    ffn_out = tree_sum([part.astype(F32) for part in ffn_parts]).astype(BF16)
    return attn_out, ffn_out, new_kv.reshape(1, 1, 2 * LANES)


def solution(mesh):
    return jax.shard_map(
        functools.partial(per_device, mesh.shape["tp"], mesh.shape["kv"]),
        mesh=mesh,
        in_specs=(
            P("grp", "tp"),
            P(None, "tp"),
            P("tp", "kv", None),
            P("tp", "kv", None),
            P("kv", "tp"),
            P("tp", None, "kv"),
            P("kv", "tp"),
            P(("grp", "tp"), None, "kv", None),
            P("grp"),
            P("grp"),
        ),
        out_specs=(P("grp", "tp"), P("grp", "tp"), P(("grp", "tp"), "kv", None)),
        check_vma=False,
    )
```

```python
import functools
import math

import jax
import jax.numpy as jnp
import numpy as np
from jax import lax
from jax.experimental import pallas as pl
from jax.experimental.pallas import tpu as pltpu
from jax.sharding import PartitionSpec as P

D = 8192
EPS = 1e-05
ROPE_BASE = 500000.0
LANES = 128
MIB = 1 << 20
GU_SHARES = (4, 6, 4, 2, 12)
F32 = jnp.float32
BF16 = jnp.bfloat16
TURN_A = 6.28125
TURN_B = 0.0019340515136718750
TURN_C = 2.0 * math.pi - TURN_A - TURN_B


def vmem():
    return pl.BlockSpec(memory_space=pltpu.VMEM)


def hbm():
    return pl.BlockSpec(memory_space=pltpu.HBM)


def in_hbm(array):
    return pltpu.with_memory_space_constraint(array, pltpu.HBM)


def exchange(arrays, axis, size):
    return [arrays[0]] + [
        lax.ppermute(arrays[s], axis, [(i, i ^ s) for i in range(size)])
        for s in range(1, size)
    ]


def tree_sum(parts):
    while len(parts) > 1:
        parts = [a + b for a, b in zip(parts[::2], parts[1::2])]
    return parts[0]


def two_parts(scaled):
    high = scaled.astype(BF16).astype(F32)
    low = scaled - high
    return jnp.concatenate([high, high, low, low], axis=0).astype(BF16)


def spread(rows16, out_ref, docs):
    width = rows16.shape[1]
    source = lax.broadcasted_iota(jnp.int32, (LANES, 2 * LANES), 0)
    target = lax.broadcasted_iota(jnp.int32, (LANES, 2 * LANES), 1)
    pick = (lax.shift_right_logical(target, 1) == source).astype(F32).astype(BF16)
    row = lax.broadcasted_iota(jnp.int32, (4 * docs, 2 * LANES), 0)
    lane = lax.broadcasted_iota(jnp.int32, (4 * docs, 2 * LANES), 1)
    keep = lax.rem(lax.div(row, docs), 2) == lax.rem(lane, 2)
    chunks = width // LANES
    stacked = jnp.concatenate(
        [rows16[:, c * LANES : (c + 1) * LANES] for c in range(chunks)], axis=0
    )
    doubled = jnp.dot(stacked, pick, preferred_element_type=F32)
    for c in range(chunks):
        piece = doubled[c * 4 * docs : (c + 1) * 4 * docs]
        out_ref[:, 2 * c * LANES : 2 * (c + 1) * LANES] = jnp.where(keep, piece, 0.0).astype(BF16)


def tile_copies(matrix, first, buf, sems):
    return [
        pltpu.make_async_copy(
            matrix.at[:, pl.ds((first + i) * LANES, LANES)], buf.at[i], sems.at[i]
        )
        for i in range(buf.shape[0])
    ]


def matrix_of(w):
    return w if len(w.shape) == 2 else w.reshape(w.shape[0] * w.shape[1], w.shape[2])


def times_tiles(left, tiles, store, tile_ready=None):
    def step(j, carry):
        if tile_ready is not None:
            tile_ready(2 * j)
            tile_ready(2 * j + 1)
        pair = jnp.concatenate([tiles[2 * j], tiles[2 * j + 1]], axis=1)
        store(j, jnp.dot(left[...], pair, preferred_element_type=F32))
        return carry

    lax.fori_loop(0, tiles.shape[0] // 2, step, 0)


def pick_row(ref, index):
    row = lax.broadcasted_iota(jnp.int32, ref.shape, 0)
    return jnp.sum(jnp.where(row == index, ref[...], 0.0), axis=0, keepdims=True)


def rope_rows(length, frequency):
    angle = length * frequency
    turns = jnp.floor(angle * (0.5 / math.pi) + 0.5)
    angle = ((angle - turns * TURN_A) - turns * TURN_B) - turns * TURN_C
    lane = lax.broadcasted_iota(jnp.int32, (1, LANES), 1)
    sine = jnp.sin(angle)
    return jnp.cos(angle), jnp.where(lane < LANES // 2, -sine, sine)


def qkv_kernel(
    tp, owner_hbm, lengths_hbm, frequency_hbm, states_hbm, gains_hbm, wq, wkv, cache, *rest
):
    outs = rest[:tp]
    table, places, cache_tiles = rest[tp : tp + 3]
    owner, lengths, frequency, states, gains = rest[tp + 3 : tp + 8]
    wq_buf, wkv_buf, spread_buf, res, kv_res, sq_res, sems, small_sems, cache_sems = rest[tp + 8 :]
    cache_copies = tile_copies(cache, 0, cache_tiles, cache_sems)
    docs, width = states.shape
    pairs = wq.shape[1]
    halves = wq_buf.shape[0]
    rows = 2 * width // halves
    small = [
        pltpu.make_async_copy(source, target, small_sems.at[i])
        for i, (source, target) in enumerate(
            [
                (states_hbm, states),
                (gains_hbm, gains),
                (owner_hbm, owner),
                (lengths_hbm, lengths),
                (frequency_hbm, frequency),
            ]
        )
    ]
    for copy in small:
        copy.start()
    kv_copy = pltpu.make_async_copy(wkv, wkv_buf, sems.at[halves * pairs])
    kv_copy.start()
    copies = []
    for c in range(halves):
        for p in range(pairs):
            copies.append(
                pltpu.make_async_copy(
                    wq.at[pl.ds(c * rows // 2, rows // 2), p],
                    wq_buf.at[c, p],
                    sems.at[c * pairs + p],
                )
            )
    for copy in copies:
        copy.start()
    for copy in small:
        copy.wait()
    me = lax.axis_index("tp")
    x = states[...].astype(F32)
    sq_res[...] = jnp.broadcast_to(jnp.sum(x * x, axis=1, keepdims=True), sq_res.shape)
    rows16 = two_parts(x * gains[0:1, :])
    spread(rows16, spread_buf, docs)
    length = lengths[owner[me]].astype(F32)
    cosine, sine = rope_rows(length, frequency[...])
    table[0:1, :] = cosine
    table[1:2, :] = sine
    table[2:3, :] = jnp.full((1, LANES), length, F32)
    table[3:, :] = jnp.zeros((table.shape[0] - 3, LANES), F32)
    for s in range(tp):
        places[s : s + 1, :] = jnp.full((1, LANES), owner[me ^ s], jnp.int32)
    kv_copy.wait()
    kv_total = jnp.dot(rows16, wkv_buf[...], preferred_element_type=F32)
    kv_res[...] = kv_total[: 2 * docs] + kv_total[2 * docs :]
    total = jnp.zeros((4 * docs, pairs * LANES), F32)
    for c in range(halves):
        for p in range(pairs):
            copies[c * pairs + p].wait()
        if c == 0:
            for copy in cache_copies:
                copy.start()
        block = jnp.concatenate(
            [wq_buf.at[c, p].reshape(rows, LANES)[...] for p in range(pairs)], axis=1
        )
        total = total + jnp.dot(
            spread_buf[:, c * rows : (c + 1) * rows], block, preferred_element_type=F32
        )
    res[...] = total[: 2 * docs] + total[2 * docs :]
    for s in range(tp):
        doc = owner[me ^ s]
        for parity in range(2):
            chosen = pick_row(res, parity * docs + doc)
            for p in range(pairs):
                outs[s][2 * p + parity : 2 * p + parity + 1, :] = chosen[
                    :, p * LANES : (p + 1) * LANES
                ]
        chosen = pick_row(kv_res, doc)
        h = 2 * pairs
        outs[s][h : h + 1, :] = chosen[:, :LANES]
        outs[s][h + 1 : h + 2, :] = chosen[:, LANES:]
        outs[s][h + 2 : h + 3, :] = pick_row(sq_res, doc)
        outs[s][h + 3 :, :] = jnp.zeros((outs[s].shape[0] - h - 3, LANES), F32)
    for copy in cache_copies:
        copy.wait()


def attend_kernel(tp, heads, rows, first, table, cache, w, *rest):
    parts = rest[:tp]
    heads_out, new_kv_out, w_ready, scores, w_sems = rest[-5:]
    w_copies = tile_copies(matrix_of(w), first, w_ready, w_sems)
    for copy in w_copies:
        copy.start()
    blocks = cache.shape[1] // rows
    sums = tree_sum([part[...] for part in parts])
    sums = sums * lax.rsqrt(sums[heads + 2 : heads + 3, :] / D + EPS)
    rotated = sums * table[0:1, :] + pltpu.roll(sums, LANES // 2, 1) * table[1:2, :]
    query = rotated[:heads].astype(BF16)
    key = rotated[heads : heads + 1].astype(BF16)
    value = sums[heads + 1 : heads + 2].astype(BF16)
    new_kv_out[:, :LANES] = key
    new_kv_out[:, LANES:] = value
    key = key.astype(F32)
    value = value.astype(F32)
    scale = LANES ** (-0.5)
    own = jnp.sum(query.astype(F32) * key, axis=1, keepdims=True) * scale
    column = lax.broadcasted_iota(jnp.int32, (heads, rows), 1).astype(F32)
    length = table[2:3, 0:1]
    top = own
    for b in range(blocks):
        block = lax.dot_general(
            query,
            cache[0, b * rows : (b + 1) * rows, :],
            (((1,), (1,)), ((), ())),
            preferred_element_type=F32,
        )
        block = jnp.where(column < length - b * rows, block * scale, -jnp.inf)
        top = jnp.maximum(top, jnp.max(block, axis=1, keepdims=True))
        scores[:, b * rows : (b + 1) * rows] = block
    own = jnp.exp(own - top)
    total = own
    acc = own.astype(BF16).astype(F32) * value
    for b in range(blocks):
        weights = jnp.exp(scores[:, b * rows : (b + 1) * rows] - top)
        total = total + jnp.sum(weights, axis=1, keepdims=True)
        acc = acc + jnp.dot(
            weights.astype(BF16),
            cache[1, b * rows : (b + 1) * rows, :],
            preferred_element_type=F32,
        )
    heads_out[...] = (acc / total).astype(BF16)
    for copy in w_copies:
        copy.wait()


def out_kernel(tp, places, w_out, *rest):
    parts = rest[:tp]
    out, left = rest[-2:]
    docs = out.shape[0]
    row = lax.broadcasted_iota(jnp.int32, (left.shape[0], LANES), 0)
    own = [parts[s][...].astype(F32) for s in range(tp)]
    for h in range(own[0].shape[0]):
        piece = jnp.zeros((left.shape[0], LANES), F32)
        for s in range(tp):
            piece = jnp.where(row == places[s : s + 1, :], own[s][h : h + 1, :], piece)
        left[:, h * LANES : (h + 1) * LANES] = piece
    terms = jnp.dot(left[...].astype(BF16), w_out[...], preferred_element_type=F32)
    out[...] = terms[:docs].astype(BF16)


def fetch_kernel(first, token, w, out, sems):
    copies = tile_copies(matrix_of(w), first, out, sems)
    for copy in copies:
        copy.start()
    for copy in copies:
        copy.wait()


def gate_up_kernel(kv, groups, first, states, gains, w, *rest):
    ready, parts = rest[:groups], rest[groups : groups + kv]
    attn_out, partial_out, w_tiles, spread_buf, w_sems = rest[groups + kv :]
    docs, width = states.shape
    hidden = w.shape[2]
    w_matrix = matrix_of(w)
    for copy in tile_copies(w_matrix, first, w_tiles, w_sems):
        copy.start()
    attn = tree_sum([part[...].astype(F32) for part in parts]).astype(BF16)
    attn_out[...] = attn
    resid = (states[...].astype(F32) + attn.astype(F32)).astype(BF16).astype(F32)
    squares = jnp.sum(resid * resid, axis=1, keepdims=True)
    spread(two_parts(resid * gains[1:2, :]), spread_buf, docs)

    def store_from(tile):
        def store(j, product):
            start = pl.multiple_of((tile + 2 * j) * LANES, 2 * LANES)
            summed = product[: 2 * docs] + product[2 * docs :]
            partial_out[:, pl.ds(start, 2 * LANES)] = summed.astype(BF16)

        return store

    def tile_ready(i):
        pltpu.make_async_copy(
            w_matrix.at[:, pl.ds(pl.multiple_of((first + i) * LANES, LANES), LANES)],
            w_tiles.at[i],
            w_sems.at[i],
        ).wait()

    tile = 0
    for group in ready:
        times_tiles(spread_buf, group, store_from(tile))
        tile += group.shape[0]
    times_tiles(spread_buf, w_tiles, store_from(tile), tile_ready)
    lane = lax.broadcasted_iota(jnp.int32, (docs, LANES), 1)
    first = squares.astype(BF16).astype(F32)
    second = (squares - first).astype(BF16).astype(F32)
    third = squares - first - second
    terms = jnp.where(lane == 0, first, jnp.where(lane == 1, second, jnp.where(lane == 2, third, 0.0)))
    partial_out[:, hidden:] = jnp.concatenate([terms, terms], axis=0).astype(BF16)


def down_kernel(tp, w_down, *rest):
    parts = rest[:tp]
    out, act_buf = rest[tp:]
    docs = out.shape[0]
    hidden = w_down.shape[1]
    summed = tree_sum([part[...].astype(F32) for part in parts])
    squares = jnp.sum(summed[:docs, hidden:], axis=1, keepdims=True)
    inverse = lax.rsqrt(squares / D + EPS)
    gate = summed[:docs, :hidden] * inverse
    up = summed[docs:, :hidden] * inverse
    act_buf[...] = (gate / (1.0 + jnp.exp(-gate)) * up).astype(BF16)

    def store(j, product):
        start = pl.multiple_of(2 * j * LANES, 2 * LANES)
        out[:, pl.ds(start, 2 * LANES)] = product.astype(BF16)

    times_tiles(act_buf, w_down, store)


def cost(micros):
    return pl.CostEstimate(flops=0, bytes_accessed=int(micros * 3.69e6), transcendentals=0)


def params(docs, mib):
    return pltpu.CompilerParams(vmem_limit_bytes=(mib if docs <= 8 else mib + 24) * MIB)


def per_device(
    tp, kv,
    states, norm_gains, w_query, w_keyval, w_out, w_gate_up, w_down, kv_cache, lengths, owner_rows
):
    docs, width = states.shape
    heads = w_query.shape[1]
    cache_len = kv_cache.shape[1]
    hidden = w_gate_up.shape[2]
    wq = w_query.reshape(width, heads // 2, 2, LANES)
    wkv = w_keyval.reshape(width, 2 * LANES)
    cache = kv_cache.reshape(cache_len, 2 * LANES)
    packed = 2 * heads
    pairs = heads // 2
    halves = 2

    half = LANES // 2
    freq = ROPE_BASE ** (-(np.arange(half, dtype=np.float64) * 2.0 / LANES))
    freq = jnp.asarray(np.concatenate([freq, freq]).astype(np.float32)[None, :])
    *qkv_parts, table, places, cache_tiles = pl.pallas_call(
        functools.partial(qkv_kernel, tp),
        out_shape=[jax.ShapeDtypeStruct((packed, LANES), F32)] * tp
        + [
            jax.ShapeDtypeStruct((8, LANES), F32),
            jax.ShapeDtypeStruct((max(tp, 8), LANES), jnp.int32),
            pltpu.VMEM((2, cache_len, LANES), BF16),
        ],
        in_specs=[hbm()] * 8,
        out_specs=[vmem()] * (tp + 3),
        scratch_shapes=[
            pltpu.SMEM((docs,), jnp.int32),
            pltpu.SMEM((docs,), jnp.int32),
            pltpu.VMEM((1, LANES), F32),
            pltpu.VMEM((docs, width), BF16),
            pltpu.VMEM((2, width), F32),
            pltpu.VMEM((halves, pairs, width // halves, 2, LANES), BF16),
            pltpu.VMEM((width, 2 * LANES), BF16),
            pltpu.VMEM((4 * docs, 2 * width), BF16),
            pltpu.VMEM((2 * docs, pairs * LANES), F32),
            pltpu.VMEM((2 * docs, 2 * LANES), F32),
            pltpu.VMEM((docs, LANES), F32),
            pltpu.SemaphoreType.DMA((halves * pairs + 1,)),
            pltpu.SemaphoreType.DMA((5,)),
            pltpu.SemaphoreType.DMA((2,)),
        ],
        compiler_params=params(docs, 10),
        cost_estimate=cost(8),
        name="qkv",
    )(*(in_hbm(a) for a in (owner_rows, lengths, freq, states, norm_gains, wq, wkv, cache)))
    w_gu = in_hbm(w_gate_up)
    bounds = np.cumsum([0] + [hidden // LANES * n // 28 for n in GU_SHARES]).tolist()
    shares = list(zip(bounds, bounds[1:]))
    fetched = []

    def tiles_of(share, rows):
        return pltpu.VMEM((share[1] - share[0], rows, LANES), BF16)

    def fetch(weights, share, rows, token):
        return pl.pallas_call(
            functools.partial(fetch_kernel, share[0]),
            out_shape=tiles_of(share, rows),
            in_specs=[hbm(), hbm()],
            out_specs=vmem(),
            scratch_shapes=[pltpu.SemaphoreType.DMA((share[1] - share[0],))],
            compiler_params=params(docs, 2),
            cost_estimate=cost(0.3 * (share[1] - share[0])),
            name="fetch",
        )(token, weights)

    fetched.append(fetch(w_gu, shares[0], 2 * width, table))
    qkv_parts = exchange(qkv_parts, "tp", tp)
    head_out, new_kv, w_ready = pl.pallas_call(
        functools.partial(attend_kernel, tp, heads, 512, shares[1][0]),
        out_shape=[
            jax.ShapeDtypeStruct((heads, LANES), BF16),
            jax.ShapeDtypeStruct((1, 2 * LANES), BF16),
            tiles_of(shares[1], 2 * width),
        ],
        in_specs=[vmem(), vmem(), hbm()] + [vmem()] * tp + [hbm()] * len(fetched),
        out_specs=[vmem()] * 3,
        scratch_shapes=[
            pltpu.VMEM((heads, cache_len), F32),
            pltpu.SemaphoreType.DMA((shares[1][1] - shares[1][0],)),
        ],
        compiler_params=params(docs, 6),
        cost_estimate=cost(8),
        name="attend",
    )(table, cache_tiles, w_gu, *qkv_parts, *fetched)
    fetched.append(w_ready)

    fetched.append(fetch(w_gu, shares[2], 2 * width, head_out))
    head_parts = exchange([head_out] * tp, "tp", tp)
    out_part = pl.pallas_call(
        functools.partial(out_kernel, tp),
        out_shape=jax.ShapeDtypeStruct((docs, width), BF16),
        in_specs=[vmem()] * (tp + 2) + [hbm()],
        out_specs=vmem(),
        scratch_shapes=[pltpu.VMEM((max(docs, 8), heads * LANES), F32)],
        compiler_params=params(docs, 6),
        cost_estimate=cost(6),
        name="attn_project",
    )(places, w_out, *head_parts, fetched[-1])

    fetched.append(fetch(w_gu, shares[3], 2 * width, out_part))
    out_parts = exchange([out_part] * kv, "kv", kv)
    attn_out, gu_part = pl.pallas_call(
        functools.partial(gate_up_kernel, kv, len(fetched), shares[4][0]),
        out_shape=[
            jax.ShapeDtypeStruct((docs, width), BF16),
            jax.ShapeDtypeStruct((2 * docs, hidden + LANES), BF16),
        ],
        in_specs=[vmem(), vmem(), hbm()] + [vmem()] * (len(fetched) + kv),
        out_specs=[vmem(), vmem()],
        scratch_shapes=[
            tiles_of(shares[4], 2 * width),
            pltpu.VMEM((4 * docs, 2 * width), BF16),
            pltpu.SemaphoreType.DMA((shares[4][1] - shares[4][0],)),
        ],
        compiler_params=params(docs, 20),
        cost_estimate=cost(10),
        name="gate_up",
    )(states, norm_gains, w_gu, *fetched, *out_parts)

    w_down_ready = fetch(in_hbm(w_down), (0, width // LANES), hidden, gu_part)
    gu_parts = exchange([gu_part] * tp, "tp", tp)
    ffn_part = pl.pallas_call(
        functools.partial(down_kernel, tp),
        out_shape=jax.ShapeDtypeStruct((docs, width), BF16),
        in_specs=[vmem()] + [vmem()] * tp,
        out_specs=vmem(),
        scratch_shapes=[pltpu.VMEM((docs, hidden), BF16)],
        compiler_params=params(docs, 6),
        cost_estimate=cost(5),
        name="down",
    )(w_down_ready, *gu_parts)
    ffn_parts = exchange([ffn_part] * kv, "kv", kv)
    ffn_out = tree_sum([part.astype(F32) for part in ffn_parts]).astype(BF16)
    return attn_out, ffn_out, new_kv.reshape(1, 1, 2 * LANES)


def solution(mesh):
    return jax.shard_map(
        functools.partial(per_device, mesh.shape["tp"], mesh.shape["kv"]),
        mesh=mesh,
        in_specs=(
            P("grp", "tp"),
            P(None, "tp"),
            P("tp", "kv", None),
            P("tp", "kv", None),
            P("kv", "tp"),
            P("tp", None, "kv"),
            P("kv", "tp"),
            P(("grp", "tp"), None, "kv", None),
            P("grp"),
            P("grp"),
        ),
        out_specs=(P("grp", "tp"), P("grp", "tp"), P(("grp", "tp"), "kv", None)),
        check_vma=False,
    )
```

```python
import functools
import math

import jax
import jax.numpy as jnp
import numpy as np
from jax import lax
from jax.experimental import pallas as pl
from jax.experimental.pallas import tpu as pltpu
from jax.sharding import PartitionSpec as P

D = 8192
EPS = 1e-05
ROPE_BASE = 500000.0
LANES = 128
MIB = 1 << 20
GU_SHARES = (6, 4, 6, 4, 8)
F32 = jnp.float32
BF16 = jnp.bfloat16
QUARTER = (1.5703125, 4.837512969970703125e-4, 7.549789948768648e-8)
SIN = (-1.9515295891e-4, 8.3321608736e-3, -1.6666654611e-1)
COS = (2.443315711809948e-5, -1.388731625493765e-3, 4.166664568298827e-2)


def vmem():
    return pl.BlockSpec(memory_space=pltpu.VMEM)


def hbm():
    return pl.BlockSpec(memory_space=pltpu.HBM)


def in_hbm(array):
    return pltpu.with_memory_space_constraint(array, pltpu.HBM)


def exchange(arrays, axis, size):
    got = [
        lax.ppermute(arrays[s], axis, [(i, i ^ s) for i in range(size)])
        for s in reversed(range(1, size))
    ]
    return [arrays[0]] + got[::-1]


def tree_sum(parts):
    while len(parts) > 1:
        parts = [a + b for a, b in zip(parts[::2], parts[1::2])]
    return parts[0]


def two_parts(scaled):
    high = scaled.astype(BF16).astype(F32)
    return high, scaled - high


def spread(rows16, out_ref, docs):
    width = rows16.shape[1]
    pick = one_hot_spread(2)
    row = lax.broadcasted_iota(jnp.int32, (4 * docs, 2 * LANES), 0)
    lane = lax.broadcasted_iota(jnp.int32, (4 * docs, 2 * LANES), 1)
    keep = lax.rem(lax.div(row, docs), 2) == lax.rem(lane, 2)
    chunks = width // LANES
    stacked = jnp.concatenate(
        [rows16[:, c * LANES : (c + 1) * LANES] for c in range(chunks)], axis=0
    )
    doubled = jnp.dot(stacked, pick, preferred_element_type=F32)
    for c in range(chunks):
        piece = doubled[c * 4 * docs : (c + 1) * 4 * docs]
        out_ref[:, 2 * c * LANES : 2 * (c + 1) * LANES] = jnp.where(keep, piece, 0.0).astype(BF16)


def tile_copies(matrix, first, buf, sems):
    return [
        pltpu.make_async_copy(
            matrix.at[:, pl.ds((first + i) * LANES, LANES)], buf.at[i], sems.at[i]
        )
        for i in range(buf.shape[0])
    ]


def matrix_of(w):
    return w if len(w.shape) == 2 else w.reshape(w.shape[0] * w.shape[1], w.shape[2])


def times_tiles(left, tiles, store, tile_ready=None):
    def step(j, carry):
        if tile_ready is not None:
            tile_ready(2 * j)
            tile_ready(2 * j + 1)
        pair = jnp.concatenate([tiles[2 * j], tiles[2 * j + 1]], axis=1)
        store(j, jnp.dot(left[...], pair, preferred_element_type=F32))
        return carry

    lax.fori_loop(0, tiles.shape[0] // 2, step, 0)


def pick_doc(value, doc, docs):
    axis = value.ndim - 2
    row = lax.broadcasted_iota(jnp.int32, value.shape, axis)
    return jnp.sum(jnp.where(lax.rem(row, docs) == doc, value, 0.0), axis=axis)


def sine_cosine(angle):
    turns = jnp.floor(angle * (2.0 / math.pi) + 0.5)
    rest = ((angle - turns * QUARTER[0]) - turns * QUARTER[1]) - turns * QUARTER[2]
    square = rest * rest
    sine = rest + rest * square * ((SIN[0] * square + SIN[1]) * square + SIN[2])
    cosine = 1.0 - 0.5 * square + square * square * (
        (COS[0] * square + COS[1]) * square + COS[2]
    )
    quadrant = turns - 4.0 * jnp.floor(turns * 0.25)
    odd = (quadrant == 1.0) | (quadrant == 3.0)
    sine, cosine = jnp.where(odd, cosine, sine), jnp.where(odd, sine, cosine)
    return (
        jnp.where(quadrant >= 2.0, -sine, sine),
        jnp.where((quadrant == 1.0) | (quadrant == 2.0), -cosine, cosine),
    )


def rope_rows(length, frequency):
    sine, cosine = sine_cosine(length * frequency)
    lane = lax.broadcasted_iota(jnp.int32, (1, LANES), 1)
    return cosine, jnp.where(lane < LANES // 2, -sine, sine)


def one_hot_spread(fold):
    source = lax.broadcasted_iota(jnp.int32, (LANES, fold * LANES), 0)
    target = lax.broadcasted_iota(jnp.int32, (LANES, fold * LANES), 1)
    return (lax.div(target, fold) == source).astype(F32).astype(BF16)


def spread_heads(rows, out_ref, heads):
    count, width = rows.shape
    chunks = width // LANES
    stacked = jnp.concatenate([rows[:, c * LANES : (c + 1) * LANES] for c in range(chunks)], axis=0)
    wide = jnp.dot(stacked.astype(BF16), one_hot_spread(heads), preferred_element_type=F32)
    columns = heads * LANES
    lane = lax.rem(lax.broadcasted_iota(jnp.int32, (count, columns), 1), heads)
    for c in range(chunks):
        piece = wide[c * count : (c + 1) * count]
        for h in range(0, heads, 2):
            pair = [jnp.where(lane == h + i, piece, 0.0) for i in range(2)]
            out_ref[h * count : (h + 2) * count, c * columns : (c + 1) * columns] = (
                jnp.concatenate(pair, axis=0).astype(BF16)
            )


def qkv_kernel(
    tp, owner_hbm, lengths_hbm, frequency_hbm, states_hbm, gains_hbm, wq, wkv, cache, *rest
):
    outs = rest[:tp]
    table, places, cache_tiles = rest[tp : tp + 3]
    owner, lengths, frequency, states, gains = rest[tp + 3 : tp + 8]
    wq_buf, wkv_buf, spread_buf, sems, small_sems, cache_sems = rest[tp + 8 :]
    docs, width = states.shape
    heads = wq.shape[0] // width
    parts = wq_buf.shape[0]
    rows = wq_buf.shape[1]
    small = [
        pltpu.make_async_copy(source, target, small_sems.at[i])
        for i, (source, target) in enumerate(
            [
                (states_hbm, states),
                (gains_hbm, gains),
                (owner_hbm, owner),
                (lengths_hbm, lengths),
                (frequency_hbm, frequency),
            ]
        )
    ]
    copies = [
        pltpu.make_async_copy(wq.at[pl.ds(c * rows, rows)], wq_buf.at[c], sems.at[c])
        for c in range(parts)
    ]
    kv_copy = pltpu.make_async_copy(wkv, wkv_buf, sems.at[parts])
    cache_copies = tile_copies(cache, 0, cache_tiles, cache_sems)
    for copy in small + [kv_copy] + copies:
        copy.start()
    for copy in small:
        copy.wait()
    me = lax.axis_index("tp")
    x = states[...].astype(F32)
    squares = jnp.broadcast_to(jnp.sum(x * x, axis=1, keepdims=True), (docs, LANES))
    both = jnp.concatenate(two_parts(x * gains[0:1, :]), axis=0)
    spread_heads(both, spread_buf, heads)
    length = lengths[owner[me]].astype(F32)
    cosine, sine = rope_rows(length, frequency[...])
    table[0:1, :] = cosine
    table[1:2, :] = sine
    table[2:3, :] = jnp.full((1, LANES), length, F32)
    table[3:, :] = jnp.zeros((table.shape[0] - 3, LANES), F32)
    for s in range(tp):
        places[s : s + 1, :] = jnp.full((1, LANES), owner[me ^ s], jnp.int32)
    kv_copy.wait()
    kv_total = jnp.dot(both.astype(BF16), wkv_buf[...], preferred_element_type=F32)
    total = jnp.zeros((heads * 2 * docs, LANES), F32)
    for c in range(parts):
        copies[c].wait()
        if c == parts // 2:
            for copy in cache_copies:
                copy.start()
        total = total + jnp.dot(
            spread_buf[:, c * rows : (c + 1) * rows], wq_buf[c], preferred_element_type=F32
        )
    total = total.reshape(heads, 2 * docs, LANES)
    for s in range(tp):
        doc = owner[me ^ s]
        out = outs[-s]
        out[:heads, :] = pick_doc(total, doc, docs)
        kv_row = pick_doc(kv_total, doc, docs)[None]
        out[heads : heads + 1, :] = kv_row[:, :LANES]
        out[heads + 1 : heads + 2, :] = kv_row[:, LANES:]
        out[heads + 2 : heads + 3, :] = pick_doc(squares, doc, docs)[None]
        out[heads + 3 :, :] = jnp.zeros((out.shape[0] - heads - 3, LANES), F32)
    for copy in cache_copies:
        copy.wait()


def attend_kernel(tp, heads, rows, first, table, cache, w, *rest):
    parts = rest[:tp]
    heads_out, new_kv_out, w_ready, scores, w_sems = rest[-5:]
    w_copies = tile_copies(matrix_of(w), first, w_ready, w_sems)
    for copy in w_copies:
        copy.start()
    blocks = cache.shape[1] // rows
    sums = tree_sum([part[...] for part in parts])
    sums = sums * lax.rsqrt(sums[heads + 2 : heads + 3, :] / D + EPS)
    rotated = sums * table[0:1, :] + pltpu.roll(sums, LANES // 2, 1) * table[1:2, :]
    query = rotated[:heads].astype(BF16)
    key = rotated[heads : heads + 1].astype(BF16)
    value = sums[heads + 1 : heads + 2].astype(BF16)
    new_kv_out[:, :LANES] = key
    new_kv_out[:, LANES:] = value
    key = key.astype(F32)
    value = value.astype(F32)
    scale = LANES ** (-0.5)
    own = jnp.sum(query.astype(F32) * key, axis=1, keepdims=True) * scale
    column = lax.broadcasted_iota(jnp.int32, (heads, LANES), 1).astype(F32)
    length = table[2:3, :]
    tops = jnp.full((heads, LANES), -jnp.inf, F32)
    for b in range(blocks):
        block = lax.dot_general(
            query,
            cache[0, b * rows : (b + 1) * rows, :],
            (((1,), (1,)), ((), ())),
            preferred_element_type=F32,
        )
        for start in range(0, rows, LANES):
            at = b * rows + start
            piece = block[:, start : start + LANES] * scale
            piece = jnp.where(column < length - at, piece, -jnp.inf)
            tops = jnp.maximum(tops, piece)
            scores[:, at : at + LANES] = piece
    top = jnp.maximum(jnp.max(tops, axis=1, keepdims=True), own)
    own = jnp.exp(own - top)
    sums_by_lane = jnp.zeros((heads, LANES), F32)
    acc = own.astype(BF16).astype(F32) * value
    for b in range(blocks):
        weights = jnp.exp(scores[:, b * rows : (b + 1) * rows] - top)
        for start in range(0, rows, LANES):
            sums_by_lane = sums_by_lane + weights[:, start : start + LANES]
        acc = acc + jnp.dot(
            weights.astype(BF16),
            cache[1, b * rows : (b + 1) * rows, :],
            preferred_element_type=F32,
        )
    total = own + jnp.sum(sums_by_lane, axis=1, keepdims=True)
    heads_out[...] = (acc / total).astype(BF16)
    for copy in w_copies:
        copy.wait()


def out_kernel(tp, places, w_out, *rest):
    parts = rest[:tp]
    out, left = rest[-2:]
    docs = out.shape[0]
    row = lax.broadcasted_iota(jnp.int32, (left.shape[0], LANES), 0)
    own = [parts[s][...].astype(F32) for s in range(tp)]
    for h in range(own[0].shape[0]):
        piece = jnp.zeros((left.shape[0], LANES), F32)
        for s in range(tp):
            piece = jnp.where(row == places[s : s + 1, :], own[s][h : h + 1, :], piece)
        left[:, h * LANES : (h + 1) * LANES] = piece
    terms = jnp.dot(left[...].astype(BF16), w_out[...], preferred_element_type=F32)
    out[...] = terms[:docs].astype(BF16)


def fetch_kernel(first, token, w, out, sems):
    copies = tile_copies(matrix_of(w), first, out, sems)
    for copy in copies:
        copy.start()
    for copy in copies:
        copy.wait()


def gate_up_kernel(kv, groups, first, states, gains, w, w_down, *rest):
    ready, parts = rest[:groups], rest[groups : groups + kv]
    attn_out, partial_out, *down_tiles = rest[groups + kv : -4]
    w_tiles, spread_buf, w_sems, down_sems = rest[-4:]
    docs, width = states.shape
    hidden = w.shape[2]
    w_matrix = matrix_of(w)
    for copy in tile_copies(w_matrix, first, w_tiles, w_sems):
        copy.start()
    down_copies = [c for tiles in down_tiles for c in tile_copies(w_down, 0, tiles, down_sems)]
    for copy in down_copies:
        copy.start()
    attn = tree_sum([part[...].astype(F32) for part in parts]).astype(BF16)
    attn_out[...] = attn
    resid = (states[...].astype(F32) + attn.astype(F32)).astype(BF16).astype(F32)
    squares = jnp.sum(resid * resid, axis=1, keepdims=True)
    high, low = two_parts(resid * gains[1:2, :])
    spread(jnp.concatenate([high, high, low, low], axis=0).astype(BF16), spread_buf, docs)

    def store_from(tile):
        def store(j, product):
            start = pl.multiple_of((tile + 2 * j) * LANES, 2 * LANES)
            summed = product[: 2 * docs] + product[2 * docs :]
            partial_out[:, pl.ds(start, 2 * LANES)] = summed.astype(BF16)

        return store

    def tile_ready(i):
        pltpu.make_async_copy(
            w_matrix.at[:, pl.ds(pl.multiple_of((first + i) * LANES, LANES), LANES)],
            w_tiles.at[i],
            w_sems.at[i],
        ).wait()

    tile = 0
    for group in ready:
        times_tiles(spread_buf, group, store_from(tile))
        tile += group.shape[0]
    times_tiles(spread_buf, w_tiles, store_from(tile), tile_ready)
    lane = lax.broadcasted_iota(jnp.int32, (docs, LANES), 1)
    first = squares.astype(BF16).astype(F32)
    second = (squares - first).astype(BF16).astype(F32)
    third = squares - first - second
    terms = jnp.where(lane == 0, first, jnp.where(lane == 1, second, jnp.where(lane == 2, third, 0.0)))
    partial_out[:, hidden:] = jnp.concatenate([terms, terms], axis=0).astype(BF16)
    for copy in down_copies:
        copy.wait()


def down_kernel(tp, groups, *rest):
    ready, parts = rest[:groups], rest[groups : groups + tp]
    out, act_buf = rest[groups + tp :]
    docs = out.shape[0]
    hidden = ready[0].shape[1]
    summed = tree_sum([part[...].astype(F32) for part in parts])
    squares = jnp.sum(summed[:docs, hidden:], axis=1, keepdims=True)
    inverse = lax.rsqrt(squares / D + EPS)
    gate = summed[:docs, :hidden] * inverse
    up = summed[docs:, :hidden] * inverse
    act_buf[...] = (gate / (1.0 + jnp.exp(-gate)) * up).astype(BF16)

    def store_from(tile):
        def store(j, product):
            start = pl.multiple_of((tile + 2 * j) * LANES, 2 * LANES)
            out[:, pl.ds(start, 2 * LANES)] = product.astype(BF16)

        return store

    tile = 0
    for group in ready:
        times_tiles(act_buf, group, store_from(tile))
        tile += group.shape[0]


def cost(micros):
    return pl.CostEstimate(flops=0, bytes_accessed=int(micros * 3.69e6), transcendentals=0)


def params(docs, mib):
    return pltpu.CompilerParams(vmem_limit_bytes=(mib if docs <= 8 else mib + 24) * MIB)


def per_device(
    tp, kv,
    states, norm_gains, w_query, w_keyval, w_out, w_gate_up, w_down, kv_cache, lengths, owner_rows
):
    docs, width = states.shape
    heads = w_query.shape[1]
    cache_len = kv_cache.shape[1]
    hidden = w_gate_up.shape[2]
    wq = w_query.reshape(width * heads, LANES)
    wkv = w_keyval.reshape(width, 2 * LANES)
    cache = kv_cache.reshape(cache_len, 2 * LANES)
    packed = 2 * heads
    wq_parts = 4

    half = LANES // 2
    freq = ROPE_BASE ** (-(np.arange(half, dtype=np.float64) * 2.0 / LANES))
    freq = jnp.asarray(np.concatenate([freq, freq]).astype(np.float32)[None, :])
    *qkv_parts, table, places, cache_tiles = pl.pallas_call(
        functools.partial(qkv_kernel, tp),
        out_shape=[jax.ShapeDtypeStruct((packed, LANES), F32)] * tp
        + [
            jax.ShapeDtypeStruct((8, LANES), F32),
            jax.ShapeDtypeStruct((max(tp, 8), LANES), jnp.int32),
            pltpu.VMEM((2, cache_len, LANES), BF16),
        ],
        in_specs=[hbm()] * 8,
        out_specs=[vmem()] * (tp + 3),
        scratch_shapes=[
            pltpu.SMEM((docs,), jnp.int32),
            pltpu.SMEM((docs,), jnp.int32),
            pltpu.VMEM((1, LANES), F32),
            pltpu.VMEM((docs, width), BF16),
            pltpu.VMEM((2, width), F32),
            pltpu.VMEM((wq_parts, width * heads // wq_parts, LANES), BF16),
            pltpu.VMEM((width, 2 * LANES), BF16),
            pltpu.VMEM((heads * 2 * docs, width * heads), BF16),
            pltpu.SemaphoreType.DMA((wq_parts + 1,)),
            pltpu.SemaphoreType.DMA((5,)),
            pltpu.SemaphoreType.DMA((2,)),
        ],
        compiler_params=params(docs, 10),
        cost_estimate=cost(8),
        name="qkv",
    )(*(in_hbm(a) for a in (owner_rows, lengths, freq, states, norm_gains, wq, wkv, cache)))
    w_gu = in_hbm(w_gate_up)
    bounds = np.cumsum([0] + [hidden // LANES * n // 28 for n in GU_SHARES]).tolist()
    shares = list(zip(bounds, bounds[1:]))
    fetched = []

    def tiles_of(share, rows):
        return pltpu.VMEM((share[1] - share[0], rows, LANES), BF16)

    def fetch(weights, share, rows, token):
        return pl.pallas_call(
            functools.partial(fetch_kernel, share[0]),
            out_shape=tiles_of(share, rows),
            in_specs=[hbm(), hbm()],
            out_specs=vmem(),
            scratch_shapes=[pltpu.SemaphoreType.DMA((share[1] - share[0],))],
            compiler_params=params(docs, 2),
            cost_estimate=cost(0.3 * (share[1] - share[0])),
            name="fetch",
        )(token, weights)

    fetched.append(fetch(w_gu, shares[0], 2 * width, table))
    qkv_parts = exchange([qkv_parts[-s] for s in range(tp)], "tp", tp)
    head_out, new_kv, w_ready = pl.pallas_call(
        functools.partial(attend_kernel, tp, heads, 512, shares[1][0]),
        out_shape=[
            jax.ShapeDtypeStruct((heads, LANES), BF16),
            jax.ShapeDtypeStruct((1, 2 * LANES), BF16),
            tiles_of(shares[1], 2 * width),
        ],
        in_specs=[vmem(), vmem(), hbm()] + [vmem()] * tp + [hbm()] * len(fetched),
        out_specs=[vmem()] * 3,
        scratch_shapes=[
            pltpu.VMEM((heads, cache_len), F32),
            pltpu.SemaphoreType.DMA((shares[1][1] - shares[1][0],)),
        ],
        compiler_params=params(docs, 6),
        cost_estimate=cost(8),
        name="attend",
    )(table, cache_tiles, w_gu, *qkv_parts, *fetched)
    fetched.append(w_ready)

    fetched.append(fetch(w_gu, shares[2], 2 * width, head_out))
    head_parts = exchange([head_out] * tp, "tp", tp)
    out_part = pl.pallas_call(
        functools.partial(out_kernel, tp),
        out_shape=jax.ShapeDtypeStruct((docs, width), BF16),
        in_specs=[vmem()] * (tp + 2) + [hbm()],
        out_specs=vmem(),
        scratch_shapes=[pltpu.VMEM((max(docs, 8), heads * LANES), F32)],
        compiler_params=params(docs, 6),
        cost_estimate=cost(6),
        name="attn_project",
    )(places, w_out, *head_parts, fetched[-1])

    fetched.append(fetch(w_gu, shares[3], 2 * width, out_part))
    out_parts = exchange([out_part] * kv, "kv", kv)
    down_cut = width // LANES // 4 * 2
    w_down = in_hbm(w_down)
    attn_out, gu_part, *down_ready = pl.pallas_call(
        functools.partial(gate_up_kernel, kv, len(fetched), shares[4][0]),
        out_shape=[
            jax.ShapeDtypeStruct((docs, width), BF16),
            jax.ShapeDtypeStruct((2 * docs, hidden + LANES), BF16),
        ]
        + [tiles_of((0, down_cut), hidden)] * (down_cut > 0),
        in_specs=[vmem(), vmem(), hbm(), hbm()] + [vmem()] * (len(fetched) + kv),
        out_specs=[vmem()] * (2 + (down_cut > 0)),
        scratch_shapes=[
            tiles_of(shares[4], 2 * width),
            pltpu.VMEM((4 * docs, 2 * width), BF16),
            pltpu.SemaphoreType.DMA((shares[4][1] - shares[4][0],)),
            pltpu.SemaphoreType.DMA((max(down_cut, 1),)),
        ],
        compiler_params=params(docs, 20),
        cost_estimate=cost(10),
        name="gate_up",
    )(states, norm_gains, w_gu, w_down, *fetched, *out_parts)

    down_ready.append(fetch(w_down, (down_cut, width // LANES), hidden, gu_part))
    gu_parts = exchange([gu_part] * tp, "tp", tp)
    ffn_part = pl.pallas_call(
        functools.partial(down_kernel, tp, len(down_ready)),
        out_shape=jax.ShapeDtypeStruct((docs, width), BF16),
        in_specs=[vmem()] * (len(down_ready) + tp),
        out_specs=vmem(),
        scratch_shapes=[pltpu.VMEM((docs, hidden), BF16)],
        compiler_params=params(docs, 6),
        cost_estimate=cost(5),
        name="down",
    )(*down_ready, *gu_parts)
    ffn_parts = exchange([ffn_part] * kv, "kv", kv)
    ffn_out = tree_sum([part.astype(F32) for part in ffn_parts]).astype(BF16)
    return attn_out, ffn_out, new_kv.reshape(1, 1, 2 * LANES)


def solution(mesh):
    return jax.shard_map(
        functools.partial(per_device, mesh.shape["tp"], mesh.shape["kv"]),
        mesh=mesh,
        in_specs=(
            P("grp", "tp"),
            P(None, "tp"),
            P("tp", "kv", None),
            P("tp", "kv", None),
            P("kv", "tp"),
            P("tp", None, "kv"),
            P("kv", "tp"),
            P(("grp", "tp"), None, "kv", None),
            P("grp"),
            P("grp"),
        ),
        out_specs=(P("grp", "tp"), P("grp", "tp"), P(("grp", "tp"), "kv", None)),
        check_vma=False,
    )
```

```python
import functools
import math

import jax
import jax.numpy as jnp
import numpy as np
from jax import lax
from jax.experimental import pallas as pl
from jax.experimental.pallas import tpu as pltpu
from jax.sharding import PartitionSpec as P

D = 8192
EPS = 1e-05
ROPE_BASE = 500000.0
LANES = 128
MIB = 1 << 20
GU_SHARES = (4, 4, 4, 2, 14)
F32 = jnp.float32
BF16 = jnp.bfloat16
QUARTER = (1.5703125, 4.837512969970703125e-4, 7.549789948768648e-8)
SIN = (-1.9515295891e-4, 8.3321608736e-3, -1.6666654611e-1)
COS = (2.443315711809948e-5, -1.388731625493765e-3, 4.166664568298827e-2)


def vmem():
    return pl.BlockSpec(memory_space=pltpu.VMEM)


def hbm():
    return pl.BlockSpec(memory_space=pltpu.HBM)


def in_hbm(array):
    return pltpu.with_memory_space_constraint(array, pltpu.HBM)


def exchange(arrays, axis, size):
    return [arrays[0]] + [
        lax.ppermute(arrays[s], axis, [(i, i ^ s) for i in range(size)])
        for s in range(1, size)
    ]


def tree_sum(parts):
    while len(parts) > 1:
        parts = [a + b for a, b in zip(parts[::2], parts[1::2])]
    return parts[0]


def two_parts(scaled):
    high = scaled.astype(BF16).astype(F32)
    return high, scaled - high


def spread(rows16, out_ref, docs):
    width = rows16.shape[1]
    pick = one_hot_spread(2)
    row = lax.broadcasted_iota(jnp.int32, (4 * docs, 2 * LANES), 0)
    lane = lax.broadcasted_iota(jnp.int32, (4 * docs, 2 * LANES), 1)
    keep = (lax.shift_right_logical(row, docs.bit_length() - 1) & 1) == (lane & 1)
    chunks = width // LANES
    stacked = jnp.concatenate(
        [rows16[:, c * LANES : (c + 1) * LANES] for c in range(chunks)], axis=0
    )
    doubled = jnp.dot(stacked, pick, preferred_element_type=F32)
    for c in range(chunks):
        piece = doubled[c * 4 * docs : (c + 1) * 4 * docs]
        out_ref[:, 2 * c * LANES : 2 * (c + 1) * LANES] = jnp.where(keep, piece, 0.0).astype(BF16)


def tile_copies(matrix, first, buf, sems):
    return [
        pltpu.make_async_copy(
            matrix.at[:, pl.ds((first + i) * LANES, LANES)], buf.at[i], sems.at[i]
        )
        for i in range(buf.shape[0])
    ]


def matrix_of(w):
    return w if len(w.shape) == 2 else w.reshape(w.shape[0] * w.shape[1], w.shape[2])


def times_tiles(left, tiles, store, tile_ready=None):
    def step(j, carry):
        if tile_ready is not None:
            tile_ready(2 * j)
            tile_ready(2 * j + 1)
        pair = jnp.concatenate([tiles[2 * j], tiles[2 * j + 1]], axis=1)
        store(j, jnp.dot(left[...], pair, preferred_element_type=F32))
        return carry

    lax.fori_loop(0, tiles.shape[0] // 2, step, 0)


def pick_doc(value, doc, docs):
    axis = value.ndim - 2
    row = lax.broadcasted_iota(jnp.int32, value.shape, axis)
    return jnp.sum(jnp.where(row & (docs - 1) == doc, value, 0.0), axis=axis)


def sine_cosine(angle):
    turns = jnp.floor(angle * (2.0 / math.pi) + 0.5)
    rest = ((angle - turns * QUARTER[0]) - turns * QUARTER[1]) - turns * QUARTER[2]
    square = rest * rest
    sine = rest + rest * square * ((SIN[0] * square + SIN[1]) * square + SIN[2])
    cosine = 1.0 - 0.5 * square + square * square * (
        (COS[0] * square + COS[1]) * square + COS[2]
    )
    quadrant = turns - 4.0 * jnp.floor(turns * 0.25)
    odd = (quadrant == 1.0) | (quadrant == 3.0)
    sine, cosine = jnp.where(odd, cosine, sine), jnp.where(odd, sine, cosine)
    return (
        jnp.where(quadrant >= 2.0, -sine, sine),
        jnp.where((quadrant == 1.0) | (quadrant == 2.0), -cosine, cosine),
    )


def rope_rows(length, frequency):
    sine, cosine = sine_cosine(length * frequency)
    lane = lax.broadcasted_iota(jnp.int32, (1, LANES), 1)
    return cosine, jnp.where(lane < LANES // 2, -sine, sine)


def one_hot_spread(fold):
    source = lax.broadcasted_iota(jnp.int32, (LANES, fold * LANES), 0)
    target = lax.broadcasted_iota(jnp.int32, (LANES, fold * LANES), 1)
    return (lax.shift_right_logical(target, fold.bit_length() - 1) == source).astype(F32).astype(BF16)


def spread_heads(rows, out_ref, heads):
    count, width = rows.shape
    chunks = width // LANES
    stacked = jnp.concatenate([rows[:, c * LANES : (c + 1) * LANES] for c in range(chunks)], axis=0)
    wide = jnp.dot(stacked.astype(BF16), one_hot_spread(heads), preferred_element_type=F32)
    columns = heads * LANES
    lane = lax.broadcasted_iota(jnp.int32, (count, columns), 1) & (heads - 1)
    for c in range(chunks):
        piece = wide[c * count : (c + 1) * count]
        for h in range(0, heads, 2):
            pair = [jnp.where(lane == h + i, piece, 0.0) for i in range(2)]
            out_ref[h * count : (h + 2) * count, c * columns : (c + 1) * columns] = (
                jnp.concatenate(pair, axis=0).astype(BF16)
            )


def qkv_kernel(
    tp, owner_hbm, lengths_hbm, frequency_hbm, states_hbm, gains_hbm, wq, wkv, cache, *rest
):
    outs = rest[:tp]
    table, places, cache_tiles = rest[tp : tp + 3]
    owner, lengths, frequency, states, gains = rest[tp + 3 : tp + 8]
    wq_buf, wkv_buf, spread_buf, sems, small_sems, cache_sems = rest[tp + 8 :]
    docs, width = states.shape
    heads = wq.shape[0] // width
    parts = wq_buf.shape[0]
    rows = wq_buf.shape[1]
    small = [
        pltpu.make_async_copy(source, target, small_sems.at[i])
        for i, (source, target) in enumerate(
            [
                (states_hbm, states),
                (gains_hbm, gains),
                (owner_hbm, owner),
                (lengths_hbm, lengths),
                (frequency_hbm, frequency),
            ]
        )
    ]
    copies = [
        pltpu.make_async_copy(wq.at[pl.ds(c * rows, rows)], wq_buf.at[c], sems.at[c])
        for c in range(parts)
    ]
    kv_copy = pltpu.make_async_copy(wkv, wkv_buf, sems.at[parts])
    cache_copies = tile_copies(cache, 0, cache_tiles, cache_sems)
    for copy in small + [kv_copy] + copies:
        copy.start()
    for copy in small:
        copy.wait()
    me = lax.axis_index("tp")
    x = states[...].astype(F32)
    squares = jnp.broadcast_to(jnp.sum(x * x, axis=1, keepdims=True), (docs, LANES))
    both = jnp.concatenate(two_parts(x * gains[0:1, :]), axis=0)
    spread_heads(both, spread_buf, heads)
    length = lengths[owner[me]].astype(F32)
    cosine, sine = rope_rows(length, frequency[...])
    table[0:1, :] = cosine
    table[1:2, :] = sine
    table[2:3, :] = jnp.full((1, LANES), length, F32)
    table[3:, :] = jnp.zeros((table.shape[0] - 3, LANES), F32)
    for s in range(tp):
        places[s : s + 1, :] = jnp.full((1, LANES), owner[me ^ s], jnp.int32)
    kv_copy.wait()
    kv_total = jnp.dot(both.astype(BF16), wkv_buf[...], preferred_element_type=F32)
    total = jnp.zeros((heads * 2 * docs, LANES), F32)
    for c in range(parts):
        copies[c].wait()
        if c == parts // 2:
            for copy in cache_copies:
                copy.start()
        total = total + jnp.dot(
            spread_buf[:, c * rows : (c + 1) * rows], wq_buf[c], preferred_element_type=F32
        )
    total = total.reshape(heads, 2 * docs, LANES)
    for s in range(tp):
        doc = owner[me ^ s]
        out = outs[-s]
        out[:heads, :] = pick_doc(total, doc, docs)
        kv_row = pick_doc(kv_total, doc, docs)[None]
        out[heads : heads + 1, :] = kv_row[:, :LANES]
        out[heads + 1 : heads + 2, :] = kv_row[:, LANES:]
        out[heads + 2 : heads + 3, :] = pick_doc(squares, doc, docs)[None]
        out[heads + 3 :, :] = jnp.zeros((out.shape[0] - heads - 3, LANES), F32)
    for copy in cache_copies:
        copy.wait()


def attend_kernel(tp, heads, rows, first, table, cache, w, *rest):
    parts = rest[:tp]
    heads_out, new_kv_out, w_ready, scores, w_sems = rest[-5:]
    w_copies = tile_copies(matrix_of(w), first, w_ready, w_sems)
    for copy in w_copies:
        copy.start()
    blocks = cache.shape[1] // rows
    sums = tree_sum([part[...] for part in parts])
    sums = sums * lax.rsqrt(sums[heads + 2 : heads + 3, :] / D + EPS)
    rotated = sums * table[0:1, :] + pltpu.roll(sums, LANES // 2, 1) * table[1:2, :]
    query = rotated[:heads].astype(BF16)
    key = rotated[heads : heads + 1].astype(BF16)
    value = sums[heads + 1 : heads + 2].astype(BF16)
    new_kv_out[:, :LANES] = key
    new_kv_out[:, LANES:] = value
    key = key.astype(F32)
    value = value.astype(F32)
    scale = LANES ** (-0.5)
    own = jnp.sum(query.astype(F32) * key, axis=1, keepdims=True) * scale
    column = lax.broadcasted_iota(jnp.int32, (heads, LANES), 1).astype(F32)
    length = table[2:3, :]
    tops = jnp.full((heads, LANES), -jnp.inf, F32)
    for b in range(blocks):
        block = lax.dot_general(
            query,
            cache[0, b * rows : (b + 1) * rows, :],
            (((1,), (1,)), ((), ())),
            preferred_element_type=F32,
        )
        for start in range(0, rows, LANES):
            at = b * rows + start
            piece = block[:, start : start + LANES] * scale
            piece = jnp.where(column < length - at, piece, -jnp.inf)
            tops = jnp.maximum(tops, piece)
            scores[:, at : at + LANES] = piece
    top = jnp.maximum(jnp.max(tops, axis=1, keepdims=True), own)
    own = jnp.exp(own - top)
    sums_by_lane = jnp.zeros((heads, LANES), F32)
    acc = own.astype(BF16).astype(F32) * value
    for b in range(blocks):
        weights = jnp.exp(scores[:, b * rows : (b + 1) * rows] - top)
        for start in range(0, rows, LANES):
            sums_by_lane = sums_by_lane + weights[:, start : start + LANES]
        acc = acc + jnp.dot(
            weights.astype(BF16),
            cache[1, b * rows : (b + 1) * rows, :],
            preferred_element_type=F32,
        )
    total = own + jnp.sum(sums_by_lane, axis=1, keepdims=True)
    heads_out[...] = (acc / total).astype(BF16)
    for copy in w_copies:
        copy.wait()


def out_kernel(tp, places, w_out, *rest):
    parts = rest[:tp]
    out, left = rest[-2:]
    docs = out.shape[0]
    row = lax.broadcasted_iota(jnp.int32, (left.shape[0], LANES), 0)
    own = [parts[s][...].astype(F32) for s in range(tp)]
    for h in range(own[0].shape[0]):
        piece = jnp.zeros((left.shape[0], LANES), F32)
        for s in range(tp):
            piece = jnp.where(row == places[s : s + 1, :], own[s][h : h + 1, :], piece)
        left[:, h * LANES : (h + 1) * LANES] = piece
    terms = jnp.dot(left[...].astype(BF16), w_out[...], preferred_element_type=F32)
    out[...] = terms[:docs].astype(BF16)


def fetch_kernel(first, token, w, out, sems):
    copies = tile_copies(matrix_of(w), first, out, sems)
    for copy in copies:
        copy.start()
    for copy in copies:
        copy.wait()


def gate_up_kernel(kv, groups, first, states, gains, w, *rest):
    ready, parts = rest[:groups], rest[groups : groups + kv]
    attn_out, partial_out, w_tiles, spread_buf, w_sems = rest[groups + kv :]
    docs, width = states.shape
    hidden = w.shape[2]
    w_matrix = matrix_of(w)
    for copy in tile_copies(w_matrix, first, w_tiles, w_sems):
        copy.start()
    attn = tree_sum([part[...].astype(F32) for part in parts]).astype(BF16)
    attn_out[...] = attn
    resid = (states[...].astype(F32) + attn.astype(F32)).astype(BF16).astype(F32)
    squares = jnp.sum(resid * resid, axis=1, keepdims=True)
    high, low = two_parts(resid * gains[1:2, :])
    spread(jnp.concatenate([high, high, low, low], axis=0).astype(BF16), spread_buf, docs)

    def store_from(tile):
        def store(j, product):
            start = pl.multiple_of((tile + 2 * j) * LANES, 2 * LANES)
            summed = product[: 2 * docs] + product[2 * docs :]
            partial_out[:, pl.ds(start, 2 * LANES)] = summed.astype(BF16)

        return store

    def tile_ready(i):
        pltpu.make_async_copy(
            w_matrix.at[:, pl.ds(pl.multiple_of((first + i) * LANES, LANES), LANES)],
            w_tiles.at[i],
            w_sems.at[i],
        ).wait()

    tile = 0
    for group in ready:
        times_tiles(spread_buf, group, store_from(tile))
        tile += group.shape[0]
    times_tiles(spread_buf, w_tiles, store_from(tile), tile_ready)
    lane = lax.broadcasted_iota(jnp.int32, (docs, LANES), 1)
    first = squares.astype(BF16).astype(F32)
    second = (squares - first).astype(BF16).astype(F32)
    third = squares - first - second
    terms = jnp.where(lane == 0, first, jnp.where(lane == 1, second, jnp.where(lane == 2, third, 0.0)))
    partial_out[:, hidden:] = jnp.concatenate([terms, terms], axis=0).astype(BF16)


def down_kernel(tp, w_down, *rest):
    parts = rest[:tp]
    out, act_buf = rest[tp:]
    docs, width = out.shape
    hidden = w_down.shape[0]
    summed = tree_sum([part[...].astype(F32) for part in parts])
    squares = jnp.sum(summed[:docs, hidden:], axis=1, keepdims=True)
    inverse = lax.rsqrt(squares / D + EPS)
    gate = summed[:docs, :hidden] * inverse
    up = summed[docs:, :hidden] * inverse
    act_buf[...] = (gate / (1.0 + jnp.exp(-gate)) * up).astype(BF16)

    def step(j, carry):
        columns = pl.ds(pl.multiple_of(2 * j * LANES, 2 * LANES), 2 * LANES)
        product = jnp.dot(act_buf[...], w_down[:, columns], preferred_element_type=F32)
        out[:, columns] = product.astype(BF16)
        return carry

    lax.fori_loop(0, width // (2 * LANES), step, 0)


def cost(micros):
    return pl.CostEstimate(flops=0, bytes_accessed=int(micros * 3.69e6), transcendentals=0)


def params(docs, mib):
    return pltpu.CompilerParams(vmem_limit_bytes=(mib if docs <= 8 else mib + 24) * MIB)


def per_device(
    tp, kv,
    states, norm_gains, w_query, w_keyval, w_out, w_gate_up, w_down, kv_cache, lengths, owner_rows
):
    docs, width = states.shape
    heads = w_query.shape[1]
    cache_len = kv_cache.shape[1]
    hidden = w_gate_up.shape[2]
    wq = w_query.reshape(width * heads, LANES)
    wkv = w_keyval.reshape(width, 2 * LANES)
    cache = kv_cache.reshape(cache_len, 2 * LANES)
    packed = 2 * heads
    wq_parts = 4

    half = LANES // 2
    freq = ROPE_BASE ** (-(np.arange(half, dtype=np.float64) * 2.0 / LANES))
    freq = jnp.asarray(np.concatenate([freq, freq]).astype(np.float32)[None, :])
    *qkv_parts, table, places, cache_tiles = pl.pallas_call(
        functools.partial(qkv_kernel, tp),
        out_shape=[jax.ShapeDtypeStruct((packed, LANES), F32)] * tp
        + [
            jax.ShapeDtypeStruct((8, LANES), F32),
            jax.ShapeDtypeStruct((max(tp, 8), LANES), jnp.int32),
            pltpu.VMEM((2, cache_len, LANES), BF16),
        ],
        in_specs=[hbm()] * 8,
        out_specs=[vmem()] * (tp + 3),
        scratch_shapes=[
            pltpu.SMEM((docs,), jnp.int32),
            pltpu.SMEM((docs,), jnp.int32),
            pltpu.VMEM((1, LANES), F32),
            pltpu.VMEM((docs, width), BF16),
            pltpu.VMEM((2, width), F32),
            pltpu.VMEM((wq_parts, width * heads // wq_parts, LANES), BF16),
            pltpu.VMEM((width, 2 * LANES), BF16),
            pltpu.VMEM((heads * 2 * docs, width * heads), BF16),
            pltpu.SemaphoreType.DMA((wq_parts + 1,)),
            pltpu.SemaphoreType.DMA((5,)),
            pltpu.SemaphoreType.DMA((2,)),
        ],
        compiler_params=params(docs, 10),
        cost_estimate=cost(8),
        name="qkv",
    )(*(in_hbm(a) for a in (owner_rows, lengths, freq, states, norm_gains, wq, wkv, cache)))
    w_gu = in_hbm(w_gate_up)
    bounds = np.cumsum([0] + [hidden // LANES * n // 28 for n in GU_SHARES]).tolist()
    shares = list(zip(bounds, bounds[1:]))
    fetched = []

    def tiles_of(share, rows):
        return pltpu.VMEM((share[1] - share[0], rows, LANES), BF16)

    def fetch(weights, share, rows, token):
        return pl.pallas_call(
            functools.partial(fetch_kernel, share[0]),
            out_shape=tiles_of(share, rows),
            in_specs=[hbm(), hbm()],
            out_specs=vmem(),
            scratch_shapes=[pltpu.SemaphoreType.DMA((share[1] - share[0],))],
            compiler_params=params(docs, 2),
            cost_estimate=cost(0.3 * (share[1] - share[0])),
            name="fetch",
        )(token, weights)

    fetched.append(fetch(w_gu, shares[0], 2 * width, table))
    qkv_parts = exchange([qkv_parts[-s] for s in range(tp)], "tp", tp)
    head_out, new_kv, w_ready = pl.pallas_call(
        functools.partial(attend_kernel, tp, heads, 512, shares[1][0]),
        out_shape=[
            jax.ShapeDtypeStruct((heads, LANES), BF16),
            jax.ShapeDtypeStruct((1, 2 * LANES), BF16),
            tiles_of(shares[1], 2 * width),
        ],
        in_specs=[vmem(), vmem(), hbm()] + [vmem()] * tp + [hbm()] * len(fetched),
        out_specs=[vmem()] * 3,
        scratch_shapes=[
            pltpu.VMEM((heads, cache_len), F32),
            pltpu.SemaphoreType.DMA((shares[1][1] - shares[1][0],)),
        ],
        compiler_params=params(docs, 6),
        cost_estimate=cost(8),
        name="attend",
    )(table, cache_tiles, w_gu, *qkv_parts, *fetched)
    fetched.append(w_ready)

    fetched.append(fetch(w_gu, shares[2], 2 * width, head_out))
    head_parts = exchange([head_out] * tp, "tp", tp)
    out_part = pl.pallas_call(
        functools.partial(out_kernel, tp),
        out_shape=jax.ShapeDtypeStruct((docs, width), BF16),
        in_specs=[vmem()] * (tp + 2) + [hbm()],
        out_specs=vmem(),
        scratch_shapes=[pltpu.VMEM((max(docs, 8), heads * LANES), F32)],
        compiler_params=params(docs, 6),
        cost_estimate=cost(6),
        name="attn_project",
    )(places, w_out, *head_parts, fetched[-1])

    fetched.append(fetch(w_gu, shares[3], 2 * width, out_part))
    out_parts = exchange([out_part] * kv, "kv", kv)
    attn_out, gu_part = pl.pallas_call(
        functools.partial(gate_up_kernel, kv, len(fetched), shares[4][0]),
        out_shape=[
            jax.ShapeDtypeStruct((docs, width), BF16),
            jax.ShapeDtypeStruct((2 * docs, hidden + LANES), BF16),
        ],
        in_specs=[vmem(), vmem(), hbm()] + [vmem()] * (len(fetched) + kv),
        out_specs=[vmem()] * 2,
        scratch_shapes=[
            tiles_of(shares[4], 2 * width),
            pltpu.VMEM((4 * docs, 2 * width), BF16),
            pltpu.SemaphoreType.DMA((shares[4][1] - shares[4][0],)),
        ],
        compiler_params=params(docs, 20),
        cost_estimate=cost(10),
        name="gate_up",
    )(states, norm_gains, w_gu, *fetched, *out_parts)

    gu_parts = exchange([gu_part] * tp, "tp", tp)
    ffn_part = pl.pallas_call(
        functools.partial(down_kernel, tp),
        out_shape=jax.ShapeDtypeStruct((docs, width), BF16),
        in_specs=[vmem()] * (1 + tp),
        out_specs=vmem(),
        scratch_shapes=[pltpu.VMEM((docs, hidden), BF16)],
        compiler_params=params(docs, 6),
        cost_estimate=cost(5),
        name="down",
    )(w_down, *gu_parts)
    ffn_parts = exchange([ffn_part] * kv, "kv", kv)
    ffn_out = tree_sum([part.astype(F32) for part in ffn_parts]).astype(BF16)
    return attn_out, ffn_out, new_kv.reshape(1, 1, 2 * LANES)


def solution(mesh):
    return jax.shard_map(
        functools.partial(per_device, mesh.shape["tp"], mesh.shape["kv"]),
        mesh=mesh,
        in_specs=(
            P("grp", "tp"),
            P(None, "tp"),
            P("tp", "kv", None),
            P("tp", "kv", None),
            P("kv", "tp"),
            P("tp", None, "kv"),
            P("kv", "tp"),
            P(("grp", "tp"), None, "kv", None),
            P("grp"),
            P("grp"),
        ),
        out_specs=(P("grp", "tp"), P("grp", "tp"), P(("grp", "tp"), "kv", None)),
        check_vma=False,
    )
```

```python
import functools
import math

import jax
import jax.numpy as jnp
import numpy as np
from jax import lax
from jax.experimental import pallas as pl
from jax.experimental.pallas import tpu as pltpu
from jax.sharding import PartitionSpec as P

D = 8192
EPS = 1e-05
ROPE_BASE = 500000.0
LANES = 128
MIB = 1 << 20
TILE_GROUP = 4
GU_SHARES = (4, 6, 6, 2, 10)
F32 = jnp.float32
BF16 = jnp.bfloat16
QUARTER = (1.5703125, 4.837512969970703125e-4, 7.549789948768648e-8)
SIN = (-1.9515295891e-4, 8.3321608736e-3, -1.6666654611e-1)
COS = (2.443315711809948e-5, -1.388731625493765e-3, 4.166664568298827e-2)


def vmem():
    return pl.BlockSpec(memory_space=pltpu.VMEM)


def hbm():
    return pl.BlockSpec(memory_space=pltpu.HBM)


def in_hbm(array):
    return pltpu.with_memory_space_constraint(array, pltpu.HBM)


def exchange(arrays, axis, size):
    return [arrays[0]] + [
        lax.ppermute(arrays[s], axis, [(i, i ^ s) for i in range(size)])
        for s in range(1, size)
    ]


def tree_sum(parts):
    while len(parts) > 1:
        parts = [a + b for a, b in zip(parts[::2], parts[1::2])]
    return parts[0]


def two_parts(scaled):
    high = scaled.astype(BF16).astype(F32)
    return high, scaled - high


def spread(rows16, out_ref, docs):
    width = rows16.shape[1]
    pick = one_hot_spread(2)
    row = lax.broadcasted_iota(jnp.int32, (4 * docs, 2 * LANES), 0)
    lane = lax.broadcasted_iota(jnp.int32, (4 * docs, 2 * LANES), 1)
    keep = (lax.shift_right_logical(row, docs.bit_length() - 1) & 1) == (lane & 1)
    chunks = width // LANES
    stacked = jnp.concatenate(
        [rows16[:, c * LANES : (c + 1) * LANES] for c in range(chunks)], axis=0
    )
    doubled = jnp.dot(stacked, pick, preferred_element_type=F32)
    for c in range(chunks):
        piece = doubled[c * 4 * docs : (c + 1) * 4 * docs]
        out_ref[:, 2 * c * LANES : 2 * (c + 1) * LANES] = jnp.where(keep, piece, 0.0).astype(BF16)


def tile_copies(matrix, first, buf, sems):
    return [
        pltpu.make_async_copy(
            matrix.at[:, pl.ds((first + i) * LANES, LANES)], buf.at[i], sems.at[i]
        )
        for i in range(buf.shape[0])
    ]


def matrix_of(w):
    return w if len(w.shape) == 2 else w.reshape(w.shape[0] * w.shape[1], w.shape[2])


def times_tiles(left, tiles, first, store, tile_ready=None):
    count = tiles.shape[0]
    for start in range(0, count, TILE_GROUP):
        group = range(start, min(start + TILE_GROUP, count))
        if tile_ready is not None:
            for i in group:
                tile_ready(i)
        columns = jnp.concatenate([tiles[i] for i in group], axis=1)
        store(first + start, jnp.dot(left[...], columns, preferred_element_type=F32))


def pick_doc(value, doc, docs):
    axis = value.ndim - 2
    row = lax.broadcasted_iota(jnp.int32, value.shape, axis)
    return jnp.sum(jnp.where(row & (docs - 1) == doc, value, 0.0), axis=axis)


def sine_cosine(angle):
    turns = jnp.floor(angle * (2.0 / math.pi) + 0.5)
    rest = ((angle - turns * QUARTER[0]) - turns * QUARTER[1]) - turns * QUARTER[2]
    square = rest * rest
    sine = rest + rest * square * ((SIN[0] * square + SIN[1]) * square + SIN[2])
    cosine = 1.0 - 0.5 * square + square * square * (
        (COS[0] * square + COS[1]) * square + COS[2]
    )
    quadrant = turns - 4.0 * jnp.floor(turns * 0.25)
    odd = (quadrant == 1.0) | (quadrant == 3.0)
    sine, cosine = jnp.where(odd, cosine, sine), jnp.where(odd, sine, cosine)
    return (
        jnp.where(quadrant >= 2.0, -sine, sine),
        jnp.where((quadrant == 1.0) | (quadrant == 2.0), -cosine, cosine),
    )


def rope_rows(length, frequency):
    sine, cosine = sine_cosine(length * frequency)
    lane = lax.broadcasted_iota(jnp.int32, (1, LANES), 1)
    return cosine, jnp.where(lane < LANES // 2, -sine, sine)


def one_hot_spread(fold):
    source = lax.broadcasted_iota(jnp.int32, (LANES, fold * LANES), 0)
    target = lax.broadcasted_iota(jnp.int32, (LANES, fold * LANES), 1)
    return (lax.shift_right_logical(target, fold.bit_length() - 1) == source).astype(F32).astype(BF16)


def spread_heads(rows, out_ref, heads):
    count, width = rows.shape
    chunks = width // LANES
    stacked = jnp.concatenate([rows[:, c * LANES : (c + 1) * LANES] for c in range(chunks)], axis=0)
    wide = jnp.dot(stacked.astype(BF16), one_hot_spread(heads), preferred_element_type=F32)
    columns = heads * LANES
    lane = lax.broadcasted_iota(jnp.int32, (count, columns), 1) & (heads - 1)
    for c in range(chunks):
        piece = wide[c * count : (c + 1) * count]
        for h in range(0, heads, 2):
            pair = [jnp.where(lane == h + i, piece, 0.0) for i in range(2)]
            out_ref[h * count : (h + 2) * count, c * columns : (c + 1) * columns] = (
                jnp.concatenate(pair, axis=0).astype(BF16)
            )


def qkv_kernel(
    tp, owner_hbm, lengths_hbm, frequency_hbm, states_hbm, gains_hbm, wq, wkv, cache, *rest
):
    outs = rest[:tp]
    table, places, cache_tiles = rest[tp : tp + 3]
    owner, lengths, frequency, states, gains = rest[tp + 3 : tp + 8]
    wq_buf, wkv_buf, spread_buf, sems, small_sems, cache_sems = rest[tp + 8 :]
    docs, width = states.shape
    heads = wq.shape[0] // width
    parts = wq_buf.shape[0]
    rows = wq_buf.shape[1]
    small = [
        pltpu.make_async_copy(source, target, small_sems.at[i])
        for i, (source, target) in enumerate(
            [
                (states_hbm, states),
                (gains_hbm, gains),
                (owner_hbm, owner),
                (lengths_hbm, lengths),
                (frequency_hbm, frequency),
            ]
        )
    ]
    copies = [
        pltpu.make_async_copy(wq.at[pl.ds(c * rows, rows)], wq_buf.at[c], sems.at[c])
        for c in range(parts)
    ]
    kv_copy = pltpu.make_async_copy(wkv, wkv_buf, sems.at[parts])
    cache_copies = tile_copies(cache, 0, cache_tiles, cache_sems)
    for copy in small + [kv_copy] + copies:
        copy.start()
    for copy in small:
        copy.wait()
    for copy in cache_copies:
        copy.start()
    me = lax.axis_index("tp")
    x = states[...].astype(F32)
    squares = jnp.broadcast_to(jnp.sum(x * x, axis=1, keepdims=True), (docs, LANES))
    both = jnp.concatenate(two_parts(x * gains[0:1, :]), axis=0)
    spread_heads(both, spread_buf, heads)
    length = lengths[owner[me]].astype(F32)
    cosine, sine = rope_rows(length, frequency[...])
    table[0:1, :] = cosine
    table[1:2, :] = sine
    table[2:3, :] = jnp.full((1, LANES), length, F32)
    table[3:, :] = jnp.zeros((table.shape[0] - 3, LANES), F32)
    for s in range(tp):
        places[s : s + 1, :] = jnp.full((1, LANES), owner[me ^ s], jnp.int32)
    kv_copy.wait()
    kv_total = jnp.dot(both.astype(BF16), wkv_buf[...], preferred_element_type=F32)
    total = jnp.zeros((heads * 2 * docs, LANES), F32)
    for c in range(parts):
        copies[c].wait()
        total = total + jnp.dot(
            spread_buf[:, c * rows : (c + 1) * rows], wq_buf[c], preferred_element_type=F32
        )
    total = total.reshape(heads, 2 * docs, LANES)
    for s in range(tp):
        doc = owner[me ^ s]
        out = outs[-s]
        out[:heads, :] = pick_doc(total, doc, docs)
        kv_row = pick_doc(kv_total, doc, docs)[None]
        out[heads : heads + 1, :] = kv_row[:, :LANES]
        out[heads + 1 : heads + 2, :] = kv_row[:, LANES:]
        out[heads + 2 : heads + 3, :] = pick_doc(squares, doc, docs)[None]
        out[heads + 3 :, :] = jnp.zeros((out.shape[0] - heads - 3, LANES), F32)
    for copy in cache_copies:
        copy.wait()


def attend_kernel(tp, heads, rows, first, table, cache, w, *rest):
    parts = rest[:tp]
    heads_out, new_kv_out, w_ready, scores, w_sems = rest[-5:]
    w_copies = tile_copies(matrix_of(w), first, w_ready, w_sems)
    for copy in w_copies:
        copy.start()
    blocks = cache.shape[1] // rows
    sums = tree_sum([part[...] for part in parts])
    sums = sums * lax.rsqrt(sums[heads + 2 : heads + 3, :] / D + EPS)
    rotated = sums * table[0:1, :] + pltpu.roll(sums, LANES // 2, 1) * table[1:2, :]
    query = rotated[:heads].astype(BF16)
    key = rotated[heads : heads + 1].astype(BF16)
    value = sums[heads + 1 : heads + 2].astype(BF16)
    new_kv_out[:, :LANES] = key
    new_kv_out[:, LANES:] = value
    key = key.astype(F32)
    value = value.astype(F32)
    scale = LANES ** (-0.5)
    own = jnp.sum(query.astype(F32) * key, axis=1, keepdims=True) * scale
    column = lax.broadcasted_iota(jnp.int32, (heads, LANES), 1).astype(F32)
    length = table[2:3, :]
    tops = jnp.full((heads, LANES), -jnp.inf, F32)
    for b in range(blocks):
        block = lax.dot_general(
            query,
            cache[0, b * rows : (b + 1) * rows, :],
            (((1,), (1,)), ((), ())),
            preferred_element_type=F32,
        )
        for start in range(0, rows, LANES):
            at = b * rows + start
            piece = block[:, start : start + LANES] * scale
            piece = jnp.where(column < length - at, piece, -jnp.inf)
            tops = jnp.maximum(tops, piece)
            scores[:, at : at + LANES] = piece
    top = jnp.maximum(jnp.max(tops, axis=1, keepdims=True), own)
    own = jnp.exp(own - top)
    sums_by_lane = jnp.zeros((heads, LANES), F32)
    acc = own.astype(BF16).astype(F32) * value
    for b in range(blocks):
        weights = jnp.exp(scores[:, b * rows : (b + 1) * rows] - top)
        for start in range(0, rows, LANES):
            sums_by_lane = sums_by_lane + weights[:, start : start + LANES]
        acc = acc + jnp.dot(
            weights.astype(BF16),
            cache[1, b * rows : (b + 1) * rows, :],
            preferred_element_type=F32,
        )
    total = own + jnp.sum(sums_by_lane, axis=1, keepdims=True)
    heads_out[...] = (acc / total).astype(BF16)
    for copy in w_copies:
        copy.wait()


def out_kernel(tp, places, w_out, *rest):
    parts = rest[:tp]
    out, left = rest[-2:]
    docs = out.shape[0]
    row = lax.broadcasted_iota(jnp.int32, (left.shape[0], LANES), 0)
    own = [parts[s][...].astype(F32) for s in range(tp)]
    for h in range(own[0].shape[0]):
        piece = jnp.zeros((left.shape[0], LANES), F32)
        for s in range(tp):
            piece = jnp.where(row == places[s : s + 1, :], own[s][h : h + 1, :], piece)
        left[:, h * LANES : (h + 1) * LANES] = piece
    terms = jnp.dot(left[...].astype(BF16), w_out[...], preferred_element_type=F32)
    out[...] = terms[:docs].astype(BF16)


def fetch_kernel(first, token, w, out, sems):
    copies = tile_copies(matrix_of(w), first, out, sems)
    for copy in copies:
        copy.start()
    for copy in copies:
        copy.wait()


def gate_up_kernel(kv, groups, first, states, gains, w, *rest):
    ready, parts = rest[:groups], rest[groups : groups + kv]
    attn_out, partial_out, w_tiles, spread_buf, w_sems = rest[groups + kv :]
    docs, width = states.shape
    hidden = w.shape[2]
    w_matrix = matrix_of(w)
    copies = tile_copies(w_matrix, first, w_tiles, w_sems)
    for copy in copies:
        copy.start()
    attn = tree_sum([part[...].astype(F32) for part in parts]).astype(BF16)
    attn_out[...] = attn
    resid = (states[...].astype(F32) + attn.astype(F32)).astype(BF16).astype(F32)
    squares = jnp.sum(resid * resid, axis=1, keepdims=True)
    high, low = two_parts(resid * gains[1:2, :])
    spread(jnp.concatenate([high, high, low, low], axis=0).astype(BF16), spread_buf, docs)

    def store(tile, product):
        summed = product[: 2 * docs] + product[2 * docs :]
        columns = slice(tile * LANES, tile * LANES + summed.shape[1])
        partial_out[:, columns] = summed.astype(BF16)

    tile = 0
    for group in ready:
        times_tiles(spread_buf, group, tile, store)
        tile += group.shape[0]
    times_tiles(spread_buf, w_tiles, tile, store, lambda i: copies[i].wait())
    lane = lax.broadcasted_iota(jnp.int32, (docs, LANES), 1)
    first = squares.astype(BF16).astype(F32)
    second = (squares - first).astype(BF16).astype(F32)
    third = squares - first - second
    terms = jnp.where(lane == 0, first, jnp.where(lane == 1, second, jnp.where(lane == 2, third, 0.0)))
    partial_out[:, hidden:] = jnp.concatenate([terms, terms], axis=0).astype(BF16)


def down_kernel(tp, w_down, *rest):
    parts = rest[:tp]
    out, act_buf = rest[tp:]
    docs, width = out.shape
    hidden = w_down.shape[0]
    summed = tree_sum([part[...].astype(F32) for part in parts])
    squares = jnp.sum(summed[:docs, hidden:], axis=1, keepdims=True)
    inverse = lax.rsqrt(squares / D + EPS)
    gate = summed[:docs, :hidden] * inverse
    up = summed[docs:, :hidden] * inverse
    act_buf[...] = (gate / (1.0 + jnp.exp(-gate)) * up).astype(BF16)

    out[...] = jnp.dot(act_buf[...], w_down[...], preferred_element_type=F32).astype(BF16)


def cost(micros):
    return pl.CostEstimate(flops=0, bytes_accessed=int(micros * 3.69e6), transcendentals=0)


def params(docs, mib):
    return pltpu.CompilerParams(vmem_limit_bytes=(mib if docs <= 8 else mib + 24) * MIB)


def per_device(
    tp, kv,
    states, norm_gains, w_query, w_keyval, w_out, w_gate_up, w_down, kv_cache, lengths, owner_rows
):
    docs, width = states.shape
    heads = w_query.shape[1]
    cache_len = kv_cache.shape[1]
    hidden = w_gate_up.shape[2]
    wq = w_query.reshape(width * heads, LANES)
    wkv = w_keyval.reshape(width, 2 * LANES)
    cache = kv_cache.reshape(cache_len, 2 * LANES)
    packed = 2 * heads
    wq_parts = 4

    half = LANES // 2
    freq = ROPE_BASE ** (-(np.arange(half, dtype=np.float64) * 2.0 / LANES))
    freq = jnp.asarray(np.concatenate([freq, freq]).astype(np.float32)[None, :])
    *qkv_parts, table, places, cache_tiles = pl.pallas_call(
        functools.partial(qkv_kernel, tp),
        out_shape=[jax.ShapeDtypeStruct((packed, LANES), F32)] * tp
        + [
            jax.ShapeDtypeStruct((8, LANES), F32),
            jax.ShapeDtypeStruct((max(tp, 8), LANES), jnp.int32),
            pltpu.VMEM((2, cache_len, LANES), BF16),
        ],
        in_specs=[hbm()] * 8,
        out_specs=[vmem()] * (tp + 3),
        scratch_shapes=[
            pltpu.SMEM((docs,), jnp.int32),
            pltpu.SMEM((docs,), jnp.int32),
            pltpu.VMEM((1, LANES), F32),
            pltpu.VMEM((docs, width), BF16),
            pltpu.VMEM((2, width), F32),
            pltpu.VMEM((wq_parts, width * heads // wq_parts, LANES), BF16),
            pltpu.VMEM((width, 2 * LANES), BF16),
            pltpu.VMEM((heads * 2 * docs, width * heads), BF16),
            pltpu.SemaphoreType.DMA((wq_parts + 1,)),
            pltpu.SemaphoreType.DMA((5,)),
            pltpu.SemaphoreType.DMA((2,)),
        ],
        compiler_params=params(docs, 10),
        cost_estimate=cost(8),
        name="qkv",
    )(*(in_hbm(a) for a in (owner_rows, lengths, freq, states, norm_gains, wq, wkv, cache)))
    w_gu = in_hbm(w_gate_up)
    bounds = np.cumsum([0] + [hidden // LANES * n // 28 for n in GU_SHARES]).tolist()
    shares = list(zip(bounds, bounds[1:]))
    fetched = []

    def tiles_of(share, rows):
        return pltpu.VMEM((share[1] - share[0], rows, LANES), BF16)

    def fetch(weights, share, rows, token):
        return pl.pallas_call(
            functools.partial(fetch_kernel, share[0]),
            out_shape=tiles_of(share, rows),
            in_specs=[hbm(), hbm()],
            out_specs=vmem(),
            scratch_shapes=[pltpu.SemaphoreType.DMA((share[1] - share[0],))],
            compiler_params=params(docs, 2),
            cost_estimate=cost(0.3 * (share[1] - share[0])),
            name="fetch",
        )(token, weights)

    fetched.append(fetch(w_gu, shares[0], 2 * width, table))
    qkv_parts = exchange([qkv_parts[-s] for s in range(tp)], "tp", tp)
    head_out, new_kv, w_ready = pl.pallas_call(
        functools.partial(attend_kernel, tp, heads, 512, shares[1][0]),
        out_shape=[
            jax.ShapeDtypeStruct((heads, LANES), BF16),
            jax.ShapeDtypeStruct((1, 2 * LANES), BF16),
            tiles_of(shares[1], 2 * width),
        ],
        in_specs=[vmem(), vmem(), hbm()] + [vmem()] * tp + [hbm()] * len(fetched),
        out_specs=[vmem()] * 3,
        scratch_shapes=[
            pltpu.VMEM((heads, cache_len), F32),
            pltpu.SemaphoreType.DMA((shares[1][1] - shares[1][0],)),
        ],
        compiler_params=params(docs, 6),
        cost_estimate=cost(8),
        name="attend",
    )(table, cache_tiles, w_gu, *qkv_parts, *fetched)
    fetched.append(w_ready)

    fetched.append(fetch(w_gu, shares[2], 2 * width, head_out))
    head_parts = exchange([head_out] * tp, "tp", tp)
    out_part = pl.pallas_call(
        functools.partial(out_kernel, tp),
        out_shape=jax.ShapeDtypeStruct((docs, width), BF16),
        in_specs=[vmem()] * (tp + 2) + [hbm()],
        out_specs=vmem(),
        scratch_shapes=[pltpu.VMEM((max(docs, 8), heads * LANES), F32)],
        compiler_params=params(docs, 6),
        cost_estimate=cost(6),
        name="attn_project",
    )(places, w_out, *head_parts, fetched[-1])

    fetched.append(fetch(w_gu, shares[3], 2 * width, out_part))
    out_parts = exchange([out_part] * kv, "kv", kv)
    attn_out, gu_part = pl.pallas_call(
        functools.partial(gate_up_kernel, kv, len(fetched), shares[4][0]),
        out_shape=[
            jax.ShapeDtypeStruct((docs, width), BF16),
            jax.ShapeDtypeStruct((2 * docs, hidden + LANES), BF16),
        ],
        in_specs=[vmem(), vmem(), hbm()] + [vmem()] * (len(fetched) + kv),
        out_specs=[vmem()] * 2,
        scratch_shapes=[
            tiles_of(shares[4], 2 * width),
            pltpu.VMEM((4 * docs, 2 * width), BF16),
            pltpu.SemaphoreType.DMA((shares[4][1] - shares[4][0],)),
        ],
        compiler_params=params(docs, 20),
        cost_estimate=cost(10),
        name="gate_up",
    )(states, norm_gains, w_gu, *fetched, *out_parts)

    gu_parts = exchange([gu_part] * tp, "tp", tp)
    ffn_part = pl.pallas_call(
        functools.partial(down_kernel, tp),
        out_shape=jax.ShapeDtypeStruct((docs, width), BF16),
        in_specs=[vmem()] * (1 + tp),
        out_specs=vmem(),
        scratch_shapes=[pltpu.VMEM((docs, hidden), BF16)],
        compiler_params=params(docs, 6),
        cost_estimate=cost(5),
        name="down",
    )(w_down, *gu_parts)
    ffn_parts = exchange([ffn_part] * kv, "kv", kv)
    ffn_out = tree_sum([part.astype(F32) for part in ffn_parts]).astype(BF16)
    return attn_out, ffn_out, new_kv.reshape(1, 1, 2 * LANES)


def solution(mesh):
    return jax.shard_map(
        functools.partial(per_device, mesh.shape["tp"], mesh.shape["kv"]),
        mesh=mesh,
        in_specs=(
            P("grp", "tp"),
            P(None, "tp"),
            P("tp", "kv", None),
            P("tp", "kv", None),
            P("kv", "tp"),
            P("tp", None, "kv"),
            P("kv", "tp"),
            P(("grp", "tp"), None, "kv", None),
            P("grp"),
            P("grp"),
        ),
        out_specs=(P("grp", "tp"), P("grp", "tp"), P(("grp", "tp"), "kv", None)),
        check_vma=False,
    )
```

```python
import functools
import math

import jax
import jax.numpy as jnp
import numpy as np
from jax import lax
from jax.experimental import pallas as pl
from jax.experimental.pallas import tpu as pltpu
from jax.sharding import PartitionSpec as P

D = 8192
EPS = 1e-05
ROPE_BASE = 500000.0
LANES = 128
MIB = 1 << 20
COPY_ROWS = 512
KEY_ROWS = 512
GU_SHARES = (8, 6, 2, 2, 4, 4, 2)
F32 = jnp.float32
BF16 = jnp.bfloat16
QUARTER = (1.5703125, 4.837512969970703125e-4, 7.549789948768648e-8)
SIN = (-1.9515295891e-4, 8.3321608736e-3, -1.6666654611e-1)
COS = (2.443315711809948e-5, -1.388731625493765e-3, 4.166664568298827e-2)


def vmem():
    return pl.BlockSpec(memory_space=pltpu.VMEM)


def hbm():
    return pl.BlockSpec(memory_space=pltpu.HBM)


def in_hbm(array):
    return pltpu.with_memory_space_constraint(array, pltpu.HBM)


def exchange(arrays, axis, size):
    return [arrays[0]] + [
        lax.ppermute(arrays[s], axis, [(i, i ^ s) for i in range(size)])
        for s in range(1, size)
    ]


def tree_sum(parts):
    while len(parts) > 1:
        parts = [a + b for a, b in zip(parts[::2], parts[1::2])]
    return parts[0]


def two_parts(scaled):
    high = scaled.astype(BF16).astype(F32)
    return high, scaled - high


def spread(rows16, out_ref, docs):
    width = rows16.shape[1]
    pick = one_hot_spread(2)
    row = lax.broadcasted_iota(jnp.int32, (4 * docs, 2 * LANES), 0)
    lane = lax.broadcasted_iota(jnp.int32, (4 * docs, 2 * LANES), 1)
    keep = (lax.shift_right_logical(row, docs.bit_length() - 1) & 1) == (lane & 1)
    chunks = width // LANES
    stacked = jnp.concatenate(
        [rows16[:, c * LANES : (c + 1) * LANES] for c in range(chunks)], axis=0
    )
    doubled = jnp.dot(stacked, pick, preferred_element_type=F32)
    for c in range(chunks):
        piece = doubled[c * 4 * docs : (c + 1) * 4 * docs]
        out_ref[:, 2 * c * LANES : 2 * (c + 1) * LANES] = jnp.where(keep, piece, 0.0).astype(BF16)


def tile_copies(matrix, first, buf, sems):
    return [
        pltpu.make_async_copy(
            matrix.at[:, pl.ds((first + i) * LANES, LANES)], buf.at[i], sems.at[i]
        )
        for i in range(buf.shape[0])
    ]


def matrix_of(w):
    return w if len(w.shape) == 2 else w.reshape(w.shape[0] * w.shape[1], w.shape[2])


def block_copies(matrix, first, buf, sems):
    rows, columns = buf.shape
    chunk = min(rows, COPY_ROWS)
    return [
        pltpu.make_async_copy(
            matrix.at[pl.ds(start, chunk), pl.ds(first * LANES, columns)],
            buf.at[pl.ds(start, chunk)],
            sems.at[start // chunk],
        )
        for start in range(0, rows, chunk)
    ]


def pick_doc(value, doc, docs):
    axis = value.ndim - 2
    row = lax.broadcasted_iota(jnp.int32, value.shape, axis)
    return jnp.sum(jnp.where(row & (docs - 1) == doc, value, 0.0), axis=axis)


def sine_cosine(angle):
    turns = jnp.floor(angle * (2.0 / math.pi) + 0.5)
    rest = ((angle - turns * QUARTER[0]) - turns * QUARTER[1]) - turns * QUARTER[2]
    square = rest * rest
    sine = rest + rest * square * ((SIN[0] * square + SIN[1]) * square + SIN[2])
    cosine = 1.0 - 0.5 * square + square * square * (
        (COS[0] * square + COS[1]) * square + COS[2]
    )
    quadrant = turns - 4.0 * jnp.floor(turns * 0.25)
    odd = (quadrant == 1.0) | (quadrant == 3.0)
    sine, cosine = jnp.where(odd, cosine, sine), jnp.where(odd, sine, cosine)
    return (
        jnp.where(quadrant >= 2.0, -sine, sine),
        jnp.where((quadrant == 1.0) | (quadrant == 2.0), -cosine, cosine),
    )


def rope_rows(length, frequency):
    sine, cosine = sine_cosine(length * frequency)
    lane = lax.broadcasted_iota(jnp.int32, (1, LANES), 1)
    return cosine, jnp.where(lane < LANES // 2, -sine, sine)


def one_hot_spread(fold):
    source = lax.broadcasted_iota(jnp.int32, (LANES, fold * LANES), 0)
    target = lax.broadcasted_iota(jnp.int32, (LANES, fold * LANES), 1)
    return (lax.shift_right_logical(target, fold.bit_length() - 1) == source).astype(F32).astype(BF16)


def spread_heads(rows, out_ref, heads):
    count, width = rows.shape
    chunks = width // LANES
    stacked = jnp.concatenate([rows[:, c * LANES : (c + 1) * LANES] for c in range(chunks)], axis=0)
    wide = jnp.dot(stacked.astype(BF16), one_hot_spread(heads), preferred_element_type=F32)
    columns = heads * LANES
    lane = lax.broadcasted_iota(jnp.int32, (count, columns), 1) & (heads - 1)
    for c in range(chunks):
        piece = wide[c * count : (c + 1) * count]
        for h in range(0, heads, 2):
            pair = [jnp.where(lane == h + i, piece, 0.0) for i in range(2)]
            out_ref[h * count : (h + 2) * count, c * columns : (c + 1) * columns] = (
                jnp.concatenate(pair, axis=0).astype(BF16)
            )


def qkv_kernel(
    tp, owner_hbm, lengths_hbm, frequency_hbm, states_hbm, gains_hbm, wq, wkv, cache, *rest
):
    outs = rest[:tp]
    table, places, cache_tiles = rest[tp : tp + 3]
    owner, lengths, frequency, states, gains = rest[tp + 3 : tp + 8]
    wq_buf, wkv_buf, spread_buf, sems, small_sems, cache_sems = rest[tp + 8 :]
    docs, width = states.shape
    heads = wq.shape[0] // width
    parts = wq_buf.shape[0]
    rows = wq_buf.shape[1]
    small = [
        pltpu.make_async_copy(source, target, small_sems.at[i])
        for i, (source, target) in enumerate(
            [
                (states_hbm, states),
                (gains_hbm, gains),
                (owner_hbm, owner),
                (lengths_hbm, lengths),
                (frequency_hbm, frequency),
            ]
        )
    ]
    copies = [
        pltpu.make_async_copy(wq.at[pl.ds(c * rows, rows)], wq_buf.at[c], sems.at[c])
        for c in range(parts)
    ]
    kv_copy = pltpu.make_async_copy(wkv, wkv_buf, sems.at[parts])
    cache_copies = tile_copies(cache, 0, cache_tiles, cache_sems)
    for copy in small + [kv_copy] + copies:
        copy.start()
    for copy in small:
        copy.wait()
    for copy in cache_copies:
        copy.start()
    me = lax.axis_index("tp")
    x = states[...].astype(F32)
    squares = jnp.broadcast_to(jnp.sum(x * x, axis=1, keepdims=True), (docs, LANES))
    both = jnp.concatenate(two_parts(x * gains[0:1, :]), axis=0)
    spread_heads(both, spread_buf, heads)
    length = lengths[owner[me]].astype(F32)
    cosine, sine = rope_rows(length, frequency[...])
    table[0:1, :] = cosine
    table[1:2, :] = sine
    table[2:3, :] = jnp.full((1, LANES), length, F32)
    table[3:, :] = jnp.zeros((table.shape[0] - 3, LANES), F32)
    for s in range(tp):
        places[s : s + 1, :] = jnp.full((1, LANES), owner[me ^ s], jnp.int32)
    kv_copy.wait()
    kv_total = jnp.dot(both.astype(BF16), wkv_buf[...], preferred_element_type=F32)
    total = jnp.zeros((heads * 2 * docs, LANES), F32)
    for c in range(parts):
        copies[c].wait()
        total = total + jnp.dot(
            spread_buf[:, c * rows : (c + 1) * rows], wq_buf[c], preferred_element_type=F32
        )
    total = total.reshape(heads, 2 * docs, LANES)
    for s in range(tp):
        doc = owner[me ^ s]
        out = outs[-s]
        out[:heads, :] = pick_doc(total, doc, docs)
        kv_row = pick_doc(kv_total, doc, docs)[None]
        out[heads : heads + 1, :] = kv_row[:, :LANES]
        out[heads + 1 : heads + 2, :] = kv_row[:, LANES:]
        out[heads + 2 : heads + 3, :] = pick_doc(squares, doc, docs)[None]
        out[heads + 3 :, :] = jnp.zeros((out.shape[0] - heads - 3, LANES), F32)
    for copy in cache_copies:
        copy.wait()


def attend_kernel(tp, heads, rows, first, table, keys, cache, w, *rest):
    parts = rest[:tp]
    heads_out, new_kv_out, w_ready, scores, w_sems = rest[-5:]
    w_copies = block_copies(matrix_of(w), first, w_ready, w_sems)
    for copy in w_copies:
        copy.start()
    blocks = cache.shape[1] // rows
    sums = tree_sum([part[...] for part in parts])
    sums = sums * lax.rsqrt(sums[heads + 2 : heads + 3, :] / D + EPS)
    rotated = sums * table[0:1, :] + pltpu.roll(sums, LANES // 2, 1) * table[1:2, :]
    query = rotated[:heads].astype(BF16)
    key = rotated[heads : heads + 1].astype(BF16)
    value = sums[heads + 1 : heads + 2].astype(BF16)
    new_kv_out[:, :LANES] = key
    new_kv_out[:, LANES:] = value
    key = key.astype(F32)
    value = value.astype(F32)
    scale = LANES ** (-0.5)
    own = jnp.sum(query.astype(F32) * key, axis=1, keepdims=True) * scale
    column = lax.broadcasted_iota(jnp.int32, (heads, LANES), 1).astype(F32)
    length = table[2:3, :]
    tops = jnp.full((heads, LANES), -jnp.inf, F32)
    for b in range(blocks):
        block = jnp.dot(
            query, keys[:, b * rows : (b + 1) * rows], preferred_element_type=F32
        )
        for start in range(0, rows, LANES):
            at = b * rows + start
            piece = block[:, start : start + LANES] * scale
            piece = jnp.where(column < length - at, piece, -jnp.inf)
            tops = jnp.maximum(tops, piece)
            scores[:, at : at + LANES] = piece
    top = jnp.maximum(jnp.max(tops, axis=1, keepdims=True), own)
    own = jnp.exp(own - top)
    sums_by_lane = jnp.zeros((heads, LANES), F32)
    acc = own.astype(BF16).astype(F32) * value
    for b in range(blocks):
        weights = jnp.exp(scores[:, b * rows : (b + 1) * rows] - top)
        for start in range(0, rows, LANES):
            sums_by_lane = sums_by_lane + weights[:, start : start + LANES]
        acc = acc + jnp.dot(
            weights.astype(BF16),
            cache[1, b * rows : (b + 1) * rows, :],
            preferred_element_type=F32,
        )
    total = own + jnp.sum(sums_by_lane, axis=1, keepdims=True)
    heads_out[...] = (acc / total).astype(BF16)
    for copy in w_copies:
        copy.wait()


def out_kernel(tp, places, w_out, *rest):
    parts = rest[:tp]
    out, left = rest[-2:]
    docs = out.shape[0]
    row = lax.broadcasted_iota(jnp.int32, (left.shape[0], LANES), 0)
    own = [parts[s][...].astype(F32) for s in range(tp)]
    for h in range(own[0].shape[0]):
        piece = jnp.zeros((left.shape[0], LANES), F32)
        for s in range(tp):
            piece = jnp.where(row == places[s : s + 1, :], own[s][h : h + 1, :], piece)
        left[:, h * LANES : (h + 1) * LANES] = piece
    terms = jnp.dot(left[...].astype(BF16), w_out[...], preferred_element_type=F32)
    out[...] = terms[:docs].astype(BF16)


def fetch_kernel(first, token, w, out, sems):
    copies = block_copies(matrix_of(w), first, out, sems)
    for copy in copies:
        copy.start()
    for copy in copies:
        copy.wait()


def fetch_and_turn_kernel(first, token, w, cache, out, turned, sems):
    copies = block_copies(matrix_of(w), first, out, sems)
    for copy in copies:
        copy.start()
    for start in range(0, cache.shape[1], KEY_ROWS):
        turned[:, start : start + KEY_ROWS] = cache[0, start : start + KEY_ROWS, :].T
    for copy in copies:
        copy.wait()


def gate_up_kernel(kv, groups, first, states, gains, w, *rest):
    ready, parts = rest[:groups], rest[groups : groups + kv]
    attn_out, partial_out, *blocks, spread_buf, w_sems = rest[groups + kv :]
    docs, width = states.shape
    hidden = w.shape[2]
    w_matrix = matrix_of(w)
    copies = []
    for i, block in enumerate(blocks):
        copies.append(block_copies(w_matrix, first, block, w_sems.at[i]))
        first += block.shape[1] // LANES
        for copy in copies[-1]:
            copy.start()
    attn = tree_sum([part[...].astype(F32) for part in parts]).astype(BF16)
    attn_out[...] = attn
    resid = (states[...].astype(F32) + attn.astype(F32)).astype(BF16).astype(F32)
    squares = jnp.sum(resid * resid, axis=1, keepdims=True)
    high, low = two_parts(resid * gains[1:2, :])
    spread(jnp.concatenate([high, high, low, low], axis=0).astype(BF16), spread_buf, docs)

    at = 0
    for i, block in enumerate([*ready, *blocks]):
        if i >= groups:
            for copy in copies[i - groups]:
                copy.wait()
        product = jnp.dot(spread_buf[...], block[...], preferred_element_type=F32)
        columns = slice(at, at + block.shape[1])
        partial_out[:, columns] = (product[: 2 * docs] + product[2 * docs :]).astype(BF16)
        at += block.shape[1]
    lane = lax.broadcasted_iota(jnp.int32, (docs, LANES), 1)
    first = squares.astype(BF16).astype(F32)
    second = (squares - first).astype(BF16).astype(F32)
    third = squares - first - second
    terms = jnp.where(lane == 0, first, jnp.where(lane == 1, second, jnp.where(lane == 2, third, 0.0)))
    partial_out[:, hidden:] = jnp.concatenate([terms, terms], axis=0).astype(BF16)


def down_kernel(tp, w_down, *rest):
    parts = rest[:tp]
    out, act_buf = rest[tp:]
    docs, width = out.shape
    hidden = w_down.shape[0]
    summed = tree_sum([part[...].astype(F32) for part in parts])
    squares = jnp.sum(summed[:docs, hidden:], axis=1, keepdims=True)
    inverse = lax.rsqrt(squares / D + EPS)
    gate = summed[:docs, :hidden] * inverse
    up = summed[docs:, :hidden] * inverse
    act_buf[...] = (gate / (1.0 + jnp.exp(-gate)) * up).astype(BF16)

    out[...] = jnp.dot(act_buf[...], w_down[...], preferred_element_type=F32).astype(BF16)


def cost(micros):
    return pl.CostEstimate(flops=0, bytes_accessed=int(micros * 3.69e6), transcendentals=0)


def params(docs, mib):
    return pltpu.CompilerParams(vmem_limit_bytes=(mib if docs <= 8 else mib + 24) * MIB)


def per_device(
    tp, kv,
    states, norm_gains, w_query, w_keyval, w_out, w_gate_up, w_down, kv_cache, lengths, owner_rows
):
    docs, width = states.shape
    heads = w_query.shape[1]
    cache_len = kv_cache.shape[1]
    hidden = w_gate_up.shape[2]
    wq = w_query.reshape(width * heads, LANES)
    wkv = w_keyval.reshape(width, 2 * LANES)
    cache = kv_cache.reshape(cache_len, 2 * LANES)
    packed = 2 * heads
    wq_parts = 4

    half = LANES // 2
    freq = ROPE_BASE ** (-(np.arange(half, dtype=np.float64) * 2.0 / LANES))
    freq = jnp.asarray(np.concatenate([freq, freq]).astype(np.float32)[None, :])
    *qkv_parts, table, places, cache_tiles = pl.pallas_call(
        functools.partial(qkv_kernel, tp),
        out_shape=[jax.ShapeDtypeStruct((packed, LANES), F32)] * tp
        + [
            jax.ShapeDtypeStruct((8, LANES), F32),
            jax.ShapeDtypeStruct((max(tp, 8), LANES), jnp.int32),
            pltpu.VMEM((2, cache_len, LANES), BF16),
        ],
        in_specs=[hbm()] * 8,
        out_specs=[vmem()] * (tp + 3),
        scratch_shapes=[
            pltpu.SMEM((docs,), jnp.int32),
            pltpu.SMEM((docs,), jnp.int32),
            pltpu.VMEM((1, LANES), F32),
            pltpu.VMEM((docs, width), BF16),
            pltpu.VMEM((2, width), F32),
            pltpu.VMEM((wq_parts, width * heads // wq_parts, LANES), BF16),
            pltpu.VMEM((width, 2 * LANES), BF16),
            pltpu.VMEM((heads * 2 * docs, width * heads), BF16),
            pltpu.SemaphoreType.DMA((wq_parts + 1,)),
            pltpu.SemaphoreType.DMA((5,)),
            pltpu.SemaphoreType.DMA((2,)),
        ],
        compiler_params=params(docs, 10),
        cost_estimate=cost(8),
        name="qkv",
    )(*(in_hbm(a) for a in (owner_rows, lengths, freq, states, norm_gains, wq, wkv, cache)))
    w_gu = in_hbm(w_gate_up)
    bounds = np.cumsum([0] + [hidden // LANES * n // 28 for n in GU_SHARES]).tolist()
    shares = list(zip(bounds, bounds[1:]))
    fetched = []

    chunks = max(2 * width // COPY_ROWS, 1)

    def block_of(share):
        return pltpu.VMEM((2 * width, (share[1] - share[0]) * LANES), BF16)

    def fetch(share, token):
        return pl.pallas_call(
            functools.partial(fetch_kernel, share[0]),
            out_shape=block_of(share),
            in_specs=[hbm(), hbm()],
            out_specs=vmem(),
            scratch_shapes=[pltpu.SemaphoreType.DMA((chunks,))],
            compiler_params=params(docs, 2),
            cost_estimate=cost(0.3 * (share[1] - share[0])),
            name="fetch",
        )(token, w_gu)

    w_ready, turned = pl.pallas_call(
        functools.partial(fetch_and_turn_kernel, shares[0][0]),
        out_shape=[block_of(shares[0]), pltpu.VMEM((LANES, cache_len), BF16)],
        in_specs=[hbm(), hbm(), vmem()],
        out_specs=[vmem(), vmem()],
        scratch_shapes=[pltpu.SemaphoreType.DMA((chunks,))],
        compiler_params=params(docs, 4),
        cost_estimate=cost(3),
        name="fetch_and_turn_keys",
    )(table, w_gu, cache_tiles)
    fetched.append(w_ready)
    qkv_parts = exchange([qkv_parts[-s] for s in range(tp)], "tp", tp)
    head_out, new_kv, w_ready = pl.pallas_call(
        functools.partial(attend_kernel, tp, heads, 512, shares[1][0]),
        out_shape=[
            jax.ShapeDtypeStruct((heads, LANES), BF16),
            jax.ShapeDtypeStruct((1, 2 * LANES), BF16),
            block_of(shares[1]),
        ],
        in_specs=[vmem(), vmem(), vmem(), hbm()] + [vmem()] * tp + [hbm()] * len(fetched),
        out_specs=[vmem()] * 3,
        scratch_shapes=[
            pltpu.VMEM((heads, cache_len), F32),
            pltpu.SemaphoreType.DMA((chunks,)),
        ],
        compiler_params=params(docs, 6),
        cost_estimate=cost(8),
        name="attend",
    )(table, turned, cache_tiles, w_gu, *qkv_parts, *fetched)
    fetched.append(w_ready)

    fetched.append(fetch(shares[2], head_out))
    head_parts = exchange([head_out] * tp, "tp", tp)
    out_part = pl.pallas_call(
        functools.partial(out_kernel, tp),
        out_shape=jax.ShapeDtypeStruct((docs, width), BF16),
        in_specs=[vmem()] * (tp + 2) + [hbm()],
        out_specs=vmem(),
        scratch_shapes=[pltpu.VMEM((max(docs, 8), heads * LANES), F32)],
        compiler_params=params(docs, 6),
        cost_estimate=cost(6),
        name="attn_project",
    )(places, w_out, *head_parts, fetched[-1])

    fetched.append(fetch(shares[3], out_part))
    out_parts = exchange([out_part] * kv, "kv", kv)
    attn_out, gu_part = pl.pallas_call(
        functools.partial(gate_up_kernel, kv, len(fetched), shares[4][0]),
        out_shape=[
            jax.ShapeDtypeStruct((docs, width), BF16),
            jax.ShapeDtypeStruct((2 * docs, hidden + LANES), BF16),
        ],
        in_specs=[vmem(), vmem(), hbm()] + [vmem()] * (len(fetched) + kv),
        out_specs=[vmem()] * 2,
        scratch_shapes=[
            *(block_of(share) for share in shares[4:]),
            pltpu.VMEM((4 * docs, 2 * width), BF16),
            pltpu.SemaphoreType.DMA((len(shares) - 4, chunks)),
        ],
        compiler_params=params(docs, 20),
        cost_estimate=cost(10),
        name="gate_up",
    )(states, norm_gains, w_gu, *fetched, *out_parts)

    gu_parts = exchange([gu_part] * tp, "tp", tp)
    ffn_part = pl.pallas_call(
        functools.partial(down_kernel, tp),
        out_shape=jax.ShapeDtypeStruct((docs, width), BF16),
        in_specs=[vmem()] * (1 + tp),
        out_specs=vmem(),
        scratch_shapes=[pltpu.VMEM((docs, hidden), BF16)],
        compiler_params=params(docs, 6),
        cost_estimate=cost(5),
        name="down",
    )(w_down, *gu_parts)
    ffn_parts = exchange([ffn_part] * kv, "kv", kv)
    ffn_out = tree_sum([part.astype(F32) for part in ffn_parts]).astype(BF16)
    return attn_out, ffn_out, new_kv.reshape(1, 1, 2 * LANES)


def solution(mesh):
    return jax.shard_map(
        functools.partial(per_device, mesh.shape["tp"], mesh.shape["kv"]),
        mesh=mesh,
        in_specs=(
            P("grp", "tp"),
            P(None, "tp"),
            P("tp", "kv", None),
            P("tp", "kv", None),
            P("kv", "tp"),
            P("tp", None, "kv"),
            P("kv", "tp"),
            P(("grp", "tp"), None, "kv", None),
            P("grp"),
            P("grp"),
        ),
        out_specs=(P("grp", "tp"), P("grp", "tp"), P(("grp", "tp"), "kv", None)),
        check_vma=False,
    )
```

```python
import functools
import math

import jax
import jax.numpy as jnp
import numpy as np
from jax import lax
from jax.experimental import pallas as pl
from jax.experimental.pallas import tpu as pltpu
from jax.sharding import PartitionSpec as P

D = 8192
EPS = 1e-05
ROPE_BASE = 500000.0
LANES = 128
MIB = 1 << 20
COPY_ROWS = 512
KEY_ROWS = 512
GU_SHARES = (8, 6, 2, 2, 4, 4, 2)
F32 = jnp.float32
BF16 = jnp.bfloat16
QUARTER = (1.5703125, 4.837512969970703125e-4, 7.549789948768648e-8)
SIN = (-1.9515295891e-4, 8.3321608736e-3, -1.6666654611e-1)
COS = (2.443315711809948e-5, -1.388731625493765e-3, 4.166664568298827e-2)


def vmem():
    return pl.BlockSpec(memory_space=pltpu.VMEM)


def hbm():
    return pl.BlockSpec(memory_space=pltpu.HBM)


def in_hbm(array):
    return pltpu.with_memory_space_constraint(array, pltpu.HBM)


def exchange(arrays, axis, size):
    return [arrays[0]] + [
        lax.ppermute(arrays[s], axis, [(i, i ^ s) for i in range(size)])
        for s in range(1, size)
    ]


def tree_sum(parts):
    while len(parts) > 1:
        parts = [a + b for a, b in zip(parts[::2], parts[1::2])]
    return parts[0]


def two_parts(scaled):
    high = scaled.astype(BF16).astype(F32)
    return high, scaled - high


def spread(rows16, out_ref, docs):
    width = rows16.shape[1]
    pick = one_hot_spread(2)
    row = lax.broadcasted_iota(jnp.int32, (4 * docs, 2 * LANES), 0)
    lane = lax.broadcasted_iota(jnp.int32, (4 * docs, 2 * LANES), 1)
    keep = (lax.shift_right_logical(row, docs.bit_length() - 1) & 1) == (lane & 1)
    chunks = width // LANES
    stacked = jnp.concatenate(
        [rows16[:, c * LANES : (c + 1) * LANES] for c in range(chunks)], axis=0
    )
    doubled = jnp.dot(stacked, pick, preferred_element_type=F32)
    for c in range(chunks):
        piece = doubled[c * 4 * docs : (c + 1) * 4 * docs]
        out_ref[:, 2 * c * LANES : 2 * (c + 1) * LANES] = jnp.where(keep, piece, 0.0).astype(BF16)


def tile_copies(matrix, first, buf, sems):
    return [
        pltpu.make_async_copy(
            matrix.at[:, pl.ds((first + i) * LANES, LANES)], buf.at[i], sems.at[i]
        )
        for i in range(buf.shape[0])
    ]


def matrix_of(w):
    return w if len(w.shape) == 2 else w.reshape(w.shape[0] * w.shape[1], w.shape[2])


def block_copies(matrix, first, buf, sems):
    rows, columns = buf.shape
    chunk = min(rows, COPY_ROWS)
    return [
        pltpu.make_async_copy(
            matrix.at[pl.ds(start, chunk), pl.ds(first * LANES, columns)],
            buf.at[pl.ds(start, chunk)],
            sems.at[start // chunk],
        )
        for start in range(0, rows, chunk)
    ]


def pick_doc(value, doc, docs):
    axis = value.ndim - 2
    row = lax.broadcasted_iota(jnp.int32, value.shape, axis)
    return jnp.sum(jnp.where(row & (docs - 1) == doc, value, 0.0), axis=axis)


def sine_cosine(angle):
    turns = jnp.floor(angle * (2.0 / math.pi) + 0.5)
    rest = ((angle - turns * QUARTER[0]) - turns * QUARTER[1]) - turns * QUARTER[2]
    square = rest * rest
    sine = rest + rest * square * ((SIN[0] * square + SIN[1]) * square + SIN[2])
    cosine = 1.0 - 0.5 * square + square * square * (
        (COS[0] * square + COS[1]) * square + COS[2]
    )
    quadrant = turns - 4.0 * jnp.floor(turns * 0.25)
    odd = (quadrant == 1.0) | (quadrant == 3.0)
    sine, cosine = jnp.where(odd, cosine, sine), jnp.where(odd, sine, cosine)
    return (
        jnp.where(quadrant >= 2.0, -sine, sine),
        jnp.where((quadrant == 1.0) | (quadrant == 2.0), -cosine, cosine),
    )


def rope_rows(length, frequency):
    sine, cosine = sine_cosine(length * frequency)
    lane = lax.broadcasted_iota(jnp.int32, (1, LANES), 1)
    return cosine, jnp.where(lane < LANES // 2, -sine, sine)


def one_hot_spread(fold):
    source = lax.broadcasted_iota(jnp.int32, (LANES, fold * LANES), 0)
    target = lax.broadcasted_iota(jnp.int32, (LANES, fold * LANES), 1)
    return (lax.shift_right_logical(target, fold.bit_length() - 1) == source).astype(F32).astype(BF16)


def spread_heads(rows, out_ref, heads):
    count, width = rows.shape
    chunks = width // LANES
    stacked = jnp.concatenate([rows[:, c * LANES : (c + 1) * LANES] for c in range(chunks)], axis=0)
    wide = jnp.dot(stacked.astype(BF16), one_hot_spread(heads), preferred_element_type=F32)
    columns = heads * LANES
    lane = lax.broadcasted_iota(jnp.int32, (count, columns), 1) & (heads - 1)
    for c in range(chunks):
        piece = wide[c * count : (c + 1) * count]
        for h in range(0, heads, 2):
            pair = [jnp.where(lane == h + i, piece, 0.0) for i in range(2)]
            out_ref[h * count : (h + 2) * count, c * columns : (c + 1) * columns] = (
                jnp.concatenate(pair, axis=0).astype(BF16)
            )


def qkv_kernel(
    tp, owner_hbm, lengths_hbm, frequency_hbm, states_hbm, gains_hbm, wq, wkv, cache, *rest
):
    outs = rest[:tp]
    table, places, cache_tiles = rest[tp : tp + 3]
    owner, lengths, frequency, states, gains = rest[tp + 3 : tp + 8]
    wq_buf, wkv_buf, spread_buf, sems, small_sems, cache_sems = rest[tp + 8 :]
    docs, width = states.shape
    heads = wq.shape[0] // width
    parts = wq_buf.shape[0]
    rows = wq_buf.shape[1]
    small = [
        pltpu.make_async_copy(source, target, small_sems.at[i])
        for i, (source, target) in enumerate(
            [
                (states_hbm, states),
                (gains_hbm, gains),
                (owner_hbm, owner),
                (lengths_hbm, lengths),
                (frequency_hbm, frequency),
            ]
        )
    ]
    copies = [
        pltpu.make_async_copy(wq.at[pl.ds(c * rows, rows)], wq_buf.at[c], sems.at[c])
        for c in range(parts)
    ]
    kv_copy = pltpu.make_async_copy(wkv, wkv_buf, sems.at[parts])
    cache_copies = tile_copies(cache, 0, cache_tiles, cache_sems)
    for copy in small + [kv_copy] + copies:
        copy.start()
    for copy in small:
        copy.wait()
    for copy in cache_copies:
        copy.start()
    me = lax.axis_index("tp")
    x = states[...].astype(F32)
    squares = jnp.broadcast_to(jnp.sum(x * x, axis=1, keepdims=True), (docs, LANES))
    both = jnp.concatenate(two_parts(x * gains[0:1, :]), axis=0)
    spread_heads(both, spread_buf, heads)
    length = lengths[owner[me]].astype(F32)
    cosine, sine = rope_rows(length, frequency[...])
    table[0:1, :] = cosine
    table[1:2, :] = sine
    table[2:3, :] = jnp.full((1, LANES), length, F32)
    table[3:, :] = jnp.zeros((table.shape[0] - 3, LANES), F32)
    for s in range(tp):
        places[s : s + 1, :] = jnp.full((1, LANES), owner[me ^ s], jnp.int32)
    kv_copy.wait()
    kv_total = jnp.dot(both.astype(BF16), wkv_buf[...], preferred_element_type=F32)
    total = jnp.zeros((heads * 2 * docs, LANES), F32)
    for c in range(parts):
        copies[c].wait()
        total = total + jnp.dot(
            spread_buf[:, c * rows : (c + 1) * rows], wq_buf[c], preferred_element_type=F32
        )
    total = total.reshape(heads, 2 * docs, LANES)
    for s in range(tp):
        doc = owner[me ^ s]
        out = outs[-s]
        out[:heads, :] = pick_doc(total, doc, docs)
        kv_row = pick_doc(kv_total, doc, docs)[None]
        out[heads : heads + 1, :] = kv_row[:, :LANES]
        out[heads + 1 : heads + 2, :] = kv_row[:, LANES:]
        out[heads + 2 : heads + 3, :] = pick_doc(squares, doc, docs)[None]
        out[heads + 3 :, :] = jnp.zeros((out.shape[0] - heads - 3, LANES), F32)
    for copy in cache_copies:
        copy.wait()


def attend_kernel(tp, heads, rows, first, table, keys, cache, w, *rest):
    parts = rest[:tp]
    heads_out, new_kv_out, w_ready, scores, w_sems = rest[-5:]
    w_copies = block_copies(matrix_of(w), first, w_ready, w_sems)
    for copy in w_copies:
        copy.start()
    blocks = cache.shape[1] // rows
    sums = tree_sum([part[...] for part in parts])
    sums = sums * lax.rsqrt(sums[heads + 2 : heads + 3, :] / D + EPS)
    rotated = sums * table[0:1, :] + pltpu.roll(sums, LANES // 2, 1) * table[1:2, :]
    query = rotated[:heads].astype(BF16)
    key = rotated[heads : heads + 1].astype(BF16)
    value = sums[heads + 1 : heads + 2].astype(BF16)
    new_kv_out[:, :LANES] = key
    new_kv_out[:, LANES:] = value
    key = key.astype(F32)
    value = value.astype(F32)
    scale = LANES ** (-0.5)
    own = jnp.sum(query.astype(F32) * key, axis=1, keepdims=True) * scale
    column = lax.broadcasted_iota(jnp.int32, (heads, LANES), 1).astype(F32)
    length = table[2:3, :]
    tops = jnp.full((heads, LANES), -jnp.inf, F32)
    for b in range(blocks):
        block = jnp.dot(
            query, keys[:, b * rows : (b + 1) * rows], preferred_element_type=F32
        )
        for start in range(0, rows, LANES):
            at = b * rows + start
            piece = block[:, start : start + LANES] * scale
            piece = jnp.where(column < length - at, piece, -jnp.inf)
            tops = jnp.maximum(tops, piece)
            scores[:, at : at + LANES] = piece
    top = jnp.maximum(jnp.max(tops, axis=1, keepdims=True), own)
    own = jnp.exp(own - top)
    sums_by_lane = jnp.zeros((heads, LANES), F32)
    acc = own.astype(BF16).astype(F32) * value
    for b in range(blocks):
        weights = jnp.exp(scores[:, b * rows : (b + 1) * rows] - top)
        for start in range(0, rows, LANES):
            sums_by_lane = sums_by_lane + weights[:, start : start + LANES]
        acc = acc + jnp.dot(
            weights.astype(BF16),
            cache[1, b * rows : (b + 1) * rows, :],
            preferred_element_type=F32,
        )
    total = own + jnp.sum(sums_by_lane, axis=1, keepdims=True)
    heads_out[...] = (acc / total).astype(BF16)
    for copy in w_copies:
        copy.wait()


def out_kernel(tp, places, w_out, *rest):
    parts = rest[:tp]
    out, left = rest[-2:]
    docs = out.shape[0]
    row = lax.broadcasted_iota(jnp.int32, (left.shape[0], LANES), 0)
    own = [parts[s][...].astype(F32) for s in range(tp)]
    for h in range(own[0].shape[0]):
        piece = jnp.zeros((left.shape[0], LANES), F32)
        for s in range(tp):
            piece = jnp.where(row == places[s : s + 1, :], own[s][h : h + 1, :], piece)
        left[:, h * LANES : (h + 1) * LANES] = piece
    terms = jnp.dot(left[...].astype(BF16), w_out[...], preferred_element_type=F32)
    out[...] = terms[:docs].astype(BF16)


def fetch_kernel(first, token, w, *rest):
    out, sems = rest[-2:]
    copies = block_copies(matrix_of(w), first, out, sems)
    for copy in copies:
        copy.start()
    for copy in copies:
        copy.wait()


def fetch_and_turn_kernel(first, token, w, cache, out, turned, sems):
    copies = block_copies(matrix_of(w), first, out, sems)
    for copy in copies:
        copy.start()
    for start in range(0, cache.shape[1], KEY_ROWS):
        turned[:, start : start + KEY_ROWS] = cache[0, start : start + KEY_ROWS, :].T
    for copy in copies:
        copy.wait()


def gate_up_kernel(kv, groups, first, states, gains, w, *rest):
    ready, parts = rest[:groups], rest[groups : groups + kv]
    attn_out, partial_out, *blocks, spread_buf, w_sems = rest[groups + kv :]
    docs, width = states.shape
    hidden = w.shape[2]
    w_matrix = matrix_of(w)
    copies = []
    for i, block in enumerate(blocks):
        copies.append(block_copies(w_matrix, first, block, w_sems.at[i]))
        first += block.shape[1] // LANES
        for copy in copies[-1]:
            copy.start()
    attn = tree_sum([part[...].astype(F32) for part in parts]).astype(BF16)
    attn_out[...] = attn
    resid = (states[...].astype(F32) + attn.astype(F32)).astype(BF16).astype(F32)
    squares = jnp.sum(resid * resid, axis=1, keepdims=True)
    high, low = two_parts(resid * gains[1:2, :])
    spread(jnp.concatenate([high, high, low, low], axis=0).astype(BF16), spread_buf, docs)

    at = 0
    for i, block in enumerate([*ready, *blocks]):
        if i >= groups:
            for copy in copies[i - groups]:
                copy.wait()
        product = jnp.dot(spread_buf[...], block[...], preferred_element_type=F32)
        columns = slice(at, at + block.shape[1])
        partial_out[:, columns] = (product[: 2 * docs] + product[2 * docs :]).astype(BF16)
        at += block.shape[1]
    lane = lax.broadcasted_iota(jnp.int32, (docs, LANES), 1)
    first = squares.astype(BF16).astype(F32)
    second = (squares - first).astype(BF16).astype(F32)
    third = squares - first - second
    terms = jnp.where(lane == 0, first, jnp.where(lane == 1, second, jnp.where(lane == 2, third, 0.0)))
    partial_out[:, hidden:] = jnp.concatenate([terms, terms], axis=0).astype(BF16)


def down_kernel(tp, w_down, *rest):
    parts = rest[:tp]
    out, act_buf = rest[tp:]
    docs, width = out.shape
    hidden = w_down.shape[0]
    summed = tree_sum([part[...].astype(F32) for part in parts])
    squares = jnp.sum(summed[:docs, hidden:], axis=1, keepdims=True)
    inverse = lax.rsqrt(squares / D + EPS)
    gate = summed[:docs, :hidden] * inverse
    up = summed[docs:, :hidden] * inverse
    act_buf[...] = (gate / (1.0 + jnp.exp(-gate)) * up).astype(BF16)

    out[...] = jnp.dot(act_buf[...], w_down[...], preferred_element_type=F32).astype(BF16)


def cost(micros):
    return pl.CostEstimate(flops=0, bytes_accessed=int(micros * 3.69e6), transcendentals=0)


def params(docs, mib):
    return pltpu.CompilerParams(vmem_limit_bytes=(mib if docs <= 8 else mib + 24) * MIB)


def per_device(
    tp, kv,
    states, norm_gains, w_query, w_keyval, w_out, w_gate_up, w_down, kv_cache, lengths, owner_rows
):
    docs, width = states.shape
    heads = w_query.shape[1]
    cache_len = kv_cache.shape[1]
    hidden = w_gate_up.shape[2]
    wq = w_query.reshape(width * heads, LANES)
    wkv = w_keyval.reshape(width, 2 * LANES)
    cache = kv_cache.reshape(cache_len, 2 * LANES)
    packed = 2 * heads
    wq_parts = 4

    half = LANES // 2
    freq = ROPE_BASE ** (-(np.arange(half, dtype=np.float64) * 2.0 / LANES))
    freq = jnp.asarray(np.concatenate([freq, freq]).astype(np.float32)[None, :])
    *qkv_parts, table, places, cache_tiles = pl.pallas_call(
        functools.partial(qkv_kernel, tp),
        out_shape=[jax.ShapeDtypeStruct((packed, LANES), F32)] * tp
        + [
            jax.ShapeDtypeStruct((8, LANES), F32),
            jax.ShapeDtypeStruct((max(tp, 8), LANES), jnp.int32),
            pltpu.VMEM((2, cache_len, LANES), BF16),
        ],
        in_specs=[hbm()] * 8,
        out_specs=[vmem()] * (tp + 3),
        scratch_shapes=[
            pltpu.SMEM((docs,), jnp.int32),
            pltpu.SMEM((docs,), jnp.int32),
            pltpu.VMEM((1, LANES), F32),
            pltpu.VMEM((docs, width), BF16),
            pltpu.VMEM((2, width), F32),
            pltpu.VMEM((wq_parts, width * heads // wq_parts, LANES), BF16),
            pltpu.VMEM((width, 2 * LANES), BF16),
            pltpu.VMEM((heads * 2 * docs, width * heads), BF16),
            pltpu.SemaphoreType.DMA((wq_parts + 1,)),
            pltpu.SemaphoreType.DMA((5,)),
            pltpu.SemaphoreType.DMA((2,)),
        ],
        compiler_params=params(docs, 10),
        cost_estimate=cost(8),
        name="qkv",
    )(*(in_hbm(a) for a in (owner_rows, lengths, freq, states, norm_gains, wq, wkv, cache)))
    w_gu = in_hbm(w_gate_up)
    bounds = np.cumsum([0] + [hidden // LANES * n // 28 for n in GU_SHARES]).tolist()
    shares = list(zip(bounds, bounds[1:]))
    fetched = []

    chunks = max(2 * width // COPY_ROWS, 1)

    def block_of(share):
        return pltpu.VMEM((2 * width, (share[1] - share[0]) * LANES), BF16)

    def fetch(share, token, *keep):
        return pl.pallas_call(
            functools.partial(fetch_kernel, share[0]),
            out_shape=block_of(share),
            in_specs=[hbm(), hbm()] + [vmem()] * len(keep),
            out_specs=vmem(),
            scratch_shapes=[pltpu.SemaphoreType.DMA((chunks,))],
            compiler_params=params(docs, 2),
            cost_estimate=cost(0.3 * (share[1] - share[0])),
            name="fetch",
        )(token, w_gu, *keep)

    w_ready, turned = pl.pallas_call(
        functools.partial(fetch_and_turn_kernel, shares[0][0]),
        out_shape=[block_of(shares[0]), pltpu.VMEM((LANES, cache_len), BF16)],
        in_specs=[hbm(), hbm(), vmem()],
        out_specs=[vmem(), vmem()],
        scratch_shapes=[pltpu.SemaphoreType.DMA((chunks,))],
        compiler_params=params(docs, 4),
        cost_estimate=cost(3),
        name="fetch_and_turn_keys",
    )(table, w_gu, cache_tiles)
    fetched.append(w_ready)
    qkv_parts = exchange([qkv_parts[-s] for s in range(tp)], "tp", tp)
    head_out, new_kv, w_ready = pl.pallas_call(
        functools.partial(attend_kernel, tp, heads, 512, shares[1][0]),
        out_shape=[
            jax.ShapeDtypeStruct((heads, LANES), BF16),
            jax.ShapeDtypeStruct((1, 2 * LANES), BF16),
            block_of(shares[1]),
        ],
        in_specs=[vmem(), vmem(), vmem(), hbm()] + [vmem()] * tp + [hbm()] * len(fetched) + [vmem()],
        out_specs=[vmem()] * 3,
        scratch_shapes=[
            pltpu.VMEM((heads, cache_len), F32),
            pltpu.SemaphoreType.DMA((chunks,)),
        ],
        compiler_params=params(docs, 6),
        cost_estimate=cost(8),
        name="attend",
    )(table, turned, cache_tiles, w_gu, *qkv_parts, *fetched, w_out)
    fetched.append(w_ready)

    fetched.append(fetch(shares[2], head_out))
    head_parts = exchange([head_out] * tp, "tp", tp)
    out_part = pl.pallas_call(
        functools.partial(out_kernel, tp),
        out_shape=jax.ShapeDtypeStruct((docs, width), BF16),
        in_specs=[vmem()] * (tp + 2) + [hbm()],
        out_specs=vmem(),
        scratch_shapes=[pltpu.VMEM((max(docs, 8), heads * LANES), F32)],
        compiler_params=params(docs, 6),
        cost_estimate=cost(6),
        name="attn_project",
    )(places, w_out, *head_parts, fetched[-1])

    fetched.append(fetch(shares[3], out_part, w_down))
    out_parts = exchange([out_part] * kv, "kv", kv)
    attn_out, gu_part = pl.pallas_call(
        functools.partial(gate_up_kernel, kv, len(fetched), shares[4][0]),
        out_shape=[
            jax.ShapeDtypeStruct((docs, width), BF16),
            jax.ShapeDtypeStruct((2 * docs, hidden + LANES), BF16),
        ],
        in_specs=[vmem(), vmem(), hbm()] + [vmem()] * (len(fetched) + kv),
        out_specs=[vmem()] * 2,
        scratch_shapes=[
            *(block_of(share) for share in shares[4:]),
            pltpu.VMEM((4 * docs, 2 * width), BF16),
            pltpu.SemaphoreType.DMA((len(shares) - 4, chunks)),
        ],
        compiler_params=params(docs, 20),
        cost_estimate=cost(10),
        name="gate_up",
    )(states, norm_gains, w_gu, *fetched, *out_parts)

    gu_parts = exchange([gu_part] * tp, "tp", tp)
    ffn_part = pl.pallas_call(
        functools.partial(down_kernel, tp),
        out_shape=jax.ShapeDtypeStruct((docs, width), BF16),
        in_specs=[vmem()] * (1 + tp),
        out_specs=vmem(),
        scratch_shapes=[pltpu.VMEM((docs, hidden), BF16)],
        compiler_params=params(docs, 6),
        cost_estimate=cost(5),
        name="down",
    )(w_down, *gu_parts)
    ffn_parts = exchange([ffn_part] * kv, "kv", kv)
    ffn_out = tree_sum([part.astype(F32) for part in ffn_parts]).astype(BF16)
    return attn_out, ffn_out, new_kv.reshape(1, 1, 2 * LANES)


def solution(mesh):
    return jax.shard_map(
        functools.partial(per_device, mesh.shape["tp"], mesh.shape["kv"]),
        mesh=mesh,
        in_specs=(
            P("grp", "tp"),
            P(None, "tp"),
            P("tp", "kv", None),
            P("tp", "kv", None),
            P("kv", "tp"),
            P("tp", None, "kv"),
            P("kv", "tp"),
            P(("grp", "tp"), None, "kv", None),
            P("grp"),
            P("grp"),
        ),
        out_specs=(P("grp", "tp"), P("grp", "tp"), P(("grp", "tp"), "kv", None)),
        check_vma=False,
    )
```

```python
import functools
import math

import jax
import jax.numpy as jnp
import numpy as np
from jax import lax
from jax.experimental import pallas as pl
from jax.experimental.pallas import tpu as pltpu
from jax.sharding import PartitionSpec as P

D = 8192
EPS = 1e-05
ROPE_BASE = 500000.0
LANES = 128
MIB = 1 << 20
COPY_ROWS = 2048
KEY_ROWS = 512
GU_SHARES = (4, 6, 2, 2, 4, 4, 4, 2)
F32 = jnp.float32
BF16 = jnp.bfloat16
QUARTER = (1.5703125, 4.837512969970703125e-4, 7.549789948768648e-8)
SIN = (-1.9515295891e-4, 8.3321608736e-3, -1.6666654611e-1)
COS = (2.443315711809948e-5, -1.388731625493765e-3, 4.166664568298827e-2)


def vmem():
    return pl.BlockSpec(memory_space=pltpu.VMEM)


def hbm():
    return pl.BlockSpec(memory_space=pltpu.HBM)


def in_hbm(array):
    return pltpu.with_memory_space_constraint(array, pltpu.HBM)


def exchange(arrays, axis, size):
    return [arrays[0]] + [
        lax.ppermute(arrays[s], axis, [(i, i ^ s) for i in range(size)])
        for s in range(1, size)
    ]


def tree_sum(parts):
    while len(parts) > 1:
        parts = [a + b for a, b in zip(parts[::2], parts[1::2])]
    return parts[0]


def two_parts(scaled):
    high = scaled.astype(BF16).astype(F32)
    return high, scaled - high


def spread(rows16, out_ref, docs):
    width = rows16.shape[1]
    pick = one_hot_spread(2)
    row = lax.broadcasted_iota(jnp.int32, (4 * docs, 2 * LANES), 0)
    lane = lax.broadcasted_iota(jnp.int32, (4 * docs, 2 * LANES), 1)
    keep = (lax.shift_right_logical(row, docs.bit_length() - 1) & 1) == (lane & 1)
    chunks = width // LANES
    stacked = jnp.concatenate(
        [rows16[:, c * LANES : (c + 1) * LANES] for c in range(chunks)], axis=0
    )
    doubled = jnp.dot(stacked, pick, preferred_element_type=F32)
    for c in range(chunks):
        piece = doubled[c * 4 * docs : (c + 1) * 4 * docs]
        out_ref[:, 2 * c * LANES : 2 * (c + 1) * LANES] = jnp.where(keep, piece, 0.0).astype(BF16)


def tile_copies(matrix, first, buf, sems):
    return [
        pltpu.make_async_copy(
            matrix.at[:, pl.ds((first + i) * LANES, LANES)], buf.at[i], sems.at[i]
        )
        for i in range(buf.shape[0])
    ]


def matrix_of(w):
    return w if len(w.shape) == 2 else w.reshape(w.shape[0] * w.shape[1], w.shape[2])


def block_copies(matrix, first, buf, sems):
    rows, columns = buf.shape
    chunk = min(rows, COPY_ROWS)
    return [
        pltpu.make_async_copy(
            matrix.at[pl.ds(start, chunk), pl.ds(first * LANES, columns)],
            buf.at[pl.ds(start, chunk)],
            sems.at[start // chunk],
        )
        for start in range(0, rows, chunk)
    ]


def pick_doc(value, doc, docs):
    axis = value.ndim - 2
    row = lax.broadcasted_iota(jnp.int32, value.shape, axis)
    return jnp.sum(jnp.where(row & (docs - 1) == doc, value, 0.0), axis=axis)


def sine_cosine(angle):
    turns = jnp.floor(angle * (2.0 / math.pi) + 0.5)
    rest = ((angle - turns * QUARTER[0]) - turns * QUARTER[1]) - turns * QUARTER[2]
    square = rest * rest
    sine = rest + rest * square * ((SIN[0] * square + SIN[1]) * square + SIN[2])
    cosine = 1.0 - 0.5 * square + square * square * (
        (COS[0] * square + COS[1]) * square + COS[2]
    )
    quadrant = turns - 4.0 * jnp.floor(turns * 0.25)
    odd = (quadrant == 1.0) | (quadrant == 3.0)
    sine, cosine = jnp.where(odd, cosine, sine), jnp.where(odd, sine, cosine)
    return (
        jnp.where(quadrant >= 2.0, -sine, sine),
        jnp.where((quadrant == 1.0) | (quadrant == 2.0), -cosine, cosine),
    )


def rope_rows(length, frequency):
    sine, cosine = sine_cosine(length * frequency)
    lane = lax.broadcasted_iota(jnp.int32, (1, LANES), 1)
    return cosine, jnp.where(lane < LANES // 2, -sine, sine)


def one_hot_spread(fold):
    source = lax.broadcasted_iota(jnp.int32, (LANES, fold * LANES), 0)
    target = lax.broadcasted_iota(jnp.int32, (LANES, fold * LANES), 1)
    return (lax.shift_right_logical(target, fold.bit_length() - 1) == source).astype(F32).astype(BF16)


def spread_heads(rows, out_ref, heads):
    count, width = rows.shape
    chunks = width // LANES
    stacked = jnp.concatenate([rows[:, c * LANES : (c + 1) * LANES] for c in range(chunks)], axis=0)
    wide = jnp.dot(stacked.astype(BF16), one_hot_spread(heads), preferred_element_type=F32)
    columns = heads * LANES
    lane = lax.broadcasted_iota(jnp.int32, (count, columns), 1) & (heads - 1)
    for c in range(chunks):
        piece = wide[c * count : (c + 1) * count]
        for h in range(0, heads, 2):
            pair = [jnp.where(lane == h + i, piece, 0.0) for i in range(2)]
            out_ref[h * count : (h + 2) * count, c * columns : (c + 1) * columns] = (
                jnp.concatenate(pair, axis=0).astype(BF16)
            )


def qkv_kernel(
    tp, owner_hbm, lengths_hbm, frequency_hbm, states_hbm, gains_hbm, wq, wkv, cache, *rest
):
    outs = rest[:tp]
    table, places, cache_tiles = rest[tp : tp + 3]
    owner, lengths, frequency, states, gains = rest[tp + 3 : tp + 8]
    wq_buf, wkv_buf, spread_buf, sems, small_sems, cache_sems = rest[tp + 8 :]
    docs, width = states.shape
    heads = wq.shape[0] // width
    parts = wq_buf.shape[0]
    rows = wq_buf.shape[1]
    small = [
        pltpu.make_async_copy(source, target, small_sems.at[i])
        for i, (source, target) in enumerate(
            [
                (states_hbm, states),
                (gains_hbm, gains),
                (owner_hbm, owner),
                (lengths_hbm, lengths),
                (frequency_hbm, frequency),
            ]
        )
    ]
    copies = [
        pltpu.make_async_copy(wq.at[pl.ds(c * rows, rows)], wq_buf.at[c], sems.at[c])
        for c in range(parts)
    ]
    kv_copy = pltpu.make_async_copy(wkv, wkv_buf, sems.at[parts])
    cache_copies = tile_copies(cache, 0, cache_tiles, cache_sems)
    for copy in small + [kv_copy] + copies:
        copy.start()
    for copy in small:
        copy.wait()
    for copy in cache_copies:
        copy.start()
    me = lax.axis_index("tp")
    x = states[...].astype(F32)
    squares = jnp.broadcast_to(jnp.sum(x * x, axis=1, keepdims=True), (docs, LANES))
    both = jnp.concatenate(two_parts(x * gains[0:1, :]), axis=0)
    spread_heads(both, spread_buf, heads)
    length = lengths[owner[me]].astype(F32)
    cosine, sine = rope_rows(length, frequency[...])
    table[0:1, :] = cosine
    table[1:2, :] = sine
    table[2:3, :] = jnp.full((1, LANES), length, F32)
    table[3:, :] = jnp.zeros((table.shape[0] - 3, LANES), F32)
    for s in range(tp):
        places[s : s + 1, :] = jnp.full((1, LANES), owner[me ^ s], jnp.int32)
    kv_copy.wait()
    kv_total = jnp.dot(both.astype(BF16), wkv_buf[...], preferred_element_type=F32)
    total = jnp.zeros((heads * 2 * docs, LANES), F32)
    for c in range(parts):
        copies[c].wait()
        total = total + jnp.dot(
            spread_buf[:, c * rows : (c + 1) * rows], wq_buf[c], preferred_element_type=F32
        )
    total = total.reshape(heads, 2 * docs, LANES)
    for s in range(tp):
        doc = owner[me ^ s]
        out = outs[s]
        out[:heads, :] = pick_doc(total, doc, docs)
        kv_row = pick_doc(kv_total, doc, docs)[None]
        out[heads : heads + 1, :] = kv_row[:, :LANES]
        out[heads + 1 : heads + 2, :] = kv_row[:, LANES:]
        out[heads + 2 : heads + 3, :] = pick_doc(squares, doc, docs)[None]
        out[heads + 3 :, :] = jnp.zeros((out.shape[0] - heads - 3, LANES), F32)
    for copy in cache_copies:
        copy.wait()


def attend_kernel(tp, heads, rows, first, table, keys, cache, w, *rest):
    parts = rest[:tp]
    heads_out, new_kv_out, w_ready, scores, w_sems = rest[-5:]
    w_copies = block_copies(matrix_of(w), first, w_ready, w_sems)
    for copy in w_copies:
        copy.start()
    blocks = cache.shape[1] // rows
    sums = tree_sum([part[...] for part in parts])
    sums = sums * lax.rsqrt(sums[heads + 2 : heads + 3, :] / D + EPS)
    rotated = sums * table[0:1, :] + pltpu.roll(sums, LANES // 2, 1) * table[1:2, :]
    query = rotated[:heads].astype(BF16)
    key = rotated[heads : heads + 1].astype(BF16)
    value = sums[heads + 1 : heads + 2].astype(BF16)
    new_kv_out[:, :LANES] = key
    new_kv_out[:, LANES:] = value
    key = key.astype(F32)
    value = value.astype(F32)
    scale = LANES ** (-0.5)
    own = jnp.sum(query.astype(F32) * key, axis=1, keepdims=True) * scale
    column = lax.broadcasted_iota(jnp.int32, (heads, LANES), 1).astype(F32)
    length = table[2:3, :]
    tops = jnp.full((heads, LANES), -jnp.inf, F32)
    for b in range(blocks):
        block = jnp.dot(
            query, keys[:, b * rows : (b + 1) * rows], preferred_element_type=F32
        )
        for start in range(0, rows, LANES):
            at = b * rows + start
            piece = block[:, start : start + LANES] * scale
            piece = jnp.where(column < length - at, piece, -jnp.inf)
            tops = jnp.maximum(tops, piece)
            scores[:, at : at + LANES] = piece
    top = jnp.maximum(jnp.max(tops, axis=1, keepdims=True), own)
    own = jnp.exp(own - top)
    sums_by_lane = jnp.zeros((heads, LANES), F32)
    acc = own.astype(BF16).astype(F32) * value
    for b in range(blocks):
        weights = jnp.exp(scores[:, b * rows : (b + 1) * rows] - top)
        for start in range(0, rows, LANES):
            sums_by_lane = sums_by_lane + weights[:, start : start + LANES]
        acc = acc + jnp.dot(
            weights.astype(BF16),
            cache[1, b * rows : (b + 1) * rows, :],
            preferred_element_type=F32,
        )
    total = own + jnp.sum(sums_by_lane, axis=1, keepdims=True)
    heads_out[...] = (acc / total).astype(BF16)
    for copy in w_copies:
        copy.wait()


def out_kernel(tp, places, w_out, *rest):
    parts = rest[:tp]
    out, left = rest[-2:]
    docs = out.shape[0]
    row = lax.broadcasted_iota(jnp.int32, (left.shape[0], LANES), 0)
    own = [parts[s][...].astype(F32) for s in range(tp)]
    for h in range(own[0].shape[0]):
        piece = jnp.zeros((left.shape[0], LANES), F32)
        for s in range(tp):
            piece = jnp.where(row == places[s : s + 1, :], own[s][h : h + 1, :], piece)
        left[:, h * LANES : (h + 1) * LANES] = piece
    terms = jnp.dot(left[...].astype(BF16), w_out[...], preferred_element_type=F32)
    out[...] = terms[:docs].astype(BF16)


def fetch_kernel(first, token, w, *rest):
    out, sems = rest[-2:]
    copies = block_copies(matrix_of(w), first, out, sems)
    for copy in copies:
        copy.start()
    for copy in copies:
        copy.wait()


def fetch_and_turn_kernel(first, token, w, cache, out, turned, sems):
    copies = block_copies(matrix_of(w), first, out, sems)
    for copy in copies:
        copy.start()
    for start in range(0, cache.shape[1], KEY_ROWS):
        turned[:, start : start + KEY_ROWS] = cache[0, start : start + KEY_ROWS, :].T
    for copy in copies:
        copy.wait()


def gate_up_kernel(kv, groups, first, states, gains, w, *rest):
    ready, parts = rest[:groups], rest[groups : groups + kv]
    attn_out, partial_out, *blocks, spread_buf, w_sems = rest[groups + kv :]
    docs, width = states.shape
    hidden = w.shape[2]
    w_matrix = matrix_of(w)
    copies = []
    for i, block in enumerate(blocks):
        copies.append(block_copies(w_matrix, first, block, w_sems.at[i]))
        first += block.shape[1] // LANES
        for copy in copies[-1]:
            copy.start()
    attn = tree_sum([part[...].astype(F32) for part in parts]).astype(BF16)
    attn_out[...] = attn
    resid = (states[...].astype(F32) + attn.astype(F32)).astype(BF16).astype(F32)
    squares = jnp.sum(resid * resid, axis=1, keepdims=True)
    high, low = two_parts(resid * gains[1:2, :])
    spread(jnp.concatenate([high, high, low, low], axis=0).astype(BF16), spread_buf, docs)

    at = 0
    for i, block in enumerate([*ready, *blocks]):
        if i >= groups:
            for copy in copies[i - groups]:
                copy.wait()
        product = jnp.dot(spread_buf[...], block[...], preferred_element_type=F32)
        columns = slice(at, at + block.shape[1])
        partial_out[:, columns] = (product[: 2 * docs] + product[2 * docs :]).astype(BF16)
        at += block.shape[1]
    lane = lax.broadcasted_iota(jnp.int32, (docs, LANES), 1)
    first = squares.astype(BF16).astype(F32)
    second = (squares - first).astype(BF16).astype(F32)
    third = squares - first - second
    terms = jnp.where(lane == 0, first, jnp.where(lane == 1, second, jnp.where(lane == 2, third, 0.0)))
    partial_out[:, hidden:] = jnp.concatenate([terms, terms], axis=0).astype(BF16)


def down_kernel(tp, w_down, *rest):
    parts = rest[:tp]
    out, act_buf = rest[tp:]
    docs, width = out.shape
    hidden = w_down.shape[0]
    summed = tree_sum([part[...].astype(F32) for part in parts])
    squares = jnp.sum(summed[:docs, hidden:], axis=1, keepdims=True)
    inverse = lax.rsqrt(squares / D + EPS)
    gate = summed[:docs, :hidden] * inverse
    up = summed[docs:, :hidden] * inverse
    act_buf[...] = (gate / (1.0 + jnp.exp(-gate)) * up).astype(BF16)

    out[...] = jnp.dot(act_buf[...], w_down[...], preferred_element_type=F32).astype(BF16)


def cost(micros):
    return pl.CostEstimate(flops=0, bytes_accessed=int(micros * 3.69e6), transcendentals=0)


def params(docs, mib):
    return pltpu.CompilerParams(vmem_limit_bytes=(mib if docs <= 8 else mib + 24) * MIB)


def per_device(
    tp, kv,
    states, norm_gains, w_query, w_keyval, w_out, w_gate_up, w_down, kv_cache, lengths, owner_rows
):
    docs, width = states.shape
    heads = w_query.shape[1]
    cache_len = kv_cache.shape[1]
    hidden = w_gate_up.shape[2]
    wq = w_query.reshape(width * heads, LANES)
    wkv = w_keyval.reshape(width, 2 * LANES)
    cache = kv_cache.reshape(cache_len, 2 * LANES)
    packed = 2 * heads
    wq_parts = 4

    half = LANES // 2
    freq = ROPE_BASE ** (-(np.arange(half, dtype=np.float64) * 2.0 / LANES))
    freq = jnp.asarray(np.concatenate([freq, freq]).astype(np.float32)[None, :])
    *qkv_parts, table, places, cache_tiles = pl.pallas_call(
        functools.partial(qkv_kernel, tp),
        out_shape=[jax.ShapeDtypeStruct((packed, LANES), F32)] * tp
        + [
            jax.ShapeDtypeStruct((8, LANES), F32),
            jax.ShapeDtypeStruct((max(tp, 8), LANES), jnp.int32),
            pltpu.VMEM((2, cache_len, LANES), BF16),
        ],
        in_specs=[hbm()] * 8,
        out_specs=[vmem()] * (tp + 3),
        scratch_shapes=[
            pltpu.SMEM((docs,), jnp.int32),
            pltpu.SMEM((docs,), jnp.int32),
            pltpu.VMEM((1, LANES), F32),
            pltpu.VMEM((docs, width), BF16),
            pltpu.VMEM((2, width), F32),
            pltpu.VMEM((wq_parts, width * heads // wq_parts, LANES), BF16),
            pltpu.VMEM((width, 2 * LANES), BF16),
            pltpu.VMEM((heads * 2 * docs, width * heads), BF16),
            pltpu.SemaphoreType.DMA((wq_parts + 1,)),
            pltpu.SemaphoreType.DMA((5,)),
            pltpu.SemaphoreType.DMA((2,)),
        ],
        compiler_params=params(docs, 10),
        cost_estimate=cost(8),
        name="qkv",
    )(*(in_hbm(a) for a in (owner_rows, lengths, freq, states, norm_gains, wq, wkv, cache)))
    w_gu = in_hbm(w_gate_up)
    bounds = np.cumsum([0] + [hidden // LANES * n // 28 for n in GU_SHARES]).tolist()
    shares = list(zip(bounds, bounds[1:]))
    fetched = []

    chunks = max(2 * width // COPY_ROWS, 1)

    def block_of(share):
        return pltpu.VMEM((2 * width, (share[1] - share[0]) * LANES), BF16)

    def fetch(share, token, *keep):
        return pl.pallas_call(
            functools.partial(fetch_kernel, share[0]),
            out_shape=block_of(share),
            in_specs=[hbm(), hbm()] + [vmem()] * len(keep),
            out_specs=vmem(),
            scratch_shapes=[pltpu.SemaphoreType.DMA((chunks,))],
            compiler_params=params(docs, 2),
            cost_estimate=cost(0.3 * (share[1] - share[0])),
            name="fetch",
        )(token, w_gu, *keep)

    w_ready, turned = pl.pallas_call(
        functools.partial(fetch_and_turn_kernel, shares[0][0]),
        out_shape=[block_of(shares[0]), pltpu.VMEM((LANES, cache_len), BF16)],
        in_specs=[hbm(), hbm(), vmem()],
        out_specs=[vmem(), vmem()],
        scratch_shapes=[pltpu.SemaphoreType.DMA((chunks,))],
        compiler_params=params(docs, 4),
        cost_estimate=cost(3),
        name="fetch_and_turn_keys",
    )(table, w_gu, cache_tiles)
    fetched.append(w_ready)
    qkv_parts = exchange(qkv_parts, "tp", tp)[::-1]
    head_out, new_kv, w_ready = pl.pallas_call(
        functools.partial(attend_kernel, tp, heads, 512, shares[1][0]),
        out_shape=[
            jax.ShapeDtypeStruct((heads, LANES), BF16),
            jax.ShapeDtypeStruct((1, 2 * LANES), BF16),
            block_of(shares[1]),
        ],
        in_specs=[vmem(), vmem(), vmem(), hbm()] + [vmem()] * tp + [hbm()] * len(fetched),
        out_specs=[vmem()] * 3,
        scratch_shapes=[
            pltpu.VMEM((heads, cache_len), F32),
            pltpu.SemaphoreType.DMA((chunks,)),
        ],
        compiler_params=params(docs, 6),
        cost_estimate=cost(8),
        name="attend",
    )(table, turned, cache_tiles, w_gu, *qkv_parts, *fetched)
    fetched.append(w_ready)

    fetched.append(fetch(shares[2], head_out))
    head_parts = exchange([head_out] * tp, "tp", tp)
    out_part = pl.pallas_call(
        functools.partial(out_kernel, tp),
        out_shape=jax.ShapeDtypeStruct((docs, width), BF16),
        in_specs=[vmem()] * (tp + 2) + [hbm()],
        out_specs=vmem(),
        scratch_shapes=[pltpu.VMEM((max(docs, 8), heads * LANES), F32)],
        compiler_params=params(docs, 6),
        cost_estimate=cost(6),
        name="attn_project",
    )(places, w_out, *head_parts, fetched[-1])

    fetched.append(fetch(shares[3], out_part, w_down))
    out_parts = exchange([out_part] * kv, "kv", kv)
    attn_out, gu_part = pl.pallas_call(
        functools.partial(gate_up_kernel, kv, len(fetched), shares[4][0]),
        out_shape=[
            jax.ShapeDtypeStruct((docs, width), BF16),
            jax.ShapeDtypeStruct((2 * docs, hidden + LANES), BF16),
        ],
        in_specs=[vmem(), vmem(), hbm()] + [vmem()] * (len(fetched) + kv),
        out_specs=[vmem()] * 2,
        scratch_shapes=[
            *(block_of(share) for share in shares[4:]),
            pltpu.VMEM((4 * docs, 2 * width), BF16),
            pltpu.SemaphoreType.DMA((len(shares) - 4, chunks)),
        ],
        compiler_params=params(docs, 19),
        cost_estimate=cost(10),
        name="gate_up",
    )(states, norm_gains, w_gu, *fetched, *out_parts)

    gu_parts = exchange([gu_part] * tp, "tp", tp)
    ffn_part = pl.pallas_call(
        functools.partial(down_kernel, tp),
        out_shape=jax.ShapeDtypeStruct((docs, width), BF16),
        in_specs=[vmem()] * (1 + tp),
        out_specs=vmem(),
        scratch_shapes=[pltpu.VMEM((docs, hidden), BF16)],
        compiler_params=params(docs, 6),
        cost_estimate=cost(5),
        name="down",
    )(w_down, *gu_parts)
    ffn_parts = exchange([ffn_part] * kv, "kv", kv)
    ffn_out = tree_sum([part.astype(F32) for part in ffn_parts]).astype(BF16)
    return attn_out, ffn_out, new_kv.reshape(1, 1, 2 * LANES)


def solution(mesh):
    return jax.shard_map(
        functools.partial(per_device, mesh.shape["tp"], mesh.shape["kv"]),
        mesh=mesh,
        in_specs=(
            P("grp", "tp"),
            P(None, "tp"),
            P("tp", "kv", None),
            P("tp", "kv", None),
            P("kv", "tp"),
            P("tp", None, "kv"),
            P("kv", "tp"),
            P(("grp", "tp"), None, "kv", None),
            P("grp"),
            P("grp"),
        ),
        out_specs=(P("grp", "tp"), P("grp", "tp"), P(("grp", "tp"), "kv", None)),
        check_vma=False,
    )
```

```python
import functools
import math

import jax
import jax.numpy as jnp
import numpy as np
from jax import lax
from jax.experimental import pallas as pl
from jax.experimental.pallas import tpu as pltpu
from jax.sharding import PartitionSpec as P

D = 8192
EPS = 1e-05
ROPE_BASE = 500000.0
LANES = 128
MIB = 1 << 20
COPY_ROWS = 2048
KEY_ROWS = 512
GU_SHARES = (4, 6, 2, 2, 4, 4, 4, 2)
F32 = jnp.float32
BF16 = jnp.bfloat16
QUARTER = (1.5703125, 4.837512969970703125e-4, 7.549789948768648e-8)
SIN = (-1.9515295891e-4, 8.3321608736e-3, -1.6666654611e-1)
COS = (2.443315711809948e-5, -1.388731625493765e-3, 4.166664568298827e-2)


def vmem():
    return pl.BlockSpec(memory_space=pltpu.VMEM)


def hbm():
    return pl.BlockSpec(memory_space=pltpu.HBM)


def in_hbm(array):
    return pltpu.with_memory_space_constraint(array, pltpu.HBM)


def exchange(arrays, axis, size):
    return [arrays[0]] + [
        lax.ppermute(arrays[s], axis, [(i, i ^ s) for i in range(size)])
        for s in range(1, size)
    ]


def tree_sum(parts):
    while len(parts) > 1:
        parts = [a + b for a, b in zip(parts[::2], parts[1::2])]
    return parts[0]


def two_parts(scaled):
    high = scaled.astype(BF16).astype(F32)
    return high, scaled - high


def spread(rows16, out_ref, docs):
    width = rows16.shape[1]
    pick = one_hot_spread(2)
    row = lax.broadcasted_iota(jnp.int32, (4 * docs, 2 * LANES), 0)
    lane = lax.broadcasted_iota(jnp.int32, (4 * docs, 2 * LANES), 1)
    keep = (lax.shift_right_logical(row, docs.bit_length() - 1) & 1) == (lane & 1)
    chunks = width // LANES
    stacked = jnp.concatenate(
        [rows16[:, c * LANES : (c + 1) * LANES] for c in range(chunks)], axis=0
    )
    doubled = jnp.dot(stacked, pick, preferred_element_type=F32)
    for c in range(chunks):
        piece = doubled[c * 4 * docs : (c + 1) * 4 * docs]
        out_ref[:, 2 * c * LANES : 2 * (c + 1) * LANES] = jnp.where(keep, piece, 0.0).astype(BF16)


def tile_copies(matrix, first, buf, sems):
    return [
        pltpu.make_async_copy(
            matrix.at[:, pl.ds((first + i) * LANES, LANES)], buf.at[i], sems.at[i]
        )
        for i in range(buf.shape[0])
    ]


def matrix_of(w):
    return w if len(w.shape) == 2 else w.reshape(w.shape[0] * w.shape[1], w.shape[2])


def block_copies(matrix, first, buf, sems):
    rows, columns = buf.shape
    chunk = min(rows, COPY_ROWS)
    return [
        pltpu.make_async_copy(
            matrix.at[pl.ds(start, chunk), pl.ds(first * LANES, columns)],
            buf.at[pl.ds(start, chunk)],
            sems.at[start // chunk],
        )
        for start in range(0, rows, chunk)
    ]


def pick_doc(value, doc, docs):
    axis = value.ndim - 2
    row = lax.broadcasted_iota(jnp.int32, value.shape, axis)
    return jnp.sum(jnp.where(row & (docs - 1) == doc, value, 0.0), axis=axis)


def sine_cosine(angle):
    turns = jnp.floor(angle * (2.0 / math.pi) + 0.5)
    rest = ((angle - turns * QUARTER[0]) - turns * QUARTER[1]) - turns * QUARTER[2]
    square = rest * rest
    sine = rest + rest * square * ((SIN[0] * square + SIN[1]) * square + SIN[2])
    cosine = 1.0 - 0.5 * square + square * square * (
        (COS[0] * square + COS[1]) * square + COS[2]
    )
    quadrant = turns - 4.0 * jnp.floor(turns * 0.25)
    odd = (quadrant == 1.0) | (quadrant == 3.0)
    sine, cosine = jnp.where(odd, cosine, sine), jnp.where(odd, sine, cosine)
    return (
        jnp.where(quadrant >= 2.0, -sine, sine),
        jnp.where((quadrant == 1.0) | (quadrant == 2.0), -cosine, cosine),
    )


def rope_rows(length, frequency):
    sine, cosine = sine_cosine(length * frequency)
    lane = lax.broadcasted_iota(jnp.int32, (1, LANES), 1)
    return cosine, jnp.where(lane < LANES // 2, -sine, sine)


def one_hot_spread(fold):
    source = lax.broadcasted_iota(jnp.int32, (LANES, fold * LANES), 0)
    target = lax.broadcasted_iota(jnp.int32, (LANES, fold * LANES), 1)
    return (lax.shift_right_logical(target, fold.bit_length() - 1) == source).astype(F32).astype(BF16)


def spread_heads(rows, out_ref, heads):
    count, width = rows.shape
    chunks = width // LANES
    stacked = jnp.concatenate([rows[:, c * LANES : (c + 1) * LANES] for c in range(chunks)], axis=0)
    wide = jnp.dot(stacked.astype(BF16), one_hot_spread(heads), preferred_element_type=F32)
    columns = heads * LANES
    lane = lax.broadcasted_iota(jnp.int32, (count, columns), 1) & (heads - 1)
    for c in range(chunks):
        piece = wide[c * count : (c + 1) * count]
        for h in range(0, heads, 2):
            pair = [jnp.where(lane == h + i, piece, 0.0) for i in range(2)]
            out_ref[h * count : (h + 2) * count, c * columns : (c + 1) * columns] = (
                jnp.concatenate(pair, axis=0).astype(BF16)
            )


def qkv_kernel(
    tp, owner_hbm, lengths_hbm, frequency_hbm, states_hbm, gains_hbm, wq, wkv, cache, *rest
):
    outs = rest[:tp]
    table, places, cache_tiles = rest[tp : tp + 3]
    owner, lengths, frequency, states, gains = rest[tp + 3 : tp + 8]
    wq_buf, wkv_buf, spread_buf, sems, small_sems, cache_sems = rest[tp + 8 :]
    docs, width = states.shape
    heads = wq.shape[0] // width
    parts = wq_buf.shape[0]
    rows = wq_buf.shape[1]
    small = [
        pltpu.make_async_copy(source, target, small_sems.at[i])
        for i, (source, target) in enumerate(
            [
                (states_hbm, states),
                (gains_hbm, gains),
                (owner_hbm, owner),
                (lengths_hbm, lengths),
                (frequency_hbm, frequency),
            ]
        )
    ]
    copies = [
        pltpu.make_async_copy(wq.at[pl.ds(c * rows, rows)], wq_buf.at[c], sems.at[c])
        for c in range(parts)
    ]
    kv_copy = pltpu.make_async_copy(wkv, wkv_buf, sems.at[parts])
    cache_copies = tile_copies(cache, 0, cache_tiles, cache_sems)
    for copy in small + [kv_copy] + copies:
        copy.start()
    for copy in small:
        copy.wait()
    for copy in cache_copies:
        copy.start()
    me = lax.axis_index("tp")
    x = states[...].astype(F32)
    squares = jnp.broadcast_to(jnp.sum(x * x, axis=1, keepdims=True), (docs, LANES))
    both = jnp.concatenate(two_parts(x * gains[0:1, :]), axis=0)
    spread_heads(both, spread_buf, heads)
    length = lengths[owner[me]].astype(F32)
    cosine, sine = rope_rows(length, frequency[...])
    table[0:1, :] = cosine
    table[1:2, :] = sine
    table[2:3, :] = jnp.full((1, LANES), length, F32)
    table[3:, :] = jnp.zeros((table.shape[0] - 3, LANES), F32)
    for s in range(tp):
        places[s : s + 1, :] = jnp.full((1, LANES), owner[me ^ s], jnp.int32)
    kv_copy.wait()
    kv_total = jnp.dot(both.astype(BF16), wkv_buf[...], preferred_element_type=F32)
    total = jnp.zeros((heads * 2 * docs, LANES), F32)
    for c in range(parts):
        copies[c].wait()
        total = total + jnp.dot(
            spread_buf[:, c * rows : (c + 1) * rows], wq_buf[c], preferred_element_type=F32
        )
    total = total.reshape(heads, 2 * docs, LANES)
    for s in range(tp):
        doc = owner[me ^ s]
        out = outs[s]
        out[:heads, :] = pick_doc(total, doc, docs)
        kv_row = pick_doc(kv_total, doc, docs)[None]
        out[heads : heads + 1, :] = kv_row[:, :LANES]
        out[heads + 1 : heads + 2, :] = kv_row[:, LANES:]
        out[heads + 2 : heads + 3, :] = pick_doc(squares, doc, docs)[None]
        out[heads + 3 :, :] = jnp.zeros((out.shape[0] - heads - 3, LANES), F32)
    for copy in cache_copies:
        copy.wait()


def attend_kernel(tp, heads, rows, first, table, keys, cache, w, *rest):
    parts = rest[:tp]
    heads_out, new_kv_out, w_ready, scores, new_kv, w_sems, out_sem = rest[-7:]
    w_copies = block_copies(matrix_of(w), first, w_ready, w_sems)
    for copy in w_copies:
        copy.start()
    blocks = cache.shape[1] // rows
    sums = tree_sum([part[...] for part in parts])
    sums = sums * lax.rsqrt(sums[heads + 2 : heads + 3, :] / D + EPS)
    rotated = sums * table[0:1, :] + pltpu.roll(sums, LANES // 2, 1) * table[1:2, :]
    query = rotated[:heads].astype(BF16)
    key = rotated[heads : heads + 1].astype(BF16)
    value = sums[heads + 1 : heads + 2].astype(BF16)
    new_kv[:, :LANES] = key
    new_kv[:, LANES:] = value
    out_copy = pltpu.make_async_copy(new_kv, new_kv_out, out_sem.at[0])
    out_copy.start()
    key = key.astype(F32)
    value = value.astype(F32)
    scale = LANES ** (-0.5)
    own = jnp.sum(query.astype(F32) * key, axis=1, keepdims=True) * scale
    column = lax.broadcasted_iota(jnp.int32, (heads, LANES), 1).astype(F32)
    length = table[2:3, :]
    tops = jnp.full((heads, LANES), -jnp.inf, F32)
    for b in range(blocks):
        block = jnp.dot(
            query, keys[:, b * rows : (b + 1) * rows], preferred_element_type=F32
        )
        for start in range(0, rows, LANES):
            at = b * rows + start
            piece = block[:, start : start + LANES] * scale
            piece = jnp.where(column < length - at, piece, -jnp.inf)
            tops = jnp.maximum(tops, piece)
            scores[:, at : at + LANES] = piece
    top = jnp.maximum(jnp.max(tops, axis=1, keepdims=True), own)
    own = jnp.exp(own - top)
    sums_by_lane = jnp.zeros((heads, LANES), F32)
    acc = own.astype(BF16).astype(F32) * value
    for b in range(blocks):
        weights = jnp.exp(scores[:, b * rows : (b + 1) * rows] - top)
        for start in range(0, rows, LANES):
            sums_by_lane = sums_by_lane + weights[:, start : start + LANES]
        acc = acc + jnp.dot(
            weights.astype(BF16),
            cache[1, b * rows : (b + 1) * rows, :],
            preferred_element_type=F32,
        )
    total = own + jnp.sum(sums_by_lane, axis=1, keepdims=True)
    heads_out[...] = (acc / total).astype(BF16)
    for copy in w_copies:
        copy.wait()
    out_copy.wait()


def out_kernel(tp, places, w_out, *rest):
    parts = rest[:tp]
    out, left = rest[-2:]
    docs = out.shape[0]
    row = lax.broadcasted_iota(jnp.int32, (left.shape[0], LANES), 0)
    own = [parts[s][...].astype(F32) for s in range(tp)]
    for h in range(own[0].shape[0]):
        piece = jnp.zeros((left.shape[0], LANES), F32)
        for s in range(tp):
            piece = jnp.where(row == places[s : s + 1, :], own[s][h : h + 1, :], piece)
        left[:, h * LANES : (h + 1) * LANES] = piece
    terms = jnp.dot(left[...].astype(BF16), w_out[...], preferred_element_type=F32)
    out[...] = terms[:docs].astype(BF16)


def fetch_kernel(first, token, w, *rest):
    out, sems = rest[-2:]
    copies = block_copies(matrix_of(w), first, out, sems)
    for copy in copies:
        copy.start()
    for copy in copies:
        copy.wait()


def fetch_and_turn_kernel(first, token, w, cache, out, turned, sems):
    copies = block_copies(matrix_of(w), first, out, sems)
    for copy in copies:
        copy.start()
    for start in range(0, cache.shape[1], KEY_ROWS):
        turned[:, start : start + KEY_ROWS] = cache[0, start : start + KEY_ROWS, :].T
    for copy in copies:
        copy.wait()


def gate_up_kernel(kv, groups, first, states, gains, w, *rest):
    ready, parts = rest[:groups], rest[groups : groups + kv]
    attn_out, partial_out, *blocks, spread_buf, attn_buf, w_sems, out_sem = rest[groups + kv :]
    docs, width = states.shape
    hidden = w.shape[2]
    w_matrix = matrix_of(w)
    copies = []
    for i, block in enumerate(blocks):
        copies.append(block_copies(w_matrix, first, block, w_sems.at[i]))
        first += block.shape[1] // LANES
        for copy in copies[-1]:
            copy.start()
    attn = tree_sum([part[...].astype(F32) for part in parts]).astype(BF16)
    attn_buf[...] = attn
    out_copy = pltpu.make_async_copy(attn_buf, attn_out, out_sem.at[0])
    out_copy.start()
    resid = (states[...].astype(F32) + attn.astype(F32)).astype(BF16).astype(F32)
    squares = jnp.sum(resid * resid, axis=1, keepdims=True)
    high, low = two_parts(resid * gains[1:2, :])
    spread(jnp.concatenate([high, high, low, low], axis=0).astype(BF16), spread_buf, docs)

    at = 0
    for i, block in enumerate([*ready, *blocks]):
        if i >= groups:
            for copy in copies[i - groups]:
                copy.wait()
        product = jnp.dot(spread_buf[...], block[...], preferred_element_type=F32)
        columns = slice(at, at + block.shape[1])
        partial_out[:, columns] = (product[: 2 * docs] + product[2 * docs :]).astype(BF16)
        at += block.shape[1]
    lane = lax.broadcasted_iota(jnp.int32, (docs, LANES), 1)
    first = squares.astype(BF16).astype(F32)
    second = (squares - first).astype(BF16).astype(F32)
    third = squares - first - second
    terms = jnp.where(lane == 0, first, jnp.where(lane == 1, second, jnp.where(lane == 2, third, 0.0)))
    partial_out[:, hidden:] = jnp.concatenate([terms, terms], axis=0).astype(BF16)
    out_copy.wait()


def down_kernel(tp, w_down, *rest):
    parts = rest[:tp]
    out, act_buf = rest[tp:]
    docs, width = out.shape
    hidden = w_down.shape[0]
    summed = tree_sum([part[...].astype(F32) for part in parts])
    squares = jnp.sum(summed[:docs, hidden:], axis=1, keepdims=True)
    inverse = lax.rsqrt(squares / D + EPS)
    gate = summed[:docs, :hidden] * inverse
    up = summed[docs:, :hidden] * inverse
    act_buf[...] = (gate / (1.0 + jnp.exp(-gate)) * up).astype(BF16)

    out[...] = jnp.dot(act_buf[...], w_down[...], preferred_element_type=F32).astype(BF16)


def cost(micros):
    return pl.CostEstimate(flops=0, bytes_accessed=int(micros * 3.69e6), transcendentals=0)


def params(docs, mib):
    return pltpu.CompilerParams(vmem_limit_bytes=(mib if docs <= 8 else mib + 24) * MIB)


def per_device(
    tp, kv,
    states, norm_gains, w_query, w_keyval, w_out, w_gate_up, w_down, kv_cache, lengths, owner_rows
):
    docs, width = states.shape
    heads = w_query.shape[1]
    cache_len = kv_cache.shape[1]
    hidden = w_gate_up.shape[2]
    wq = w_query.reshape(width * heads, LANES)
    wkv = w_keyval.reshape(width, 2 * LANES)
    cache = kv_cache.reshape(cache_len, 2 * LANES)
    packed = 2 * heads
    wq_parts = 4

    half = LANES // 2
    freq = ROPE_BASE ** (-(np.arange(half, dtype=np.float64) * 2.0 / LANES))
    freq = jnp.asarray(np.concatenate([freq, freq]).astype(np.float32)[None, :])
    *qkv_parts, table, places, cache_tiles = pl.pallas_call(
        functools.partial(qkv_kernel, tp),
        out_shape=[jax.ShapeDtypeStruct((packed, LANES), F32)] * tp
        + [
            jax.ShapeDtypeStruct((8, LANES), F32),
            jax.ShapeDtypeStruct((max(tp, 8), LANES), jnp.int32),
            pltpu.VMEM((2, cache_len, LANES), BF16),
        ],
        in_specs=[hbm()] * 8,
        out_specs=[vmem()] * (tp + 3),
        scratch_shapes=[
            pltpu.SMEM((docs,), jnp.int32),
            pltpu.SMEM((docs,), jnp.int32),
            pltpu.VMEM((1, LANES), F32),
            pltpu.VMEM((docs, width), BF16),
            pltpu.VMEM((2, width), F32),
            pltpu.VMEM((wq_parts, width * heads // wq_parts, LANES), BF16),
            pltpu.VMEM((width, 2 * LANES), BF16),
            pltpu.VMEM((heads * 2 * docs, width * heads), BF16),
            pltpu.SemaphoreType.DMA((wq_parts + 1,)),
            pltpu.SemaphoreType.DMA((5,)),
            pltpu.SemaphoreType.DMA((2,)),
        ],
        compiler_params=params(docs, 10),
        cost_estimate=cost(8),
        name="qkv",
    )(*(in_hbm(a) for a in (owner_rows, lengths, freq, states, norm_gains, wq, wkv, cache)))
    w_gu = in_hbm(w_gate_up)
    bounds = np.cumsum([0] + [hidden // LANES * n // 28 for n in GU_SHARES]).tolist()
    shares = list(zip(bounds, bounds[1:]))
    fetched = []

    chunks = max(2 * width // COPY_ROWS, 1)

    def block_of(share):
        return pltpu.VMEM((2 * width, (share[1] - share[0]) * LANES), BF16)

    def fetch(share, token, *keep):
        return pl.pallas_call(
            functools.partial(fetch_kernel, share[0]),
            out_shape=block_of(share),
            in_specs=[hbm(), hbm()] + [vmem()] * len(keep),
            out_specs=vmem(),
            scratch_shapes=[pltpu.SemaphoreType.DMA((chunks,))],
            compiler_params=params(docs, 2),
            cost_estimate=cost(0.3 * (share[1] - share[0])),
            name="fetch",
        )(token, w_gu, *keep)

    w_ready, turned = pl.pallas_call(
        functools.partial(fetch_and_turn_kernel, shares[0][0]),
        out_shape=[block_of(shares[0]), pltpu.VMEM((LANES, cache_len), BF16)],
        in_specs=[hbm(), hbm(), vmem()],
        out_specs=[vmem(), vmem()],
        scratch_shapes=[pltpu.SemaphoreType.DMA((chunks,))],
        compiler_params=params(docs, 4),
        cost_estimate=cost(3),
        name="fetch_and_turn_keys",
    )(table, w_gu, cache_tiles)
    fetched.append(w_ready)
    qkv_parts = exchange(qkv_parts, "tp", tp)[::-1]
    head_out, new_kv, w_ready = pl.pallas_call(
        functools.partial(attend_kernel, tp, heads, 512, shares[1][0]),
        out_shape=[
            jax.ShapeDtypeStruct((heads, LANES), BF16),
            jax.ShapeDtypeStruct((1, 2 * LANES), BF16),
            block_of(shares[1]),
        ],
        in_specs=[vmem(), vmem(), vmem(), hbm()] + [vmem()] * tp + [hbm()] * len(fetched),
        out_specs=[vmem(), hbm(), vmem()],
        scratch_shapes=[
            pltpu.VMEM((heads, cache_len), F32),
            pltpu.VMEM((1, 2 * LANES), BF16),
            pltpu.SemaphoreType.DMA((chunks,)),
            pltpu.SemaphoreType.DMA((1,)),
        ],
        compiler_params=params(docs, 6),
        cost_estimate=cost(8),
        name="attend",
    )(table, turned, cache_tiles, w_gu, *qkv_parts, *fetched)
    fetched.append(w_ready)

    fetched.append(fetch(shares[2], head_out))
    head_parts = exchange([head_out] * tp, "tp", tp)
    out_part = pl.pallas_call(
        functools.partial(out_kernel, tp),
        out_shape=jax.ShapeDtypeStruct((docs, width), BF16),
        in_specs=[vmem()] * (tp + 2) + [hbm()],
        out_specs=vmem(),
        scratch_shapes=[pltpu.VMEM((max(docs, 8), heads * LANES), F32)],
        compiler_params=params(docs, 6),
        cost_estimate=cost(6),
        name="attn_project",
    )(places, w_out, *head_parts, fetched[-1])

    fetched.append(fetch(shares[3], out_part, w_down))
    out_parts = exchange([out_part] * kv, "kv", kv)
    attn_out, gu_part = pl.pallas_call(
        functools.partial(gate_up_kernel, kv, len(fetched), shares[4][0]),
        out_shape=[
            jax.ShapeDtypeStruct((docs, width), BF16),
            jax.ShapeDtypeStruct((2 * docs, hidden + LANES), BF16),
        ],
        in_specs=[vmem(), vmem(), hbm()] + [vmem()] * (len(fetched) + kv),
        out_specs=[hbm(), vmem()],
        scratch_shapes=[
            *(block_of(share) for share in shares[4:]),
            pltpu.VMEM((4 * docs, 2 * width), BF16),
            pltpu.VMEM((docs, width), BF16),
            pltpu.SemaphoreType.DMA((len(shares) - 4, chunks)),
            pltpu.SemaphoreType.DMA((1,)),
        ],
        compiler_params=params(docs, 19),
        cost_estimate=cost(10),
        name="gate_up",
    )(states, norm_gains, w_gu, *fetched, *out_parts)

    gu_parts = exchange([gu_part] * tp, "tp", tp)
    ffn_part = pl.pallas_call(
        functools.partial(down_kernel, tp),
        out_shape=jax.ShapeDtypeStruct((docs, width), BF16),
        in_specs=[vmem()] * (1 + tp),
        out_specs=vmem(),
        scratch_shapes=[pltpu.VMEM((docs, hidden), BF16)],
        compiler_params=params(docs, 6),
        cost_estimate=cost(5),
        name="down",
    )(w_down, *gu_parts)
    ffn_parts = exchange([ffn_part] * kv, "kv", kv)
    ffn_out = tree_sum([part.astype(F32) for part in ffn_parts]).astype(BF16)
    return attn_out, ffn_out, new_kv.reshape(1, 1, 2 * LANES)


def solution(mesh):
    return jax.shard_map(
        functools.partial(per_device, mesh.shape["tp"], mesh.shape["kv"]),
        mesh=mesh,
        in_specs=(
            P("grp", "tp"),
            P(None, "tp"),
            P("tp", "kv", None),
            P("tp", "kv", None),
            P("kv", "tp"),
            P("tp", None, "kv"),
            P("kv", "tp"),
            P(("grp", "tp"), None, "kv", None),
            P("grp"),
            P("grp"),
        ),
        out_specs=(P("grp", "tp"), P("grp", "tp"), P(("grp", "tp"), "kv", None)),
        check_vma=False,
    )
```

```python
import functools
import math

import jax
import jax.numpy as jnp
import numpy as np
from jax import lax
from jax.experimental import pallas as pl
from jax.experimental.pallas import tpu as pltpu
from jax.sharding import PartitionSpec as P

D = 8192
EPS = 1e-05
ROPE_BASE = 500000.0
LANES = 128
MIB = 1 << 20
COPY_ROWS = 2048
DOWN_ROWS = 1024
GU_SHARES = (4, 6, 4, 2, 4, 4, 2, 2)
F32 = jnp.float32
BF16 = jnp.bfloat16
QUARTER = (1.5703125, 4.837512969970703125e-4, 7.549789948768648e-8)
SIN = (-1.9515295891e-4, 8.3321608736e-3, -1.6666654611e-1)
COS = (2.443315711809948e-5, -1.388731625493765e-3, 4.166664568298827e-2)


def vmem():
    return pl.BlockSpec(memory_space=pltpu.VMEM)


def hbm():
    return pl.BlockSpec(memory_space=pltpu.HBM)


def in_hbm(array):
    return pltpu.with_memory_space_constraint(array, pltpu.HBM)


def exchange(arrays, axis, size):
    return [arrays[0]] + [
        lax.ppermute(arrays[s], axis, [(i, i ^ s) for i in range(size)])
        for s in range(1, size)
    ]


def tree_sum(parts):
    while len(parts) > 1:
        parts = [a + b for a, b in zip(parts[::2], parts[1::2])]
    return parts[0]


def two_parts(scaled):
    high = scaled.astype(BF16).astype(F32)
    return high, scaled - high


def spread(rows16, out_ref, docs):
    width = rows16.shape[1]
    pick = one_hot_spread(2)
    row = lax.broadcasted_iota(jnp.int32, (4 * docs, 2 * LANES), 0)
    lane = lax.broadcasted_iota(jnp.int32, (4 * docs, 2 * LANES), 1)
    keep = (lax.shift_right_logical(row, docs.bit_length() - 1) & 1) == (lane & 1)
    chunks = width // LANES
    stacked = jnp.concatenate(
        [rows16[:, c * LANES : (c + 1) * LANES] for c in range(chunks)], axis=0
    )
    doubled = jnp.dot(stacked, pick, preferred_element_type=F32)
    for c in range(chunks):
        piece = doubled[c * 4 * docs : (c + 1) * 4 * docs]
        out_ref[:, 2 * c * LANES : 2 * (c + 1) * LANES] = jnp.where(keep, piece, 0.0).astype(BF16)


def matrix_of(w):
    return w if len(w.shape) == 2 else w.reshape(w.shape[0] * w.shape[1], w.shape[2])


def block_copies(matrix, first, buf, sems):
    rows, columns = buf.shape
    chunk = min(rows, COPY_ROWS)
    return [
        pltpu.make_async_copy(
            matrix.at[pl.ds(start, chunk), pl.ds(first * LANES, columns)],
            buf.at[pl.ds(start, chunk)],
            sems.at[start // chunk],
        )
        for start in range(0, rows, chunk)
    ]


def pick_doc(value, doc, docs):
    axis = value.ndim - 2
    row = lax.broadcasted_iota(jnp.int32, value.shape, axis)
    return jnp.sum(jnp.where(row & (docs - 1) == doc, value, 0.0), axis=axis)


def sine_cosine(angle):
    turns = jnp.floor(angle * (2.0 / math.pi) + 0.5)
    rest = ((angle - turns * QUARTER[0]) - turns * QUARTER[1]) - turns * QUARTER[2]
    square = rest * rest
    sine = rest + rest * square * ((SIN[0] * square + SIN[1]) * square + SIN[2])
    cosine = 1.0 - 0.5 * square + square * square * (
        (COS[0] * square + COS[1]) * square + COS[2]
    )
    quadrant = turns - 4.0 * jnp.floor(turns * 0.25)
    odd = (quadrant == 1.0) | (quadrant == 3.0)
    sine, cosine = jnp.where(odd, cosine, sine), jnp.where(odd, sine, cosine)
    return (
        jnp.where(quadrant >= 2.0, -sine, sine),
        jnp.where((quadrant == 1.0) | (quadrant == 2.0), -cosine, cosine),
    )


def rope_rows(length, frequency):
    sine, cosine = sine_cosine(length * frequency)
    lane = lax.broadcasted_iota(jnp.int32, (1, LANES), 1)
    return cosine, jnp.where(lane < LANES // 2, -sine, sine)


def one_hot_spread(fold):
    source = lax.broadcasted_iota(jnp.int32, (LANES, fold * LANES), 0)
    target = lax.broadcasted_iota(jnp.int32, (LANES, fold * LANES), 1)
    return (lax.shift_right_logical(target, fold.bit_length() - 1) == source).astype(F32).astype(BF16)


def spread_heads(rows, out_ref, heads):
    count, width = rows.shape
    chunks = width // LANES
    stacked = jnp.concatenate([rows[:, c * LANES : (c + 1) * LANES] for c in range(chunks)], axis=0)
    wide = jnp.dot(stacked.astype(BF16), one_hot_spread(heads), preferred_element_type=F32)
    columns = heads * LANES
    lane = lax.broadcasted_iota(jnp.int32, (count, columns), 1) & (heads - 1)
    for c in range(chunks):
        piece = wide[c * count : (c + 1) * count]
        for h in range(0, heads, 2):
            pair = [jnp.where(lane == h + i, piece, 0.0) for i in range(2)]
            out_ref[h * count : (h + 2) * count, c * columns : (c + 1) * columns] = (
                jnp.concatenate(pair, axis=0).astype(BF16)
            )


def qkv_kernel(tp, owner_hbm, lengths_hbm, frequency_hbm, states_hbm, gains_hbm, wq, wkv, *rest):
    outs = rest[:tp]
    table, places = rest[tp : tp + 2]
    owner, lengths, frequency, states, gains = rest[tp + 2 : tp + 7]
    wq_buf, wkv_buf, spread_buf, sems, small_sems = rest[tp + 7 :]
    docs, width = states.shape
    heads = wq.shape[0] // width
    parts = wq_buf.shape[0]
    rows = wq_buf.shape[1]
    small = [
        pltpu.make_async_copy(source, target, small_sems.at[i])
        for i, (source, target) in enumerate(
            [
                (states_hbm, states),
                (gains_hbm, gains),
                (owner_hbm, owner),
                (lengths_hbm, lengths),
                (frequency_hbm, frequency),
            ]
        )
    ]
    copies = [
        pltpu.make_async_copy(wq.at[pl.ds(c * rows, rows)], wq_buf.at[c], sems.at[c])
        for c in range(parts)
    ]
    kv_copy = pltpu.make_async_copy(wkv, wkv_buf, sems.at[parts])
    for copy in small + [kv_copy] + copies:
        copy.start()
    for copy in small:
        copy.wait()
    me = lax.axis_index("tp")
    x = states[...].astype(F32)
    squares = jnp.broadcast_to(jnp.sum(x * x, axis=1, keepdims=True), (docs, LANES))
    both = jnp.concatenate(two_parts(x * gains[0:1, :]), axis=0)
    kv_copy.wait()
    kv_total = jnp.dot(both.astype(BF16), wkv_buf[...], preferred_element_type=F32)
    spread_heads(both, spread_buf, heads)
    length = lengths[owner[me]].astype(F32)
    cosine, sine = rope_rows(length, frequency[...])
    table[0:1, :] = cosine
    table[1:2, :] = sine
    table[2:3, :] = jnp.full((1, LANES), length, F32)
    table[3:, :] = jnp.zeros((table.shape[0] - 3, LANES), F32)
    for s in range(tp):
        places[s : s + 1, :] = jnp.full((1, LANES), owner[me ^ s], jnp.int32)
    total = jnp.zeros((heads * 2 * docs, LANES), F32)
    for c in range(parts):
        copies[c].wait()
        total = total + jnp.dot(
            spread_buf[:, c * rows : (c + 1) * rows], wq_buf[c], preferred_element_type=F32
        )
    total = total.reshape(heads, 2 * docs, LANES)
    for s in range(tp):
        doc = owner[me ^ s]
        out = outs[s]
        out[:heads, :] = pick_doc(total, doc, docs)
        kv_row = pick_doc(kv_total, doc, docs)[None]
        out[heads : heads + 1, :] = kv_row[:, :LANES]
        out[heads + 1 : heads + 2, :] = kv_row[:, LANES:]
        out[heads + 2 : heads + 3, :] = pick_doc(squares, doc, docs)[None]
        out[heads + 3 :, :] = jnp.zeros((out.shape[0] - heads - 3, LANES), F32)


def attend_kernel(tp, heads, rows, first, table, cache, w, *rest):
    parts = rest[:tp]
    heads_out, new_kv_out, w_ready, scores, new_kv, w_sems, out_sem = rest[-7:]
    w_copies = block_copies(matrix_of(w), first, w_ready, w_sems)
    for copy in w_copies:
        copy.start()
    blocks = cache.shape[0] // rows
    sums = tree_sum([part[...] for part in parts])
    sums = sums * lax.rsqrt(sums[heads + 2 : heads + 3, :] / D + EPS)
    rotated = sums * table[0:1, :] + pltpu.roll(sums, LANES // 2, 1) * table[1:2, :]
    query = rotated[:heads].astype(BF16)
    key = rotated[heads : heads + 1].astype(BF16)
    value = sums[heads + 1 : heads + 2].astype(BF16)
    new_kv[:, :LANES] = key
    new_kv[:, LANES:] = value
    out_copy = pltpu.make_async_copy(new_kv, new_kv_out, out_sem.at[0])
    out_copy.start()
    key = key.astype(F32)
    value = value.astype(F32)
    scale = LANES ** (-0.5)
    own = jnp.sum(query.astype(F32) * key, axis=1, keepdims=True) * scale
    column = lax.broadcasted_iota(jnp.int32, (heads, LANES), 1).astype(F32)
    length = table[2:3, :]
    tops = jnp.full((heads, LANES), -jnp.inf, F32)
    for b in range(blocks):
        block = lax.dot_general(
            query,
            cache[b * rows : (b + 1) * rows, :LANES],
            (((1,), (1,)), ((), ())),
            preferred_element_type=F32,
        )
        for start in range(0, rows, LANES):
            at = b * rows + start
            piece = block[:, start : start + LANES] * scale
            piece = jnp.where(column < length - at, piece, -jnp.inf)
            tops = jnp.maximum(tops, piece)
            scores[:, at : at + LANES] = piece
    top = jnp.maximum(jnp.max(tops, axis=1, keepdims=True), own)
    own = jnp.exp(own - top)
    sums_by_lane = jnp.zeros((heads, LANES), F32)
    acc = own.astype(BF16).astype(F32) * value
    for b in range(blocks):
        weights = jnp.exp(scores[:, b * rows : (b + 1) * rows] - top)
        for start in range(0, rows, LANES):
            sums_by_lane = sums_by_lane + weights[:, start : start + LANES]
        acc = acc + jnp.dot(
            weights.astype(BF16),
            cache[b * rows : (b + 1) * rows, LANES:],
            preferred_element_type=F32,
        )
    total = own + jnp.sum(sums_by_lane, axis=1, keepdims=True)
    heads_out[...] = (acc / total).astype(BF16)
    for copy in w_copies:
        copy.wait()
    out_copy.wait()


def out_kernel(tp, places, w_out, *rest):
    parts = rest[:tp]
    out, left = rest[-2:]
    docs = out.shape[0]
    row = lax.broadcasted_iota(jnp.int32, (left.shape[0], LANES), 0)
    own = [parts[s][...].astype(F32) for s in range(tp)]
    for h in range(own[0].shape[0]):
        piece = jnp.zeros((left.shape[0], LANES), F32)
        for s in range(tp):
            piece = jnp.where(row == places[s : s + 1, :], own[s][h : h + 1, :], piece)
        left[:, h * LANES : (h + 1) * LANES] = piece
    terms = jnp.dot(left[...].astype(BF16), w_out[...], preferred_element_type=F32)
    out[...] = terms[:docs].astype(BF16)


def fetch_kernel(first, token, w, *rest):
    out, sems = rest[-2:]
    copies = block_copies(matrix_of(w), first, out, sems)
    for copy in copies:
        copy.start()
    for copy in copies:
        copy.wait()


def gate_up_kernel(kv, groups, first, states, gains, w, *rest):
    ready, parts = rest[:groups], rest[groups : groups + kv]
    attn_out, partial_out, *blocks, spread_buf, attn_buf, w_sems, out_sem = rest[groups + kv :]
    docs, width = states.shape
    hidden = w.shape[2]
    w_matrix = matrix_of(w)
    copies = []
    for i, block in enumerate(blocks):
        copies.append(block_copies(w_matrix, first, block, w_sems.at[i]))
        first += block.shape[1] // LANES
        for copy in copies[-1]:
            copy.start()
    attn = tree_sum([part[...].astype(F32) for part in parts]).astype(BF16)
    attn_buf[...] = attn
    out_copy = pltpu.make_async_copy(attn_buf, attn_out, out_sem.at[0])
    out_copy.start()
    resid = (states[...].astype(F32) + attn.astype(F32)).astype(BF16).astype(F32)
    squares = jnp.sum(resid * resid, axis=1, keepdims=True)
    high, low = two_parts(resid * gains[1:2, :])
    spread(jnp.concatenate([high, high, low, low], axis=0).astype(BF16), spread_buf, docs)

    at = 0
    for i, block in enumerate([*ready, *blocks]):
        if i >= groups:
            for copy in copies[i - groups]:
                copy.wait()
        product = jnp.dot(spread_buf[...], block[...], preferred_element_type=F32)
        columns = slice(at, at + block.shape[1])
        partial_out[:, columns] = (product[: 2 * docs] + product[2 * docs :]).astype(BF16)
        at += block.shape[1]
    lane = lax.broadcasted_iota(jnp.int32, (docs, LANES), 1)
    first = squares.astype(BF16).astype(F32)
    second = (squares - first).astype(BF16).astype(F32)
    third = squares - first - second
    terms = jnp.where(lane == 0, first, jnp.where(lane == 1, second, jnp.where(lane == 2, third, 0.0)))
    partial_out[:, hidden:] = jnp.concatenate([terms, terms], axis=0).astype(BF16)
    out_copy.wait()


def down_kernel(tp, w_down, *rest):
    parts, out = rest[:tp], rest[tp]
    docs, width = out.shape
    hidden = w_down.shape[0]

    def summed(start, size):
        return tree_sum([part[:, start : start + size].astype(F32) for part in parts])

    squares = jnp.sum(summed(hidden, LANES)[:docs], axis=1, keepdims=True)
    inverse = lax.rsqrt(squares / D + EPS)
    total = jnp.zeros((docs, width), F32)
    for start in range(0, hidden, DOWN_ROWS):
        size = min(DOWN_ROWS, hidden - start)
        both = summed(start, size)
        gate = both[:docs] * inverse
        up = both[docs:] * inverse
        act = (gate / (1.0 + jnp.exp(-gate)) * up).astype(BF16)
        total = total + jnp.dot(
            act, w_down[start : start + size, :], preferred_element_type=F32
        )
    out[...] = total.astype(BF16)


def cost(micros):
    return pl.CostEstimate(flops=0, bytes_accessed=int(micros * 3.69e6), transcendentals=0)


def params(docs, mib):
    return pltpu.CompilerParams(vmem_limit_bytes=(mib if docs <= 8 else mib + 24) * MIB)


def per_device(
    tp, kv,
    states, norm_gains, w_query, w_keyval, w_out, w_gate_up, w_down, kv_cache, lengths, owner_rows
):
    docs, width = states.shape
    heads = w_query.shape[1]
    cache_len = kv_cache.shape[1]
    hidden = w_gate_up.shape[2]
    wq = w_query.reshape(width * heads, LANES)
    wkv = w_keyval.reshape(width, 2 * LANES)
    cache = kv_cache.reshape(cache_len, 2 * LANES)
    packed = 2 * heads
    wq_parts = 4

    half = LANES // 2
    freq = ROPE_BASE ** (-(np.arange(half, dtype=np.float64) * 2.0 / LANES))
    freq = jnp.asarray(np.concatenate([freq, freq]).astype(np.float32)[None, :])
    *qkv_parts, table, places = pl.pallas_call(
        functools.partial(qkv_kernel, tp),
        out_shape=[jax.ShapeDtypeStruct((packed, LANES), F32)] * tp
        + [
            jax.ShapeDtypeStruct((8, LANES), F32),
            jax.ShapeDtypeStruct((max(tp, 8), LANES), jnp.int32),
        ],
        in_specs=[hbm()] * 7,
        out_specs=[vmem()] * (tp + 2),
        scratch_shapes=[
            pltpu.SMEM((docs,), jnp.int32),
            pltpu.SMEM((docs,), jnp.int32),
            pltpu.VMEM((1, LANES), F32),
            pltpu.VMEM((docs, width), BF16),
            pltpu.VMEM((2, width), F32),
            pltpu.VMEM((wq_parts, width * heads // wq_parts, LANES), BF16),
            pltpu.VMEM((width, 2 * LANES), BF16),
            pltpu.VMEM((heads * 2 * docs, width * heads), BF16),
            pltpu.SemaphoreType.DMA((wq_parts + 1,)),
            pltpu.SemaphoreType.DMA((5,)),
        ],
        compiler_params=params(docs, 10),
        cost_estimate=cost(8),
        name="qkv",
    )(*(in_hbm(a) for a in (owner_rows, lengths, freq, states, norm_gains, wq, wkv)))
    w_gu = in_hbm(w_gate_up)
    bounds = np.cumsum([0] + [hidden // LANES * n // 28 for n in GU_SHARES]).tolist()
    shares = list(zip(bounds, bounds[1:]))
    fetched = []

    chunks = max(2 * width // COPY_ROWS, 1)

    def block_of(share):
        return pltpu.VMEM((2 * width, (share[1] - share[0]) * LANES), BF16)

    def fetch(share, token, *keep):
        return pl.pallas_call(
            functools.partial(fetch_kernel, share[0]),
            out_shape=block_of(share),
            in_specs=[hbm(), hbm()] + [vmem()] * len(keep),
            out_specs=vmem(),
            scratch_shapes=[pltpu.SemaphoreType.DMA((chunks,))],
            compiler_params=params(docs, 2),
            cost_estimate=cost(0.3 * (share[1] - share[0])),
            name="fetch",
        )(token, w_gu, *keep)

    fetched.append(fetch(shares[0], table, cache))
    qkv_parts = exchange(qkv_parts, "tp", tp)[::-1]
    head_out, new_kv, w_ready = pl.pallas_call(
        functools.partial(attend_kernel, tp, heads, 512, shares[1][0]),
        out_shape=[
            jax.ShapeDtypeStruct((heads, LANES), BF16),
            jax.ShapeDtypeStruct((1, 2 * LANES), BF16),
            block_of(shares[1]),
        ],
        in_specs=[vmem(), vmem(), hbm()] + [vmem()] * tp + [hbm()] * len(fetched),
        out_specs=[vmem(), hbm(), vmem()],
        scratch_shapes=[
            pltpu.VMEM((heads, cache_len), F32),
            pltpu.VMEM((1, 2 * LANES), BF16),
            pltpu.SemaphoreType.DMA((chunks,)),
            pltpu.SemaphoreType.DMA((1,)),
        ],
        compiler_params=params(docs, 6),
        cost_estimate=cost(8),
        name="attend",
    )(table, cache, w_gu, *qkv_parts, *fetched)
    fetched.append(w_ready)

    fetched.append(fetch(shares[2], head_out))
    head_parts = exchange([head_out] * tp, "tp", tp)
    out_part = pl.pallas_call(
        functools.partial(out_kernel, tp),
        out_shape=jax.ShapeDtypeStruct((docs, width), BF16),
        in_specs=[vmem()] * (tp + 2) + [hbm()],
        out_specs=vmem(),
        scratch_shapes=[pltpu.VMEM((max(docs, 8), heads * LANES), F32)],
        compiler_params=params(docs, 6),
        cost_estimate=cost(6),
        name="attn_project",
    )(places, w_out, *head_parts, fetched[-1])

    fetched.append(fetch(shares[3], out_part))
    out_parts = exchange([out_part] * kv, "kv", kv)
    attn_out, gu_part = pl.pallas_call(
        functools.partial(gate_up_kernel, kv, len(fetched), shares[4][0]),
        out_shape=[
            jax.ShapeDtypeStruct((docs, width), BF16),
            jax.ShapeDtypeStruct((2 * docs, hidden + LANES), BF16),
        ],
        in_specs=[vmem(), vmem(), hbm()] + [vmem()] * (len(fetched) + kv),
        out_specs=[hbm(), vmem()],
        scratch_shapes=[
            *(block_of(share) for share in shares[4:]),
            pltpu.VMEM((4 * docs, 2 * width), BF16),
            pltpu.VMEM((docs, width), BF16),
            pltpu.SemaphoreType.DMA((len(shares) - 4, chunks)),
            pltpu.SemaphoreType.DMA((1,)),
        ],
        compiler_params=params(docs, 19),
        cost_estimate=cost(10),
        name="gate_up",
    )(states, norm_gains, w_gu, *fetched, *out_parts)

    gu_parts = exchange([gu_part] * tp, "tp", tp)
    ffn_part = pl.pallas_call(
        functools.partial(down_kernel, tp),
        out_shape=jax.ShapeDtypeStruct((docs, width), BF16),
        in_specs=[vmem()] * (1 + tp),
        out_specs=vmem(),
        compiler_params=params(docs, 6),
        cost_estimate=cost(5),
        name="down",
    )(w_down, *gu_parts)
    ffn_parts = exchange([ffn_part] * kv, "kv", kv)
    ffn_out = tree_sum([part.astype(F32) for part in ffn_parts]).astype(BF16)
    return attn_out, ffn_out, new_kv.reshape(1, 1, 2 * LANES)


def solution(mesh):
    return jax.shard_map(
        functools.partial(per_device, mesh.shape["tp"], mesh.shape["kv"]),
        mesh=mesh,
        in_specs=(
            P("grp", "tp"),
            P(None, "tp"),
            P("tp", "kv", None),
            P("tp", "kv", None),
            P("kv", "tp"),
            P("tp", None, "kv"),
            P("kv", "tp"),
            P(("grp", "tp"), None, "kv", None),
            P("grp"),
            P("grp"),
        ),
        out_specs=(P("grp", "tp"), P("grp", "tp"), P(("grp", "tp"), "kv", None)),
        check_vma=False,
    )
```

```python
import functools
import math

import jax
import jax.numpy as jnp
import numpy as np
from jax import lax
from jax.experimental import pallas as pl
from jax.experimental.pallas import tpu as pltpu
from jax.sharding import PartitionSpec as P

D = 8192
EPS = 1e-05
ROPE_BASE = 500000.0
LANES = 128
MIB = 1 << 20
COPY_ROWS = 2048
DOWN_ROWS = 1024
GU_SHARES = (4, 6, 4, 2, 4, 4, 2, 2)
F32 = jnp.float32
BF16 = jnp.bfloat16
QUARTER = (1.5703125, 4.837512969970703125e-4, 7.549789948768648e-8)
SIN = (-1.9515295891e-4, 8.3321608736e-3, -1.6666654611e-1)
COS = (2.443315711809948e-5, -1.388731625493765e-3, 4.166664568298827e-2)


def vmem():
    return pl.BlockSpec(memory_space=pltpu.VMEM)


def hbm():
    return pl.BlockSpec(memory_space=pltpu.HBM)


def in_hbm(array):
    return pltpu.with_memory_space_constraint(array, pltpu.HBM)


def exchange(arrays, axis, size):
    return [arrays[0]] + [
        lax.ppermute(arrays[s], axis, [(i, i ^ s) for i in range(size)])
        for s in range(1, size)
    ]


def tree_sum(parts):
    while len(parts) > 1:
        parts = [a + b for a, b in zip(parts[::2], parts[1::2])]
    return parts[0]


def two_parts(scaled):
    high = scaled.astype(BF16).astype(F32)
    return high, scaled - high


def spread(rows16, out_ref, docs):
    width = rows16.shape[1]
    pick = one_hot_spread(2)
    row = lax.broadcasted_iota(jnp.int32, (4 * docs, 2 * LANES), 0)
    lane = lax.broadcasted_iota(jnp.int32, (4 * docs, 2 * LANES), 1)
    keep = (lax.shift_right_logical(row, docs.bit_length() - 1) & 1) == (lane & 1)
    chunks = width // LANES
    stacked = jnp.concatenate(
        [rows16[:, c * LANES : (c + 1) * LANES] for c in range(chunks)], axis=0
    )
    doubled = jnp.dot(stacked, pick, preferred_element_type=F32)
    for c in range(chunks):
        piece = doubled[c * 4 * docs : (c + 1) * 4 * docs]
        out_ref[:, 2 * c * LANES : 2 * (c + 1) * LANES] = jnp.where(keep, piece, 0.0).astype(BF16)


def start_all(copies):
    for i, copy in enumerate(copies):
        copy.start(priority=i % 2)


def matrix_of(w):
    return w if len(w.shape) == 2 else w.reshape(w.shape[0] * w.shape[1], w.shape[2])


def block_copies(matrix, first, buf, sems):
    rows, columns = buf.shape
    chunk = min(rows, COPY_ROWS)
    return [
        pltpu.make_async_copy(
            matrix.at[pl.ds(start, chunk), pl.ds(first * LANES, columns)],
            buf.at[pl.ds(start, chunk)],
            sems.at[start // chunk],
        )
        for start in range(0, rows, chunk)
    ]


def pick_doc(value, doc, docs):
    axis = value.ndim - 2
    row = lax.broadcasted_iota(jnp.int32, value.shape, axis)
    return jnp.sum(jnp.where(row & (docs - 1) == doc, value, 0.0), axis=axis)


def sine_cosine(angle):
    turns = jnp.floor(angle * (2.0 / math.pi) + 0.5)
    rest = ((angle - turns * QUARTER[0]) - turns * QUARTER[1]) - turns * QUARTER[2]
    square = rest * rest
    sine = rest + rest * square * ((SIN[0] * square + SIN[1]) * square + SIN[2])
    cosine = 1.0 - 0.5 * square + square * square * (
        (COS[0] * square + COS[1]) * square + COS[2]
    )
    quadrant = turns - 4.0 * jnp.floor(turns * 0.25)
    odd = (quadrant == 1.0) | (quadrant == 3.0)
    sine, cosine = jnp.where(odd, cosine, sine), jnp.where(odd, sine, cosine)
    return (
        jnp.where(quadrant >= 2.0, -sine, sine),
        jnp.where((quadrant == 1.0) | (quadrant == 2.0), -cosine, cosine),
    )


def rope_rows(length, frequency):
    sine, cosine = sine_cosine(length * frequency)
    lane = lax.broadcasted_iota(jnp.int32, (1, LANES), 1)
    return cosine, jnp.where(lane < LANES // 2, -sine, sine)


def one_hot_spread(fold):
    source = lax.broadcasted_iota(jnp.int32, (LANES, fold * LANES), 0)
    target = lax.broadcasted_iota(jnp.int32, (LANES, fold * LANES), 1)
    return (lax.shift_right_logical(target, fold.bit_length() - 1) == source).astype(F32).astype(BF16)


def spread_heads(rows, out_ref, heads):
    count, width = rows.shape
    chunks = width // LANES
    stacked = jnp.concatenate([rows[:, c * LANES : (c + 1) * LANES] for c in range(chunks)], axis=0)
    wide = jnp.dot(stacked.astype(BF16), one_hot_spread(heads), preferred_element_type=F32)
    columns = heads * LANES
    lane = lax.broadcasted_iota(jnp.int32, (count, columns), 1) & (heads - 1)
    for c in range(chunks):
        piece = wide[c * count : (c + 1) * count]
        for h in range(0, heads, 2):
            pair = [jnp.where(lane == h + i, piece, 0.0) for i in range(2)]
            out_ref[h * count : (h + 2) * count, c * columns : (c + 1) * columns] = (
                jnp.concatenate(pair, axis=0).astype(BF16)
            )


def qkv_kernel(tp, owner_hbm, lengths_hbm, frequency_hbm, states_hbm, gains_hbm, wq, wkv, *rest):
    outs = rest[:tp]
    table, places = rest[tp : tp + 2]
    owner, lengths, frequency, states, gains = rest[tp + 2 : tp + 7]
    wq_buf, wkv_buf, spread_buf, sems, small_sems = rest[tp + 7 :]
    docs, width = states.shape
    heads = wq.shape[0] // width
    parts = wq_buf.shape[0]
    rows = wq_buf.shape[1]
    small = [
        pltpu.make_async_copy(source, target, small_sems.at[i])
        for i, (source, target) in enumerate(
            [
                (states_hbm, states),
                (gains_hbm, gains),
                (owner_hbm, owner),
                (lengths_hbm, lengths),
                (frequency_hbm, frequency),
            ]
        )
    ]
    copies = [
        pltpu.make_async_copy(wq.at[pl.ds(c * rows, rows)], wq_buf.at[c], sems.at[c])
        for c in range(parts)
    ]
    kv_copy = pltpu.make_async_copy(wkv, wkv_buf, sems.at[parts])
    for copy in small:
        copy.start()
    start_all([kv_copy] + copies)
    for copy in small:
        copy.wait()
    me = lax.axis_index("tp")
    x = states[...].astype(F32)
    squares = jnp.broadcast_to(jnp.sum(x * x, axis=1, keepdims=True), (docs, LANES))
    both = jnp.concatenate(two_parts(x * gains[0:1, :]), axis=0)
    kv_copy.wait()
    kv_total = jnp.dot(both.astype(BF16), wkv_buf[...], preferred_element_type=F32)
    spread_heads(both, spread_buf, heads)
    length = lengths[owner[me]].astype(F32)
    cosine, sine = rope_rows(length, frequency[...])
    table[0:1, :] = cosine
    table[1:2, :] = sine
    table[2:3, :] = jnp.full((1, LANES), length, F32)
    table[3:, :] = jnp.zeros((table.shape[0] - 3, LANES), F32)
    for s in range(tp):
        places[s : s + 1, :] = jnp.full((1, LANES), owner[me ^ s], jnp.int32)
    total = jnp.zeros((heads * 2 * docs, LANES), F32)
    for c in range(parts):
        copies[c].wait()
        total = total + jnp.dot(
            spread_buf[:, c * rows : (c + 1) * rows], wq_buf[c], preferred_element_type=F32
        )
    total = total.reshape(heads, 2 * docs, LANES)
    for s in range(tp):
        doc = owner[me ^ s]
        out = outs[s]
        out[:heads, :] = pick_doc(total, doc, docs)
        kv_row = pick_doc(kv_total, doc, docs)[None]
        out[heads : heads + 1, :] = kv_row[:, :LANES]
        out[heads + 1 : heads + 2, :] = kv_row[:, LANES:]
        out[heads + 2 : heads + 3, :] = pick_doc(squares, doc, docs)[None]
        out[heads + 3 :, :] = jnp.zeros((out.shape[0] - heads - 3, LANES), F32)


def attend_kernel(tp, heads, rows, first, table, cache, w, *rest):
    parts = rest[:tp]
    heads_out, new_kv_out, w_ready, scores, new_kv, w_sems, out_sem = rest[-7:]
    w_copies = block_copies(matrix_of(w), first, w_ready, w_sems)
    start_all(w_copies)
    blocks = cache.shape[0] // rows
    sums = tree_sum([part[...] for part in parts])
    sums = sums * lax.rsqrt(sums[heads + 2 : heads + 3, :] / D + EPS)
    rotated = sums * table[0:1, :] + pltpu.roll(sums, LANES // 2, 1) * table[1:2, :]
    query = rotated[:heads].astype(BF16)
    key = rotated[heads : heads + 1].astype(BF16)
    value = sums[heads + 1 : heads + 2].astype(BF16)
    new_kv[:, :LANES] = key
    new_kv[:, LANES:] = value
    out_copy = pltpu.make_async_copy(new_kv, new_kv_out, out_sem.at[0])
    out_copy.start()
    key = key.astype(F32)
    value = value.astype(F32)
    scale = LANES ** (-0.5)
    own = jnp.sum(query.astype(F32) * key, axis=1, keepdims=True) * scale
    column = lax.broadcasted_iota(jnp.int32, (heads, LANES), 1).astype(F32)
    length = table[2:3, :]
    tops = jnp.full((heads, LANES), -jnp.inf, F32)
    for b in range(blocks):
        block = lax.dot_general(
            query,
            cache[b * rows : (b + 1) * rows, :LANES],
            (((1,), (1,)), ((), ())),
            preferred_element_type=F32,
        )
        for start in range(0, rows, LANES):
            at = b * rows + start
            piece = block[:, start : start + LANES] * scale
            piece = jnp.where(column < length - at, piece, -jnp.inf)
            tops = jnp.maximum(tops, piece)
            scores[:, at : at + LANES] = piece
    top = jnp.maximum(jnp.max(tops, axis=1, keepdims=True), own)
    own = jnp.exp(own - top)
    sums_by_lane = jnp.zeros((heads, LANES), F32)
    acc = own.astype(BF16).astype(F32) * value
    for b in range(blocks):
        weights = jnp.exp(scores[:, b * rows : (b + 1) * rows] - top)
        for start in range(0, rows, LANES):
            sums_by_lane = sums_by_lane + weights[:, start : start + LANES]
        acc = acc + jnp.dot(
            weights.astype(BF16),
            cache[b * rows : (b + 1) * rows, LANES:],
            preferred_element_type=F32,
        )
    total = own + jnp.sum(sums_by_lane, axis=1, keepdims=True)
    heads_out[...] = (acc / total).astype(BF16)
    for copy in w_copies:
        copy.wait()
    out_copy.wait()


def out_kernel(tp, places, w_out, *rest):
    parts = rest[:tp]
    out, left = rest[-2:]
    docs = out.shape[0]
    row = lax.broadcasted_iota(jnp.int32, (left.shape[0], LANES), 0)
    own = [parts[s][...].astype(F32) for s in range(tp)]
    for h in range(own[0].shape[0]):
        piece = jnp.zeros((left.shape[0], LANES), F32)
        for s in range(tp):
            piece = jnp.where(row == places[s : s + 1, :], own[s][h : h + 1, :], piece)
        left[:, h * LANES : (h + 1) * LANES] = piece
    terms = jnp.dot(left[...].astype(BF16), w_out[...], preferred_element_type=F32)
    out[...] = terms[:docs].astype(BF16)


def fetch_kernel(first, token, w, *rest):
    out, sems = rest[-2:]
    copies = block_copies(matrix_of(w), first, out, sems)
    start_all(copies)
    for copy in copies:
        copy.wait()


def gate_up_kernel(kv, groups, first, states, gains, w, *rest):
    ready, parts = rest[:groups], rest[groups : groups + kv]
    attn_out, partial_out, *blocks, spread_buf, attn_buf, w_sems, out_sem = rest[groups + kv :]
    docs, width = states.shape
    hidden = w.shape[2]
    w_matrix = matrix_of(w)
    copies = []
    for i, block in enumerate(blocks):
        copies.append(block_copies(w_matrix, first, block, w_sems.at[i]))
        first += block.shape[1] // LANES
        start_all(copies[-1])
    attn = tree_sum([part[...].astype(F32) for part in parts]).astype(BF16)
    attn_buf[...] = attn
    out_copy = pltpu.make_async_copy(attn_buf, attn_out, out_sem.at[0])
    out_copy.start()
    resid = (states[...].astype(F32) + attn.astype(F32)).astype(BF16).astype(F32)
    squares = jnp.sum(resid * resid, axis=1, keepdims=True)
    high, low = two_parts(resid * gains[1:2, :])
    spread(jnp.concatenate([high, high, low, low], axis=0).astype(BF16), spread_buf, docs)

    lane = lax.broadcasted_iota(jnp.int32, (docs, LANES), 1)
    first = squares.astype(BF16).astype(F32)
    second = (squares - first).astype(BF16).astype(F32)
    third = squares - first - second
    terms = jnp.where(lane == 0, first, jnp.where(lane == 1, second, jnp.where(lane == 2, third, 0.0)))
    partial_out[:, hidden:] = jnp.concatenate([terms, terms], axis=0).astype(BF16)
    at = 0
    for i, block in enumerate([*ready, *blocks]):
        if i >= groups:
            for copy in copies[i - groups]:
                copy.wait()
        product = jnp.dot(spread_buf[...], block[...], preferred_element_type=F32)
        columns = slice(at, at + block.shape[1])
        partial_out[:, columns] = (product[: 2 * docs] + product[2 * docs :]).astype(BF16)
        at += block.shape[1]
    out_copy.wait()


def down_kernel(tp, w_down, *rest):
    parts, out = rest[:tp], rest[tp]
    docs, width = out.shape
    hidden = w_down.shape[0]

    def summed(start, size):
        return tree_sum([part[:, start : start + size].astype(F32) for part in parts])

    squares = jnp.sum(summed(hidden, LANES)[:docs], axis=1, keepdims=True)
    inverse = lax.rsqrt(squares / D + EPS)
    total = jnp.zeros((docs, width), F32)
    for start in range(0, hidden, DOWN_ROWS):
        size = min(DOWN_ROWS, hidden - start)
        both = summed(start, size)
        gate = both[:docs] * inverse
        up = both[docs:] * inverse
        act = (gate / (1.0 + jnp.exp(-gate)) * up).astype(BF16)
        total = total + jnp.dot(
            act, w_down[start : start + size, :], preferred_element_type=F32
        )
    out[...] = total.astype(BF16)


def cost(micros):
    return pl.CostEstimate(flops=0, bytes_accessed=int(micros * 3.69e6), transcendentals=0)


def params(docs, mib):
    return pltpu.CompilerParams(vmem_limit_bytes=(mib if docs <= 8 else mib + 24) * MIB)


def per_device(
    tp, kv,
    states, norm_gains, w_query, w_keyval, w_out, w_gate_up, w_down, kv_cache, lengths, owner_rows
):
    docs, width = states.shape
    heads = w_query.shape[1]
    cache_len = kv_cache.shape[1]
    hidden = w_gate_up.shape[2]
    wq = w_query.reshape(width * heads, LANES)
    wkv = w_keyval.reshape(width, 2 * LANES)
    cache = kv_cache.reshape(cache_len, 2 * LANES)
    packed = 2 * heads
    wq_parts = 4

    half = LANES // 2
    freq = ROPE_BASE ** (-(np.arange(half, dtype=np.float64) * 2.0 / LANES))
    freq = jnp.asarray(np.concatenate([freq, freq]).astype(np.float32)[None, :])
    *qkv_parts, table, places = pl.pallas_call(
        functools.partial(qkv_kernel, tp),
        out_shape=[jax.ShapeDtypeStruct((packed, LANES), F32)] * tp
        + [
            jax.ShapeDtypeStruct((8, LANES), F32),
            jax.ShapeDtypeStruct((max(tp, 8), LANES), jnp.int32),
        ],
        in_specs=[hbm()] * 7,
        out_specs=[vmem()] * (tp + 2),
        scratch_shapes=[
            pltpu.SMEM((docs,), jnp.int32),
            pltpu.SMEM((docs,), jnp.int32),
            pltpu.VMEM((1, LANES), F32),
            pltpu.VMEM((docs, width), BF16),
            pltpu.VMEM((2, width), F32),
            pltpu.VMEM((wq_parts, width * heads // wq_parts, LANES), BF16),
            pltpu.VMEM((width, 2 * LANES), BF16),
            pltpu.VMEM((heads * 2 * docs, width * heads), BF16),
            pltpu.SemaphoreType.DMA((wq_parts + 1,)),
            pltpu.SemaphoreType.DMA((5,)),
        ],
        compiler_params=params(docs, 10),
        cost_estimate=cost(8),
        name="qkv",
    )(*(in_hbm(a) for a in (owner_rows, lengths, freq, states, norm_gains, wq, wkv)))
    w_gu = in_hbm(w_gate_up)
    bounds = np.cumsum([0] + [hidden // LANES * n // 28 for n in GU_SHARES]).tolist()
    shares = list(zip(bounds, bounds[1:]))
    fetched = []

    chunks = max(2 * width // COPY_ROWS, 1)

    def block_of(share):
        return pltpu.VMEM((2 * width, (share[1] - share[0]) * LANES), BF16)

    def fetch(share, token, *keep):
        return pl.pallas_call(
            functools.partial(fetch_kernel, share[0]),
            out_shape=block_of(share),
            in_specs=[hbm(), hbm()] + [vmem()] * len(keep),
            out_specs=vmem(),
            scratch_shapes=[pltpu.SemaphoreType.DMA((chunks,))],
            compiler_params=params(docs, 2),
            cost_estimate=cost(0.3 * (share[1] - share[0])),
            name="fetch",
        )(token, w_gu, *keep)

    fetched.append(fetch(shares[0], table, cache))
    qkv_parts = exchange(qkv_parts, "tp", tp)[::-1]
    head_out, new_kv, w_ready = pl.pallas_call(
        functools.partial(attend_kernel, tp, heads, 512, shares[1][0]),
        out_shape=[
            jax.ShapeDtypeStruct((heads, LANES), BF16),
            jax.ShapeDtypeStruct((1, 2 * LANES), BF16),
            block_of(shares[1]),
        ],
        in_specs=[vmem(), vmem(), hbm()] + [vmem()] * tp + [hbm()] * len(fetched),
        out_specs=[vmem(), hbm(), vmem()],
        scratch_shapes=[
            pltpu.VMEM((heads, cache_len), F32),
            pltpu.VMEM((1, 2 * LANES), BF16),
            pltpu.SemaphoreType.DMA((chunks,)),
            pltpu.SemaphoreType.DMA((1,)),
        ],
        compiler_params=params(docs, 6),
        cost_estimate=cost(8),
        name="attend",
    )(table, cache, w_gu, *qkv_parts, *fetched)
    fetched.append(w_ready)

    fetched.append(fetch(shares[2], head_out))
    head_parts = exchange([head_out] * tp, "tp", tp)
    out_part = pl.pallas_call(
        functools.partial(out_kernel, tp),
        out_shape=jax.ShapeDtypeStruct((docs, width), BF16),
        in_specs=[vmem()] * (tp + 2) + [hbm()],
        out_specs=vmem(),
        scratch_shapes=[pltpu.VMEM((max(docs, 8), heads * LANES), F32)],
        compiler_params=params(docs, 6),
        cost_estimate=cost(6),
        name="attn_project",
    )(places, w_out, *head_parts, fetched[-1])

    fetched.append(fetch(shares[3], out_part))
    out_parts = exchange([out_part] * kv, "kv", kv)
    attn_out, gu_part = pl.pallas_call(
        functools.partial(gate_up_kernel, kv, len(fetched), shares[4][0]),
        out_shape=[
            jax.ShapeDtypeStruct((docs, width), BF16),
            jax.ShapeDtypeStruct((2 * docs, hidden + LANES), BF16),
        ],
        in_specs=[vmem(), vmem(), hbm()] + [vmem()] * (len(fetched) + kv),
        out_specs=[hbm(), vmem()],
        scratch_shapes=[
            *(block_of(share) for share in shares[4:]),
            pltpu.VMEM((4 * docs, 2 * width), BF16),
            pltpu.VMEM((docs, width), BF16),
            pltpu.SemaphoreType.DMA((len(shares) - 4, chunks)),
            pltpu.SemaphoreType.DMA((1,)),
        ],
        compiler_params=params(docs, 19),
        cost_estimate=cost(10),
        name="gate_up",
    )(states, norm_gains, w_gu, *fetched, *out_parts)

    gu_parts = exchange([gu_part] * tp, "tp", tp)
    ffn_part = pl.pallas_call(
        functools.partial(down_kernel, tp),
        out_shape=jax.ShapeDtypeStruct((docs, width), BF16),
        in_specs=[vmem()] * (1 + tp),
        out_specs=vmem(),
        compiler_params=params(docs, 6),
        cost_estimate=cost(5),
        name="down",
    )(w_down, *gu_parts)
    ffn_parts = exchange([ffn_part] * kv, "kv", kv)
    ffn_out = tree_sum([part.astype(F32) for part in ffn_parts]).astype(BF16)
    return attn_out, ffn_out, new_kv.reshape(1, 1, 2 * LANES)


def solution(mesh):
    return jax.shard_map(
        functools.partial(per_device, mesh.shape["tp"], mesh.shape["kv"]),
        mesh=mesh,
        in_specs=(
            P("grp", "tp"),
            P(None, "tp"),
            P("tp", "kv", None),
            P("tp", "kv", None),
            P("kv", "tp"),
            P("tp", None, "kv"),
            P("kv", "tp"),
            P(("grp", "tp"), None, "kv", None),
            P("grp"),
            P("grp"),
        ),
        out_specs=(P("grp", "tp"), P("grp", "tp"), P(("grp", "tp"), "kv", None)),
        check_vma=False,
    )
```

```python
import functools
import math

import jax
import jax.numpy as jnp
import numpy as np
from jax import lax
from jax.experimental import pallas as pl
from jax.experimental.pallas import tpu as pltpu
from jax.sharding import PartitionSpec as P

D = 8192
EPS = 1e-05
ROPE_BASE = 500000.0
LANES = 128
MIB = 1 << 20
COPY_ROWS = 2048
DOWN_ROWS = 1024
GU_SHARES = (4, 6, 4, 3, 4, 4, 3)
F32 = jnp.float32
BF16 = jnp.bfloat16
QUARTER = (1.5703125, 4.837512969970703125e-4, 7.549789948768648e-8)
SIN = (-1.9515295891e-4, 8.3321608736e-3, -1.6666654611e-1)
COS = (2.443315711809948e-5, -1.388731625493765e-3, 4.166664568298827e-2)


def vmem():
    return pl.BlockSpec(memory_space=pltpu.VMEM)


def hbm():
    return pl.BlockSpec(memory_space=pltpu.HBM)


def in_hbm(array):
    return pltpu.with_memory_space_constraint(array, pltpu.HBM)


def exchange(arrays, axis, size):
    return [arrays[0]] + [
        lax.ppermute(arrays[s], axis, [(i, i ^ s) for i in range(size)])
        for s in range(1, size)
    ]


def tree_sum(parts):
    while len(parts) > 1:
        parts = [a + b for a, b in zip(parts[::2], parts[1::2])]
    return parts[0]


def two_parts(scaled):
    high = scaled.astype(BF16).astype(F32)
    return high, scaled - high


def spread(rows16, out_ref, docs):
    width = rows16.shape[1]
    pick = one_hot_spread(2)
    row = lax.broadcasted_iota(jnp.int32, (4 * docs, 2 * LANES), 0)
    lane = lax.broadcasted_iota(jnp.int32, (4 * docs, 2 * LANES), 1)
    keep = (lax.shift_right_logical(row, docs.bit_length() - 1) & 1) == (lane & 1)
    chunks = width // LANES
    stacked = jnp.concatenate(
        [rows16[:, c * LANES : (c + 1) * LANES] for c in range(chunks)], axis=0
    )
    doubled = jnp.dot(stacked, pick, preferred_element_type=F32)
    for c in range(chunks):
        piece = doubled[c * 4 * docs : (c + 1) * 4 * docs]
        out_ref[:, 2 * c * LANES : 2 * (c + 1) * LANES] = jnp.where(keep, piece, 0.0).astype(BF16)


def start_all(copies):
    for copy in copies:
        copy.start(priority=1)


def matrix_of(w):
    return w if len(w.shape) == 2 else w.reshape(w.shape[0] * w.shape[1], w.shape[2])


def block_copies(matrix, first, buf, sems):
    rows, columns = buf.shape
    chunk = min(rows, COPY_ROWS)
    return [
        pltpu.make_async_copy(
            matrix.at[pl.ds(start, chunk), pl.ds(first * LANES, columns)],
            buf.at[pl.ds(start, chunk)],
            sems.at[start // chunk],
        )
        for start in range(0, rows, chunk)
    ]


def pick_doc(value, doc, docs):
    axis = value.ndim - 2
    row = lax.broadcasted_iota(jnp.int32, value.shape, axis)
    return jnp.sum(jnp.where(row & (docs - 1) == doc, value, 0.0), axis=axis)


def sine_cosine(angle):
    turns = jnp.floor(angle * (2.0 / math.pi) + 0.5)
    rest = ((angle - turns * QUARTER[0]) - turns * QUARTER[1]) - turns * QUARTER[2]
    square = rest * rest
    sine = rest + rest * square * ((SIN[0] * square + SIN[1]) * square + SIN[2])
    cosine = 1.0 - 0.5 * square + square * square * (
        (COS[0] * square + COS[1]) * square + COS[2]
    )
    quadrant = turns - 4.0 * jnp.floor(turns * 0.25)
    odd = (quadrant == 1.0) | (quadrant == 3.0)
    sine, cosine = jnp.where(odd, cosine, sine), jnp.where(odd, sine, cosine)
    return (
        jnp.where(quadrant >= 2.0, -sine, sine),
        jnp.where((quadrant == 1.0) | (quadrant == 2.0), -cosine, cosine),
    )


def rope_rows(length, frequency):
    sine, cosine = sine_cosine(length * frequency)
    lane = lax.broadcasted_iota(jnp.int32, (1, LANES), 1)
    return cosine, jnp.where(lane < LANES // 2, -sine, sine)


def one_hot_spread(fold):
    source = lax.broadcasted_iota(jnp.int32, (LANES, fold * LANES), 0)
    target = lax.broadcasted_iota(jnp.int32, (LANES, fold * LANES), 1)
    return (lax.shift_right_logical(target, fold.bit_length() - 1) == source).astype(F32).astype(BF16)


def spread_heads(rows, out_ref, heads):
    count, width = rows.shape
    chunks = width // LANES
    stacked = jnp.concatenate([rows[:, c * LANES : (c + 1) * LANES] for c in range(chunks)], axis=0)
    wide = jnp.dot(stacked.astype(BF16), one_hot_spread(heads), preferred_element_type=F32)
    columns = heads * LANES
    lane = lax.broadcasted_iota(jnp.int32, (count, columns), 1) & (heads - 1)
    for c in range(chunks):
        piece = wide[c * count : (c + 1) * count]
        for h in range(0, heads, 2):
            pair = [jnp.where(lane == h + i, piece, 0.0) for i in range(2)]
            out_ref[h * count : (h + 2) * count, c * columns : (c + 1) * columns] = (
                jnp.concatenate(pair, axis=0).astype(BF16)
            )


def qkv_kernel(tp, owner_hbm, lengths_hbm, frequency_hbm, states_hbm, gains_hbm, wq, wkv, *rest):
    outs = rest[:tp]
    table, places = rest[tp : tp + 2]
    owner, lengths, frequency, states, gains = rest[tp + 2 : tp + 7]
    wq_buf, wkv_buf, spread_buf, sems, small_sems = rest[tp + 7 :]
    docs, width = states.shape
    heads = wq.shape[0] // width
    parts = wq_buf.shape[0]
    rows = wq_buf.shape[1]
    small = [
        pltpu.make_async_copy(source, target, small_sems.at[i])
        for i, (source, target) in enumerate(
            [
                (states_hbm, states),
                (gains_hbm, gains),
                (owner_hbm, owner),
                (lengths_hbm, lengths),
                (frequency_hbm, frequency),
            ]
        )
    ]
    copies = [
        pltpu.make_async_copy(wq.at[pl.ds(c * rows, rows)], wq_buf.at[c], sems.at[c])
        for c in range(parts)
    ]
    kv_copy = pltpu.make_async_copy(wkv, wkv_buf, sems.at[parts])
    for copy in small:
        copy.start()
    start_all([kv_copy] + copies)
    for copy in small:
        copy.wait()
    me = lax.axis_index("tp")
    x = states[...].astype(F32)
    squares = jnp.broadcast_to(jnp.sum(x * x, axis=1, keepdims=True), (docs, LANES))
    both = jnp.concatenate(two_parts(x * gains[0:1, :]), axis=0)
    kv_copy.wait()
    kv_total = jnp.dot(both.astype(BF16), wkv_buf[...], preferred_element_type=F32)
    spread_heads(both, spread_buf, heads)
    length = lengths[owner[me]].astype(F32)
    cosine, sine = rope_rows(length, frequency[...])
    table[0:1, :] = cosine
    table[1:2, :] = sine
    table[2:3, :] = jnp.full((1, LANES), length, F32)
    table[3:, :] = jnp.zeros((table.shape[0] - 3, LANES), F32)
    for s in range(tp):
        places[s : s + 1, :] = jnp.full((1, LANES), owner[me ^ s], jnp.int32)
    total = jnp.zeros((heads * 2 * docs, LANES), F32)
    for c in range(parts):
        copies[c].wait()
        total = total + jnp.dot(
            spread_buf[:, c * rows : (c + 1) * rows], wq_buf[c], preferred_element_type=F32
        )
    total = total.reshape(heads, 2 * docs, LANES)
    for s in range(tp):
        doc = owner[me ^ s]
        out = outs[s]
        out[:heads, :] = pick_doc(total, doc, docs)
        kv_row = pick_doc(kv_total, doc, docs)[None]
        out[heads : heads + 1, :] = kv_row[:, :LANES]
        out[heads + 1 : heads + 2, :] = kv_row[:, LANES:]
        out[heads + 2 : heads + 3, :] = pick_doc(squares, doc, docs)[None]
        out[heads + 3 :, :] = jnp.zeros((out.shape[0] - heads - 3, LANES), F32)


def attend_kernel(tp, heads, rows, first, table, cache, w, *rest):
    parts = rest[:tp]
    heads_out, new_kv_out, w_ready, scores, new_kv, w_sems, out_sem = rest[-7:]
    w_copies = block_copies(matrix_of(w), first, w_ready, w_sems)
    start_all(w_copies)
    blocks = cache.shape[0] // rows
    sums = tree_sum([part[...] for part in parts])
    sums = sums * lax.rsqrt(sums[heads + 2 : heads + 3, :] / D + EPS)
    rotated = sums * table[0:1, :] + pltpu.roll(sums, LANES // 2, 1) * table[1:2, :]
    query = rotated[:heads].astype(BF16)
    key = rotated[heads : heads + 1].astype(BF16)
    value = sums[heads + 1 : heads + 2].astype(BF16)
    new_kv[:, :LANES] = key
    new_kv[:, LANES:] = value
    out_copy = pltpu.make_async_copy(new_kv, new_kv_out, out_sem.at[0])
    out_copy.start()
    key = key.astype(F32)
    value = value.astype(F32)
    scale = LANES ** (-0.5)
    own = jnp.sum(query.astype(F32) * key, axis=1, keepdims=True) * scale
    column = lax.broadcasted_iota(jnp.int32, (heads, LANES), 1).astype(F32)
    length = table[2:3, :]
    tops = jnp.full((heads, LANES), -jnp.inf, F32)
    for b in range(blocks):
        block = lax.dot_general(
            query,
            cache[b * rows : (b + 1) * rows, :LANES],
            (((1,), (1,)), ((), ())),
            preferred_element_type=F32,
        )
        for start in range(0, rows, LANES):
            at = b * rows + start
            piece = block[:, start : start + LANES] * scale
            piece = jnp.where(column < length - at, piece, -jnp.inf)
            tops = jnp.maximum(tops, piece)
            scores[:, at : at + LANES] = piece
    top = jnp.maximum(jnp.max(tops, axis=1, keepdims=True), own)
    own = jnp.exp(own - top)
    sums_by_lane = jnp.zeros((heads, LANES), F32)
    acc = own.astype(BF16).astype(F32) * value
    for b in range(blocks):
        weights = jnp.exp(scores[:, b * rows : (b + 1) * rows] - top)
        for start in range(0, rows, LANES):
            sums_by_lane = sums_by_lane + weights[:, start : start + LANES]
        acc = acc + jnp.dot(
            weights.astype(BF16),
            cache[b * rows : (b + 1) * rows, LANES:],
            preferred_element_type=F32,
        )
    total = own + jnp.sum(sums_by_lane, axis=1, keepdims=True)
    heads_out[...] = (acc / total).astype(BF16)
    for copy in w_copies:
        copy.wait()
    out_copy.wait()


def out_kernel(tp, places, w_out, *rest):
    parts = rest[:tp]
    out, left = rest[-2:]
    docs = out.shape[0]
    row = lax.broadcasted_iota(jnp.int32, (left.shape[0], LANES), 0)
    own = [parts[s][...].astype(F32) for s in range(tp)]
    for h in range(own[0].shape[0]):
        piece = jnp.zeros((left.shape[0], LANES), F32)
        for s in range(tp):
            piece = jnp.where(row == places[s : s + 1, :], own[s][h : h + 1, :], piece)
        left[:, h * LANES : (h + 1) * LANES] = piece
    terms = jnp.dot(left[...].astype(BF16), w_out[...], preferred_element_type=F32)
    out[...] = terms[:docs].astype(BF16)


def fetch_kernel(first, token, w, *rest):
    out, sems = rest[-2:]
    copies = block_copies(matrix_of(w), first, out, sems)
    start_all(copies)
    for copy in copies:
        copy.wait()


def gate_up_kernel(kv, groups, first, states, gains, w, *rest):
    ready, parts = rest[:groups], rest[groups : groups + kv]
    attn_out, partial_out, *blocks, spread_buf, attn_buf, w_sems, out_sem = rest[groups + kv :]
    docs, width = states.shape
    hidden = w.shape[2]
    w_matrix = matrix_of(w)
    copies = []
    for i, block in enumerate(blocks):
        copies.append(block_copies(w_matrix, first, block, w_sems.at[i]))
        first += block.shape[1] // LANES
        start_all(copies[-1])
    attn = tree_sum([part[...].astype(F32) for part in parts]).astype(BF16)
    attn_buf[...] = attn
    out_copy = pltpu.make_async_copy(attn_buf, attn_out, out_sem.at[0])
    out_copy.start()
    resid = (states[...].astype(F32) + attn.astype(F32)).astype(BF16).astype(F32)
    squares = jnp.sum(resid * resid, axis=1, keepdims=True)
    high, low = two_parts(resid * gains[1:2, :])
    spread(jnp.concatenate([high, high, low, low], axis=0).astype(BF16), spread_buf, docs)

    lane = lax.broadcasted_iota(jnp.int32, (docs, LANES), 1)
    first = squares.astype(BF16).astype(F32)
    second = (squares - first).astype(BF16).astype(F32)
    third = squares - first - second
    terms = jnp.where(lane == 0, first, jnp.where(lane == 1, second, jnp.where(lane == 2, third, 0.0)))
    partial_out[:, hidden:] = jnp.concatenate([terms, terms], axis=0).astype(BF16)
    at = 0
    for i, block in enumerate([*ready, *blocks]):
        if i >= groups:
            for copy in copies[i - groups]:
                copy.wait()
        product = jnp.dot(spread_buf[...], block[...], preferred_element_type=F32)
        columns = slice(at, at + block.shape[1])
        partial_out[:, columns] = (product[: 2 * docs] + product[2 * docs :]).astype(BF16)
        at += block.shape[1]
    out_copy.wait()


def down_kernel(tp, w_down, *rest):
    parts, out = rest[:tp], rest[tp]
    docs, width = out.shape
    hidden = w_down.shape[0]

    def summed(start, size):
        return tree_sum([part[:, start : start + size].astype(F32) for part in parts])

    squares = jnp.sum(summed(hidden, LANES)[:docs], axis=1, keepdims=True)
    inverse = lax.rsqrt(squares / D + EPS)
    total = jnp.zeros((docs, width), F32)
    for start in range(0, hidden, DOWN_ROWS):
        size = min(DOWN_ROWS, hidden - start)
        both = summed(start, size)
        gate = both[:docs] * inverse
        up = both[docs:] * inverse
        act = (gate / (1.0 + jnp.exp(-gate)) * up).astype(BF16)
        total = total + jnp.dot(
            act, w_down[start : start + size, :], preferred_element_type=F32
        )
    out[...] = total.astype(BF16)


def cost(micros):
    return pl.CostEstimate(flops=0, bytes_accessed=int(micros * 3.69e6), transcendentals=0)


def params(docs, mib):
    return pltpu.CompilerParams(vmem_limit_bytes=(mib if docs <= 8 else mib + 24) * MIB)


def per_device(
    tp, kv,
    states, norm_gains, w_query, w_keyval, w_out, w_gate_up, w_down, kv_cache, lengths, owner_rows
):
    docs, width = states.shape
    heads = w_query.shape[1]
    cache_len = kv_cache.shape[1]
    hidden = w_gate_up.shape[2]
    wq = w_query.reshape(width * heads, LANES)
    wkv = w_keyval.reshape(width, 2 * LANES)
    cache = kv_cache.reshape(cache_len, 2 * LANES)
    packed = 2 * heads
    wq_parts = 4

    half = LANES // 2
    freq = ROPE_BASE ** (-(np.arange(half, dtype=np.float64) * 2.0 / LANES))
    freq = jnp.asarray(np.concatenate([freq, freq]).astype(np.float32)[None, :])
    *qkv_parts, table, places = pl.pallas_call(
        functools.partial(qkv_kernel, tp),
        out_shape=[jax.ShapeDtypeStruct((packed, LANES), F32)] * tp
        + [
            jax.ShapeDtypeStruct((8, LANES), F32),
            jax.ShapeDtypeStruct((max(tp, 8), LANES), jnp.int32),
        ],
        in_specs=[hbm()] * 7,
        out_specs=[vmem()] * (tp + 2),
        scratch_shapes=[
            pltpu.SMEM((docs,), jnp.int32),
            pltpu.SMEM((docs,), jnp.int32),
            pltpu.VMEM((1, LANES), F32),
            pltpu.VMEM((docs, width), BF16),
            pltpu.VMEM((2, width), F32),
            pltpu.VMEM((wq_parts, width * heads // wq_parts, LANES), BF16),
            pltpu.VMEM((width, 2 * LANES), BF16),
            pltpu.VMEM((heads * 2 * docs, width * heads), BF16),
            pltpu.SemaphoreType.DMA((wq_parts + 1,)),
            pltpu.SemaphoreType.DMA((5,)),
        ],
        compiler_params=params(docs, 10),
        cost_estimate=cost(8),
        name="qkv",
    )(*(in_hbm(a) for a in (owner_rows, lengths, freq, states, norm_gains, wq, wkv)))
    w_gu = in_hbm(w_gate_up)
    bounds = np.cumsum([0] + [hidden // LANES * n // 28 for n in GU_SHARES]).tolist()
    shares = list(zip(bounds, bounds[1:]))
    fetched = []

    chunks = max(2 * width // COPY_ROWS, 1)

    def block_of(share):
        return pltpu.VMEM((2 * width, (share[1] - share[0]) * LANES), BF16)

    def fetch(share, token, *keep):
        return pl.pallas_call(
            functools.partial(fetch_kernel, share[0]),
            out_shape=block_of(share),
            in_specs=[hbm(), hbm()] + [vmem()] * len(keep),
            out_specs=vmem(),
            scratch_shapes=[pltpu.SemaphoreType.DMA((chunks,))],
            compiler_params=params(docs, 2),
            cost_estimate=cost(0.3 * (share[1] - share[0])),
            name="fetch",
        )(token, w_gu, *keep)

    fetched.append(fetch(shares[0], table, cache))
    qkv_parts = exchange(qkv_parts, "tp", tp)[::-1]
    head_out, new_kv, w_ready = pl.pallas_call(
        functools.partial(attend_kernel, tp, heads, 512, shares[1][0]),
        out_shape=[
            jax.ShapeDtypeStruct((heads, LANES), BF16),
            jax.ShapeDtypeStruct((1, 2 * LANES), BF16),
            block_of(shares[1]),
        ],
        in_specs=[vmem(), vmem(), hbm()] + [vmem()] * tp + [hbm()] * len(fetched),
        out_specs=[vmem(), hbm(), vmem()],
        scratch_shapes=[
            pltpu.VMEM((heads, cache_len), F32),
            pltpu.VMEM((1, 2 * LANES), BF16),
            pltpu.SemaphoreType.DMA((chunks,)),
            pltpu.SemaphoreType.DMA((1,)),
        ],
        compiler_params=params(docs, 6),
        cost_estimate=cost(8),
        name="attend",
    )(table, cache, w_gu, *qkv_parts, *fetched)
    fetched.append(w_ready)

    fetched.append(fetch(shares[2], head_out))
    head_parts = exchange([head_out] * tp, "tp", tp)
    out_part = pl.pallas_call(
        functools.partial(out_kernel, tp),
        out_shape=jax.ShapeDtypeStruct((docs, width), BF16),
        in_specs=[vmem()] * (tp + 2) + [hbm()],
        out_specs=vmem(),
        scratch_shapes=[pltpu.VMEM((max(docs, 8), heads * LANES), F32)],
        compiler_params=params(docs, 6),
        cost_estimate=cost(6),
        name="attn_project",
    )(places, w_out, *head_parts, fetched[-1])

    fetched.append(fetch(shares[3], out_part))
    out_parts = exchange([out_part] * kv, "kv", kv)
    attn_out, gu_part = pl.pallas_call(
        functools.partial(gate_up_kernel, kv, len(fetched), shares[4][0]),
        out_shape=[
            jax.ShapeDtypeStruct((docs, width), BF16),
            jax.ShapeDtypeStruct((2 * docs, hidden + LANES), BF16),
        ],
        in_specs=[vmem(), vmem(), hbm()] + [vmem()] * (len(fetched) + kv),
        out_specs=[hbm(), vmem()],
        scratch_shapes=[
            *(block_of(share) for share in shares[4:]),
            pltpu.VMEM((4 * docs, 2 * width), BF16),
            pltpu.VMEM((docs, width), BF16),
            pltpu.SemaphoreType.DMA((len(shares) - 4, chunks)),
            pltpu.SemaphoreType.DMA((1,)),
        ],
        compiler_params=params(docs, 19),
        cost_estimate=cost(10),
        name="gate_up",
    )(states, norm_gains, w_gu, *fetched, *out_parts)

    gu_parts = exchange([gu_part] * tp, "tp", tp)
    ffn_part = pl.pallas_call(
        functools.partial(down_kernel, tp),
        out_shape=jax.ShapeDtypeStruct((docs, width), BF16),
        in_specs=[vmem()] * (1 + tp),
        out_specs=vmem(),
        compiler_params=params(docs, 6),
        cost_estimate=cost(5),
        name="down",
    )(w_down, *gu_parts)
    ffn_parts = exchange([ffn_part] * kv, "kv", kv)
    ffn_out = tree_sum([part.astype(F32) for part in ffn_parts]).astype(BF16)
    return attn_out, ffn_out, new_kv.reshape(1, 1, 2 * LANES)


def solution(mesh):
    return jax.shard_map(
        functools.partial(per_device, mesh.shape["tp"], mesh.shape["kv"]),
        mesh=mesh,
        in_specs=(
            P("grp", "tp"),
            P(None, "tp"),
            P("tp", "kv", None),
            P("tp", "kv", None),
            P("kv", "tp"),
            P("tp", None, "kv"),
            P("kv", "tp"),
            P(("grp", "tp"), None, "kv", None),
            P("grp"),
            P("grp"),
        ),
        out_specs=(P("grp", "tp"), P("grp", "tp"), P(("grp", "tp"), "kv", None)),
        check_vma=False,
    )
```

```python
import functools
import math

import jax
import jax.numpy as jnp
import numpy as np
from jax import lax
from jax.experimental import pallas as pl
from jax.experimental.pallas import tpu as pltpu
from jax.sharding import PartitionSpec as P

D = 8192
EPS = 1e-05
ROPE_BASE = 500000.0
LANES = 128
MIB = 1 << 20
COPY_ROWS = 2048
DOWN_ROWS = 1024
GU_SHARES = (4, 6, 4, 3, 4, 4, 3)
F32 = jnp.float32
BF16 = jnp.bfloat16
QUARTER = (1.5703125, 4.837512969970703125e-4, 7.549789948768648e-8)
SIN = (-1.9515295891e-4, 8.3321608736e-3, -1.6666654611e-1)
COS = (2.443315711809948e-5, -1.388731625493765e-3, 4.166664568298827e-2)


def vmem():
    return pl.BlockSpec(memory_space=pltpu.VMEM)


def hbm():
    return pl.BlockSpec(memory_space=pltpu.HBM)


def in_hbm(array):
    return pltpu.with_memory_space_constraint(array, pltpu.HBM)


def exchange(arrays, axis, size):
    return [arrays[0]] + [
        lax.ppermute(arrays[s], axis, [(i, i ^ s) for i in range(size)])
        for s in range(1, size)
    ]


def tree_sum(parts):
    while len(parts) > 1:
        parts = [a + b for a, b in zip(parts[::2], parts[1::2])]
    return parts[0]


def two_parts(scaled):
    high = scaled.astype(BF16).astype(F32)
    return high, scaled - high


def spread(rows16, out_ref, docs):
    width = rows16.shape[1]
    pick = one_hot_spread(2)
    row = lax.broadcasted_iota(jnp.int32, (4 * docs, 2 * LANES), 0)
    lane = lax.broadcasted_iota(jnp.int32, (4 * docs, 2 * LANES), 1)
    keep = (lax.shift_right_logical(row, docs.bit_length() - 1) & 1) == (lane & 1)
    chunks = width // LANES
    stacked = jnp.concatenate(
        [rows16[:, c * LANES : (c + 1) * LANES] for c in range(chunks)], axis=0
    )
    doubled = jnp.dot(stacked, pick, preferred_element_type=F32)
    for c in range(chunks):
        piece = doubled[c * 4 * docs : (c + 1) * 4 * docs]
        out_ref[:, 2 * c * LANES : 2 * (c + 1) * LANES] = jnp.where(keep, piece, 0.0).astype(BF16)


def start_all(copies):
    for copy in copies:
        copy.start(priority=1)


def matrix_of(w):
    return w if len(w.shape) == 2 else w.reshape(w.shape[0] * w.shape[1], w.shape[2])


def block_copies(matrix, first, buf, sems):
    rows, columns = buf.shape
    chunk = min(rows, COPY_ROWS)
    return [
        pltpu.make_async_copy(
            matrix.at[pl.ds(start, chunk), pl.ds(first * LANES, columns)],
            buf.at[pl.ds(start, chunk)],
            sems.at[start // chunk],
        )
        for start in range(0, rows, chunk)
    ]


def pick_doc(value, doc, docs):
    axis = value.ndim - 2
    row = lax.broadcasted_iota(jnp.int32, value.shape, axis)
    return jnp.sum(jnp.where(row & (docs - 1) == doc, value, 0.0), axis=axis)


def sine_cosine(angle):
    turns = jnp.floor(angle * (2.0 / math.pi) + 0.5)
    rest = ((angle - turns * QUARTER[0]) - turns * QUARTER[1]) - turns * QUARTER[2]
    square = rest * rest
    sine = rest + rest * square * ((SIN[0] * square + SIN[1]) * square + SIN[2])
    cosine = 1.0 - 0.5 * square + square * square * (
        (COS[0] * square + COS[1]) * square + COS[2]
    )
    quadrant = turns - 4.0 * jnp.floor(turns * 0.25)
    odd = (quadrant == 1.0) | (quadrant == 3.0)
    sine, cosine = jnp.where(odd, cosine, sine), jnp.where(odd, sine, cosine)
    return (
        jnp.where(quadrant >= 2.0, -sine, sine),
        jnp.where((quadrant == 1.0) | (quadrant == 2.0), -cosine, cosine),
    )


def rope_rows(length, frequency):
    sine, cosine = sine_cosine(length * frequency)
    lane = lax.broadcasted_iota(jnp.int32, (1, LANES), 1)
    return cosine, jnp.where(lane < LANES // 2, -sine, sine)


def one_hot_spread(fold):
    source = lax.broadcasted_iota(jnp.int32, (LANES, fold * LANES), 0)
    target = lax.broadcasted_iota(jnp.int32, (LANES, fold * LANES), 1)
    return (lax.shift_right_logical(target, fold.bit_length() - 1) == source).astype(F32).astype(BF16)


def spread_heads(rows, out_ref, heads):
    count, width = rows.shape
    chunks = width // LANES
    stacked = jnp.concatenate([rows[:, c * LANES : (c + 1) * LANES] for c in range(chunks)], axis=0)
    wide = jnp.dot(stacked.astype(BF16), one_hot_spread(heads), preferred_element_type=F32)
    columns = heads * LANES
    lane = lax.broadcasted_iota(jnp.int32, (count, columns), 1) & (heads - 1)
    for c in range(chunks):
        piece = wide[c * count : (c + 1) * count]
        for h in range(0, heads, 2):
            pair = [jnp.where(lane == h + i, piece, 0.0) for i in range(2)]
            out_ref[h * count : (h + 2) * count, c * columns : (c + 1) * columns] = (
                jnp.concatenate(pair, axis=0).astype(BF16)
            )


def qkv_kernel(tp, owner_hbm, lengths_hbm, frequency_hbm, states_hbm, gains_hbm, wq, wkv, *rest):
    outs = rest[:tp]
    table, places = rest[tp : tp + 2]
    owner, lengths, frequency, states, gains = rest[tp + 2 : tp + 7]
    wq_buf, wkv_buf, spread_buf, sems, small_sems = rest[tp + 7 :]
    docs, width = states.shape
    heads = wq.shape[0] // width
    parts = wq_buf.shape[0]
    rows = wq_buf.shape[1]
    small = [
        pltpu.make_async_copy(source, target, small_sems.at[i])
        for i, (source, target) in enumerate(
            [
                (states_hbm, states),
                (gains_hbm, gains),
                (owner_hbm, owner),
                (lengths_hbm, lengths),
                (frequency_hbm, frequency),
            ]
        )
    ]
    copies = [
        pltpu.make_async_copy(wq.at[pl.ds(c * rows, rows)], wq_buf.at[c], sems.at[c])
        for c in range(parts)
    ]
    kv_copy = pltpu.make_async_copy(wkv, wkv_buf, sems.at[parts])
    start_all(small + [kv_copy] + copies)
    for copy in small:
        copy.wait()
    me = lax.axis_index("tp")
    x = states[...].astype(F32)
    squares = jnp.broadcast_to(jnp.sum(x * x, axis=1, keepdims=True), (docs, LANES))
    both = jnp.concatenate(two_parts(x * gains[0:1, :]), axis=0)
    kv_copy.wait()
    kv_total = jnp.dot(both.astype(BF16), wkv_buf[...], preferred_element_type=F32)
    spread_heads(both, spread_buf, heads)
    length = lengths[owner[me]].astype(F32)
    cosine, sine = rope_rows(length, frequency[...])
    table[0:1, :] = cosine
    table[1:2, :] = sine
    table[2:3, :] = jnp.full((1, LANES), length, F32)
    table[3:, :] = jnp.zeros((table.shape[0] - 3, LANES), F32)
    for s in range(tp):
        places[s : s + 1, :] = jnp.full((1, LANES), owner[me ^ s], jnp.int32)
    total = jnp.zeros((heads * 2 * docs, LANES), F32)
    for c in range(parts):
        copies[c].wait()
        total = total + jnp.dot(
            spread_buf[:, c * rows : (c + 1) * rows], wq_buf[c], preferred_element_type=F32
        )
    total = total.reshape(heads, 2 * docs, LANES)
    for s in range(tp):
        doc = owner[me ^ s]
        out = outs[s]
        out[:heads, :] = pick_doc(total, doc, docs)
        kv_row = pick_doc(kv_total, doc, docs)[None]
        out[heads : heads + 1, :] = kv_row[:, :LANES]
        out[heads + 1 : heads + 2, :] = kv_row[:, LANES:]
        out[heads + 2 : heads + 3, :] = pick_doc(squares, doc, docs)[None]
        out[heads + 3 :, :] = jnp.zeros((out.shape[0] - heads - 3, LANES), F32)


def attend_kernel(tp, heads, rows, first, table, cache, w, *rest):
    parts = rest[:tp]
    heads_out, new_kv_out, w_ready, scores, new_kv, w_sems, out_sem = rest[-7:]
    w_copies = block_copies(matrix_of(w), first, w_ready, w_sems)
    start_all(w_copies)
    blocks = cache.shape[0] // rows
    sums = tree_sum([part[...] for part in parts])
    sums = sums * lax.rsqrt(sums[heads + 2 : heads + 3, :] / D + EPS)
    rotated = sums * table[0:1, :] + pltpu.roll(sums, LANES // 2, 1) * table[1:2, :]
    query = rotated[:heads].astype(BF16)
    key = rotated[heads : heads + 1].astype(BF16)
    value = sums[heads + 1 : heads + 2].astype(BF16)
    new_kv[:, :LANES] = key
    new_kv[:, LANES:] = value
    out_copy = pltpu.make_async_copy(new_kv, new_kv_out, out_sem.at[0])
    out_copy.start()
    key = key.astype(F32)
    value = value.astype(F32)
    scale = LANES ** (-0.5)
    own = jnp.sum(query.astype(F32) * key, axis=1, keepdims=True) * scale
    column = lax.broadcasted_iota(jnp.int32, (heads, LANES), 1).astype(F32)
    length = table[2:3, :]
    tops = jnp.full((heads, LANES), -jnp.inf, F32)
    for b in range(blocks):
        block = lax.dot_general(
            query,
            cache[b * rows : (b + 1) * rows, :LANES],
            (((1,), (1,)), ((), ())),
            preferred_element_type=F32,
        )
        for start in range(0, rows, LANES):
            at = b * rows + start
            piece = block[:, start : start + LANES] * scale
            piece = jnp.where(column < length - at, piece, -jnp.inf)
            tops = jnp.maximum(tops, piece)
            scores[:, at : at + LANES] = piece
    top = jnp.maximum(jnp.max(tops, axis=1, keepdims=True), own)
    own = jnp.exp(own - top)
    sums_by_lane = jnp.zeros((heads, LANES), F32)
    acc = own.astype(BF16).astype(F32) * value
    for b in range(blocks):
        weights = jnp.exp(scores[:, b * rows : (b + 1) * rows] - top)
        for start in range(0, rows, LANES):
            sums_by_lane = sums_by_lane + weights[:, start : start + LANES]
        acc = acc + jnp.dot(
            weights.astype(BF16),
            cache[b * rows : (b + 1) * rows, LANES:],
            preferred_element_type=F32,
        )
    total = own + jnp.sum(sums_by_lane, axis=1, keepdims=True)
    heads_out[...] = (acc / total).astype(BF16)
    for copy in w_copies:
        copy.wait()
    out_copy.wait()


def out_kernel(tp, places, w_out, *rest):
    parts = rest[:tp]
    out, left = rest[-2:]
    docs = out.shape[0]
    row = lax.broadcasted_iota(jnp.int32, (left.shape[0], LANES), 0)
    own = [parts[s][...].astype(F32) for s in range(tp)]
    for h in range(own[0].shape[0]):
        piece = jnp.zeros((left.shape[0], LANES), F32)
        for s in range(tp):
            piece = jnp.where(row == places[s : s + 1, :], own[s][h : h + 1, :], piece)
        left[:, h * LANES : (h + 1) * LANES] = piece
    terms = jnp.dot(left[...].astype(BF16), w_out[...], preferred_element_type=F32)
    out[...] = terms[:docs].astype(BF16)


def fetch_kernel(first, token, w, *rest):
    out, sems = rest[-2:]
    copies = block_copies(matrix_of(w), first, out, sems)
    start_all(copies)
    for copy in copies:
        copy.wait()


def gate_up_kernel(kv, groups, first, states, gains, w, *rest):
    ready, parts = rest[:groups], rest[groups : groups + kv]
    attn_out, partial_out, *blocks, spread_buf, attn_buf, w_sems, out_sem = rest[groups + kv :]
    docs, width = states.shape
    hidden = w.shape[2]
    w_matrix = matrix_of(w)
    copies = []
    for i, block in enumerate(blocks):
        copies.append(block_copies(w_matrix, first, block, w_sems.at[i]))
        first += block.shape[1] // LANES
        start_all(copies[-1])
    attn = tree_sum([part[...].astype(F32) for part in parts]).astype(BF16)
    attn_buf[...] = attn
    out_copy = pltpu.make_async_copy(attn_buf, attn_out, out_sem.at[0])
    out_copy.start()
    resid = (states[...].astype(F32) + attn.astype(F32)).astype(BF16).astype(F32)
    squares = jnp.sum(resid * resid, axis=1, keepdims=True)
    high, low = two_parts(resid * gains[1:2, :])
    spread(jnp.concatenate([high, high, low, low], axis=0).astype(BF16), spread_buf, docs)

    lane = lax.broadcasted_iota(jnp.int32, (docs, LANES), 1)
    first = squares.astype(BF16).astype(F32)
    second = (squares - first).astype(BF16).astype(F32)
    third = squares - first - second
    terms = jnp.where(lane == 0, first, jnp.where(lane == 1, second, jnp.where(lane == 2, third, 0.0)))
    partial_out[:, hidden:] = jnp.concatenate([terms, terms], axis=0).astype(BF16)
    at = 0
    for i, block in enumerate([*ready, *blocks]):
        if i >= groups:
            for copy in copies[i - groups]:
                copy.wait()
        product = jnp.dot(spread_buf[...], block[...], preferred_element_type=F32)
        columns = slice(at, at + block.shape[1])
        partial_out[:, columns] = (product[: 2 * docs] + product[2 * docs :]).astype(BF16)
        at += block.shape[1]
    out_copy.wait()


def down_kernel(tp, w_down, *rest):
    parts, out = rest[:tp], rest[tp]
    docs, width = out.shape
    hidden = w_down.shape[0]

    def summed(start, size):
        return tree_sum([part[:, start : start + size].astype(F32) for part in parts])

    squares = jnp.sum(summed(hidden, LANES)[:docs], axis=1, keepdims=True)
    inverse = lax.rsqrt(squares / D + EPS)
    total = jnp.zeros((docs, width), F32)
    for start in range(0, hidden, DOWN_ROWS):
        size = min(DOWN_ROWS, hidden - start)
        both = summed(start, size)
        gate = both[:docs] * inverse
        up = both[docs:] * inverse
        act = (gate / (1.0 + jnp.exp(-gate)) * up).astype(BF16)
        total = total + jnp.dot(
            act, w_down[start : start + size, :], preferred_element_type=F32
        )
    out[...] = total.astype(BF16)


def cost(micros):
    return pl.CostEstimate(flops=0, bytes_accessed=int(micros * 3.69e6), transcendentals=0)


def params(docs, mib):
    return pltpu.CompilerParams(vmem_limit_bytes=(mib if docs <= 8 else mib + 24) * MIB)


def per_device(
    tp, kv,
    states, norm_gains, w_query, w_keyval, w_out, w_gate_up, w_down, kv_cache, lengths, owner_rows
):
    docs, width = states.shape
    heads = w_query.shape[1]
    cache_len = kv_cache.shape[1]
    hidden = w_gate_up.shape[2]
    wq = w_query.reshape(width * heads, LANES)
    wkv = w_keyval.reshape(width, 2 * LANES)
    cache = kv_cache.reshape(cache_len, 2 * LANES)
    packed = 2 * heads
    wq_parts = 4

    half = LANES // 2
    freq = ROPE_BASE ** (-(np.arange(half, dtype=np.float64) * 2.0 / LANES))
    freq = jnp.asarray(np.concatenate([freq, freq]).astype(np.float32)[None, :])
    *qkv_parts, table, places = pl.pallas_call(
        functools.partial(qkv_kernel, tp),
        out_shape=[jax.ShapeDtypeStruct((packed, LANES), F32)] * tp
        + [
            jax.ShapeDtypeStruct((8, LANES), F32),
            jax.ShapeDtypeStruct((max(tp, 8), LANES), jnp.int32),
        ],
        in_specs=[hbm()] * 7,
        out_specs=[vmem()] * (tp + 2),
        scratch_shapes=[
            pltpu.SMEM((docs,), jnp.int32),
            pltpu.SMEM((docs,), jnp.int32),
            pltpu.VMEM((1, LANES), F32),
            pltpu.VMEM((docs, width), BF16),
            pltpu.VMEM((2, width), F32),
            pltpu.VMEM((wq_parts, width * heads // wq_parts, LANES), BF16),
            pltpu.VMEM((width, 2 * LANES), BF16),
            pltpu.VMEM((heads * 2 * docs, width * heads), BF16),
            pltpu.SemaphoreType.DMA((wq_parts + 1,)),
            pltpu.SemaphoreType.DMA((5,)),
        ],
        compiler_params=params(docs, 10),
        cost_estimate=cost(8),
        name="qkv",
    )(*(in_hbm(a) for a in (owner_rows, lengths, freq, states, norm_gains, wq, wkv)))
    w_gu = in_hbm(w_gate_up)
    bounds = np.cumsum([0] + [hidden // LANES * n // 28 for n in GU_SHARES]).tolist()
    shares = list(zip(bounds, bounds[1:]))
    fetched = []

    chunks = max(2 * width // COPY_ROWS, 1)

    def block_of(share):
        return pltpu.VMEM((2 * width, (share[1] - share[0]) * LANES), BF16)

    def fetch(share, token, *keep):
        return pl.pallas_call(
            functools.partial(fetch_kernel, share[0]),
            out_shape=block_of(share),
            in_specs=[hbm(), hbm()] + [vmem()] * len(keep),
            out_specs=vmem(),
            scratch_shapes=[pltpu.SemaphoreType.DMA((chunks,))],
            compiler_params=params(docs, 2),
            cost_estimate=cost(0.3 * (share[1] - share[0])),
            name="fetch",
        )(token, w_gu, *keep)

    fetched.append(fetch(shares[0], table, cache))
    qkv_parts = exchange(qkv_parts, "tp", tp)[::-1]
    head_out, new_kv, w_ready = pl.pallas_call(
        functools.partial(attend_kernel, tp, heads, 512, shares[1][0]),
        out_shape=[
            jax.ShapeDtypeStruct((heads, LANES), BF16),
            jax.ShapeDtypeStruct((1, 2 * LANES), BF16),
            block_of(shares[1]),
        ],
        in_specs=[vmem(), vmem(), hbm()] + [vmem()] * tp + [hbm()] * len(fetched),
        out_specs=[vmem(), hbm(), vmem()],
        scratch_shapes=[
            pltpu.VMEM((heads, cache_len), F32),
            pltpu.VMEM((1, 2 * LANES), BF16),
            pltpu.SemaphoreType.DMA((chunks,)),
            pltpu.SemaphoreType.DMA((1,)),
        ],
        compiler_params=params(docs, 6),
        cost_estimate=cost(8),
        name="attend",
    )(table, cache, w_gu, *qkv_parts, *fetched)
    fetched.append(w_ready)

    fetched.append(fetch(shares[2], head_out))
    head_parts = exchange([head_out] * tp, "tp", tp)
    out_part = pl.pallas_call(
        functools.partial(out_kernel, tp),
        out_shape=jax.ShapeDtypeStruct((docs, width), BF16),
        in_specs=[vmem()] * (tp + 2) + [hbm()],
        out_specs=vmem(),
        scratch_shapes=[pltpu.VMEM((max(docs, 8), heads * LANES), F32)],
        compiler_params=params(docs, 6),
        cost_estimate=cost(6),
        name="attn_project",
    )(places, w_out, *head_parts, fetched[-1])

    fetched.append(fetch(shares[3], out_part, w_down))
    out_parts = exchange([out_part] * kv, "kv", kv)
    attn_out, gu_part = pl.pallas_call(
        functools.partial(gate_up_kernel, kv, len(fetched), shares[4][0]),
        out_shape=[
            jax.ShapeDtypeStruct((docs, width), BF16),
            jax.ShapeDtypeStruct((2 * docs, hidden + LANES), BF16),
        ],
        in_specs=[vmem(), vmem(), hbm()] + [vmem()] * (len(fetched) + kv),
        out_specs=[hbm(), vmem()],
        scratch_shapes=[
            *(block_of(share) for share in shares[4:]),
            pltpu.VMEM((4 * docs, 2 * width), BF16),
            pltpu.VMEM((docs, width), BF16),
            pltpu.SemaphoreType.DMA((len(shares) - 4, chunks)),
            pltpu.SemaphoreType.DMA((1,)),
        ],
        compiler_params=params(docs, 19),
        cost_estimate=cost(10),
        name="gate_up",
    )(states, norm_gains, w_gu, *fetched, *out_parts)

    gu_parts = exchange([gu_part] * tp, "tp", tp)
    ffn_part = pl.pallas_call(
        functools.partial(down_kernel, tp),
        out_shape=jax.ShapeDtypeStruct((docs, width), BF16),
        in_specs=[vmem()] * (1 + tp),
        out_specs=vmem(),
        compiler_params=params(docs, 6),
        cost_estimate=cost(5),
        name="down",
    )(w_down, *gu_parts)
    ffn_parts = exchange([ffn_part] * kv, "kv", kv)
    ffn_out = tree_sum([part.astype(F32) for part in ffn_parts]).astype(BF16)
    return attn_out, ffn_out, new_kv.reshape(1, 1, 2 * LANES)


def solution(mesh):
    return jax.shard_map(
        functools.partial(per_device, mesh.shape["tp"], mesh.shape["kv"]),
        mesh=mesh,
        in_specs=(
            P("grp", "tp"),
            P(None, "tp"),
            P("tp", "kv", None),
            P("tp", "kv", None),
            P("kv", "tp"),
            P("tp", None, "kv"),
            P("kv", "tp"),
            P(("grp", "tp"), None, "kv", None),
            P("grp"),
            P("grp"),
        ),
        out_specs=(P("grp", "tp"), P("grp", "tp"), P(("grp", "tp"), "kv", None)),
        check_vma=False,
    )
```

```python
import functools
import math

import jax
import jax.numpy as jnp
import numpy as np
from jax import lax
from jax.experimental import pallas as pl
from jax.experimental.pallas import tpu as pltpu
from jax.sharding import PartitionSpec as P

D = 8192
EPS = 1e-05
ROPE_BASE = 500000.0
LANES = 128
MIB = 1 << 20
COPY_ROWS = 2048
DOWN_ROWS = 1024
GU_SHARES = (4, 6, 2, 3, 4, 4, 3, 2)
F32 = jnp.float32
BF16 = jnp.bfloat16
QUARTER = (1.5703125, 4.837512969970703125e-4, 7.549789948768648e-8)
SIN = (-1.9515295891e-4, 8.3321608736e-3, -1.6666654611e-1)
COS = (2.443315711809948e-5, -1.388731625493765e-3, 4.166664568298827e-2)


def vmem():
    return pl.BlockSpec(memory_space=pltpu.VMEM)


def hbm():
    return pl.BlockSpec(memory_space=pltpu.HBM)


def in_hbm(array):
    return pltpu.with_memory_space_constraint(array, pltpu.HBM)


def exchange(arrays, axis, size):
    return [arrays[0]] + [
        lax.ppermute(arrays[s], axis, [(i, i ^ s) for i in range(size)])
        for s in range(1, size)
    ]


def tree_sum(parts):
    while len(parts) > 1:
        parts = [a + b for a, b in zip(parts[::2], parts[1::2])]
    return parts[0]


def two_parts(scaled):
    high = scaled.astype(BF16).astype(F32)
    return high, scaled - high


def spread(rows16, out_ref, docs):
    width = rows16.shape[1]
    pick = one_hot_spread(2)
    row = lax.broadcasted_iota(jnp.int32, (4 * docs, 2 * LANES), 0)
    lane = lax.broadcasted_iota(jnp.int32, (4 * docs, 2 * LANES), 1)
    keep = (lax.shift_right_logical(row, docs.bit_length() - 1) & 1) == (lane & 1)
    chunks = width // LANES
    stacked = jnp.concatenate(
        [rows16[:, c * LANES : (c + 1) * LANES] for c in range(chunks)], axis=0
    )
    doubled = jnp.dot(stacked, pick, preferred_element_type=F32)
    for c in range(chunks):
        piece = doubled[c * 4 * docs : (c + 1) * 4 * docs]
        out_ref[:, 2 * c * LANES : 2 * (c + 1) * LANES] = jnp.where(keep, piece, 0.0).astype(BF16)


def start_all(copies):
    for copy in copies:
        copy.start(priority=1)


def matrix_of(w):
    return w if len(w.shape) == 2 else w.reshape(w.shape[0] * w.shape[1], w.shape[2])


def block_copies(matrix, first, buf, sems):
    rows, columns = buf.shape
    chunk = min(rows, COPY_ROWS)
    return [
        pltpu.make_async_copy(
            matrix.at[pl.ds(start, chunk), pl.ds(first * LANES, columns)],
            buf.at[pl.ds(start, chunk)],
            sems.at[start // chunk],
        )
        for start in range(0, rows, chunk)
    ]


def pick_doc(value, doc, docs):
    axis = value.ndim - 2
    row = lax.broadcasted_iota(jnp.int32, value.shape, axis)
    return jnp.sum(jnp.where(row & (docs - 1) == doc, value, 0.0), axis=axis)


def sine_cosine(angle):
    turns = jnp.floor(angle * (2.0 / math.pi) + 0.5)
    rest = ((angle - turns * QUARTER[0]) - turns * QUARTER[1]) - turns * QUARTER[2]
    square = rest * rest
    sine = rest + rest * square * ((SIN[0] * square + SIN[1]) * square + SIN[2])
    cosine = 1.0 - 0.5 * square + square * square * (
        (COS[0] * square + COS[1]) * square + COS[2]
    )
    quadrant = turns - 4.0 * jnp.floor(turns * 0.25)
    odd = (quadrant == 1.0) | (quadrant == 3.0)
    sine, cosine = jnp.where(odd, cosine, sine), jnp.where(odd, sine, cosine)
    return (
        jnp.where(quadrant >= 2.0, -sine, sine),
        jnp.where((quadrant == 1.0) | (quadrant == 2.0), -cosine, cosine),
    )


def rope_rows(length, frequency):
    sine, cosine = sine_cosine(length * frequency)
    lane = lax.broadcasted_iota(jnp.int32, (1, LANES), 1)
    return cosine, jnp.where(lane < LANES // 2, -sine, sine)


def one_hot_spread(fold):
    source = lax.broadcasted_iota(jnp.int32, (LANES, fold * LANES), 0)
    target = lax.broadcasted_iota(jnp.int32, (LANES, fold * LANES), 1)
    return (lax.shift_right_logical(target, fold.bit_length() - 1) == source).astype(F32).astype(BF16)


def spread_heads(rows, out_ref, heads):
    count, width = rows.shape
    chunks = width // LANES
    stacked = jnp.concatenate([rows[:, c * LANES : (c + 1) * LANES] for c in range(chunks)], axis=0)
    wide = jnp.dot(stacked.astype(BF16), one_hot_spread(heads), preferred_element_type=F32)
    columns = heads * LANES
    lane = lax.broadcasted_iota(jnp.int32, (count, columns), 1) & (heads - 1)
    for c in range(chunks):
        piece = wide[c * count : (c + 1) * count]
        for h in range(0, heads, 2):
            pair = [jnp.where(lane == h + i, piece, 0.0) for i in range(2)]
            out_ref[h * count : (h + 2) * count, c * columns : (c + 1) * columns] = (
                jnp.concatenate(pair, axis=0).astype(BF16)
            )


def qkv_kernel(tp, owner_hbm, lengths_hbm, frequency_hbm, states_hbm, gains_hbm, wq, wkv, *rest):
    outs = rest[:tp]
    table, places = rest[tp : tp + 2]
    owner, lengths, frequency, states, gains = rest[tp + 2 : tp + 7]
    wq_buf, wkv_buf, spread_buf, sems, small_sems = rest[tp + 7 :]
    docs, width = states.shape
    heads = wq.shape[0] // width
    parts = wq_buf.shape[0]
    rows = wq_buf.shape[1]
    small = [
        pltpu.make_async_copy(source, target, small_sems.at[i])
        for i, (source, target) in enumerate(
            [
                (states_hbm, states),
                (gains_hbm, gains),
                (owner_hbm, owner),
                (lengths_hbm, lengths),
                (frequency_hbm, frequency),
            ]
        )
    ]
    copies = [
        pltpu.make_async_copy(wq.at[pl.ds(c * rows, rows)], wq_buf.at[c], sems.at[c])
        for c in range(parts)
    ]
    kv_copy = pltpu.make_async_copy(wkv, wkv_buf, sems.at[parts])
    for copy in small:
        copy.start()
    start_all([kv_copy] + copies)
    for copy in small:
        copy.wait()
    me = lax.axis_index("tp")
    x = states[...].astype(F32)
    squares = jnp.broadcast_to(jnp.sum(x * x, axis=1, keepdims=True), (docs, LANES))
    both = jnp.concatenate(two_parts(x * gains[0:1, :]), axis=0)
    kv_copy.wait()
    kv_total = jnp.dot(both.astype(BF16), wkv_buf[...], preferred_element_type=F32)
    spread_heads(both, spread_buf, heads)
    length = lengths[owner[me]].astype(F32)
    cosine, sine = rope_rows(length, frequency[...])
    table[0:1, :] = cosine
    table[1:2, :] = sine
    table[2:3, :] = jnp.full((1, LANES), length, F32)
    table[3:, :] = jnp.zeros((table.shape[0] - 3, LANES), F32)
    for s in range(tp):
        places[s : s + 1, :] = jnp.full((1, LANES), owner[me ^ s], jnp.int32)
    total = jnp.zeros((heads * 2 * docs, LANES), F32)
    for c in range(parts):
        copies[c].wait()
        total = total + jnp.dot(
            spread_buf[:, c * rows : (c + 1) * rows], wq_buf[c], preferred_element_type=F32
        )
    total = total.reshape(heads, 2 * docs, LANES)
    for s in range(tp):
        doc = owner[me ^ s]
        out = outs[s]
        out[:heads, :] = pick_doc(total, doc, docs)
        kv_row = pick_doc(kv_total, doc, docs)[None]
        out[heads : heads + 1, :] = kv_row[:, :LANES]
        out[heads + 1 : heads + 2, :] = kv_row[:, LANES:]
        out[heads + 2 : heads + 3, :] = pick_doc(squares, doc, docs)[None]
        out[heads + 3 :, :] = jnp.zeros((out.shape[0] - heads - 3, LANES), F32)


def attend_kernel(tp, heads, rows, first, table, cache, w, *rest):
    parts = rest[:tp]
    heads_out, new_kv_out, w_ready, scores, new_kv, w_sems, out_sem = rest[-7:]
    w_copies = block_copies(matrix_of(w), first, w_ready, w_sems)
    start_all(w_copies)
    blocks = cache.shape[0] // rows
    sums = tree_sum([part[...] for part in parts])
    sums = sums * lax.rsqrt(sums[heads + 2 : heads + 3, :] / D + EPS)
    rotated = sums * table[0:1, :] + pltpu.roll(sums, LANES // 2, 1) * table[1:2, :]
    query = rotated[:heads].astype(BF16)
    key = rotated[heads : heads + 1].astype(BF16)
    value = sums[heads + 1 : heads + 2].astype(BF16)
    new_kv[:, :LANES] = key
    new_kv[:, LANES:] = value
    out_copy = pltpu.make_async_copy(new_kv, new_kv_out, out_sem.at[0])
    out_copy.start()
    key = key.astype(F32)
    value = value.astype(F32)
    scale = LANES ** (-0.5)
    own = jnp.sum(query.astype(F32) * key, axis=1, keepdims=True) * scale
    column = lax.broadcasted_iota(jnp.int32, (heads, LANES), 1).astype(F32)
    length = table[2:3, :]
    tops = jnp.full((heads, LANES), -jnp.inf, F32)
    for b in range(blocks):
        block = lax.dot_general(
            query,
            cache[b * rows : (b + 1) * rows, :LANES],
            (((1,), (1,)), ((), ())),
            preferred_element_type=F32,
        )
        for start in range(0, rows, LANES):
            at = b * rows + start
            piece = block[:, start : start + LANES] * scale
            piece = jnp.where(column < length - at, piece, -jnp.inf)
            tops = jnp.maximum(tops, piece)
            scores[:, at : at + LANES] = piece
    top = jnp.maximum(jnp.max(tops, axis=1, keepdims=True), own)
    own = jnp.exp(own - top)
    sums_by_lane = jnp.zeros((heads, LANES), F32)
    acc = own.astype(BF16).astype(F32) * value
    for b in range(blocks):
        weights = jnp.exp(scores[:, b * rows : (b + 1) * rows] - top)
        for start in range(0, rows, LANES):
            sums_by_lane = sums_by_lane + weights[:, start : start + LANES]
        acc = acc + jnp.dot(
            weights.astype(BF16),
            cache[b * rows : (b + 1) * rows, LANES:],
            preferred_element_type=F32,
        )
    total = own + jnp.sum(sums_by_lane, axis=1, keepdims=True)
    heads_out[...] = (acc / total).astype(BF16)
    for copy in w_copies:
        copy.wait()
    out_copy.wait()


def out_kernel(tp, places, w_out, *rest):
    parts = rest[:tp]
    out, left = rest[-2:]
    docs = out.shape[0]
    row = lax.broadcasted_iota(jnp.int32, (left.shape[0], LANES), 0)
    own = [parts[s][...].astype(F32) for s in range(tp)]
    for h in range(own[0].shape[0]):
        piece = jnp.zeros((left.shape[0], LANES), F32)
        for s in range(tp):
            piece = jnp.where(row == places[s : s + 1, :], own[s][h : h + 1, :], piece)
        left[:, h * LANES : (h + 1) * LANES] = piece
    terms = jnp.dot(left[...].astype(BF16), w_out[...], preferred_element_type=F32)
    out[...] = terms[:docs].astype(BF16)


def fetch_kernel(first, token, w, *rest):
    out, sems = rest[-2:]
    copies = block_copies(matrix_of(w), first, out, sems)
    start_all(copies)
    for copy in copies:
        copy.wait()


def gate_up_kernel(kv, groups, first, states, gains, w, *rest):
    ready, parts = rest[:groups], rest[groups : groups + kv]
    attn_out, partial_out, *blocks, spread_buf, attn_buf, w_sems, out_sem = rest[groups + kv :]
    docs, width = states.shape
    hidden = w.shape[2]
    w_matrix = matrix_of(w)
    copies = []
    for i, block in enumerate(blocks):
        copies.append(block_copies(w_matrix, first, block, w_sems.at[i]))
        first += block.shape[1] // LANES
        start_all(copies[-1])
    attn = tree_sum([part[...].astype(F32) for part in parts]).astype(BF16)
    attn_buf[...] = attn
    out_copy = pltpu.make_async_copy(attn_buf, attn_out, out_sem.at[0])
    out_copy.start()
    resid = (states[...].astype(F32) + attn.astype(F32)).astype(BF16).astype(F32)
    squares = jnp.sum(resid * resid, axis=1, keepdims=True)
    high, low = two_parts(resid * gains[1:2, :])
    spread(jnp.concatenate([high, high, low, low], axis=0).astype(BF16), spread_buf, docs)

    lane = lax.broadcasted_iota(jnp.int32, (docs, LANES), 1)
    first = squares.astype(BF16).astype(F32)
    second = (squares - first).astype(BF16).astype(F32)
    third = squares - first - second
    terms = jnp.where(lane == 0, first, jnp.where(lane == 1, second, jnp.where(lane == 2, third, 0.0)))
    partial_out[:, hidden:] = jnp.concatenate([terms, terms], axis=0).astype(BF16)
    at = 0
    for i, block in enumerate([*ready, *blocks]):
        if i >= groups:
            for copy in copies[i - groups]:
                copy.wait()
        product = jnp.dot(spread_buf[...], block[...], preferred_element_type=F32)
        columns = slice(at, at + block.shape[1])
        partial_out[:, columns] = (product[: 2 * docs] + product[2 * docs :]).astype(BF16)
        at += block.shape[1]
    out_copy.wait()


def down_kernel(tp, w_down, *rest):
    parts, out = rest[:tp], rest[tp]
    docs, width = out.shape
    hidden = w_down.shape[0]

    def summed(start, size):
        return tree_sum([part[:, start : start + size].astype(F32) for part in parts])

    squares = jnp.sum(summed(hidden, LANES)[:docs], axis=1, keepdims=True)
    inverse = lax.rsqrt(squares / D + EPS)
    total = jnp.zeros((docs, width), F32)
    for start in range(0, hidden, DOWN_ROWS):
        size = min(DOWN_ROWS, hidden - start)
        both = summed(start, size)
        gate = both[:docs] * inverse
        up = both[docs:] * inverse
        act = (gate / (1.0 + jnp.exp(-gate)) * up).astype(BF16)
        total = total + jnp.dot(
            act, w_down[start : start + size, :], preferred_element_type=F32
        )
    out[...] = total.astype(BF16)


def cost(micros):
    return pl.CostEstimate(flops=0, bytes_accessed=int(micros * 3.69e6), transcendentals=0)


def params(docs, mib):
    return pltpu.CompilerParams(vmem_limit_bytes=(mib if docs <= 8 else mib + 24) * MIB)


def per_device(
    tp, kv,
    states, norm_gains, w_query, w_keyval, w_out, w_gate_up, w_down, kv_cache, lengths, owner_rows
):
    docs, width = states.shape
    heads = w_query.shape[1]
    cache_len = kv_cache.shape[1]
    hidden = w_gate_up.shape[2]
    wq = w_query.reshape(width * heads, LANES)
    wkv = w_keyval.reshape(width, 2 * LANES)
    cache = kv_cache.reshape(cache_len, 2 * LANES)
    packed = 2 * heads
    wq_parts = 4

    half = LANES // 2
    freq = ROPE_BASE ** (-(np.arange(half, dtype=np.float64) * 2.0 / LANES))
    freq = jnp.asarray(np.concatenate([freq, freq]).astype(np.float32)[None, :])
    *qkv_parts, table, places = pl.pallas_call(
        functools.partial(qkv_kernel, tp),
        out_shape=[jax.ShapeDtypeStruct((packed, LANES), F32)] * tp
        + [
            jax.ShapeDtypeStruct((8, LANES), F32),
            jax.ShapeDtypeStruct((max(tp, 8), LANES), jnp.int32),
        ],
        in_specs=[hbm()] * 7,
        out_specs=[vmem()] * (tp + 2),
        scratch_shapes=[
            pltpu.SMEM((docs,), jnp.int32),
            pltpu.SMEM((docs,), jnp.int32),
            pltpu.VMEM((1, LANES), F32),
            pltpu.VMEM((docs, width), BF16),
            pltpu.VMEM((2, width), F32),
            pltpu.VMEM((wq_parts, width * heads // wq_parts, LANES), BF16),
            pltpu.VMEM((width, 2 * LANES), BF16),
            pltpu.VMEM((heads * 2 * docs, width * heads), BF16),
            pltpu.SemaphoreType.DMA((wq_parts + 1,)),
            pltpu.SemaphoreType.DMA((5,)),
        ],
        compiler_params=params(docs, 10),
        cost_estimate=cost(8),
        name="qkv",
    )(*(in_hbm(a) for a in (owner_rows, lengths, freq, states, norm_gains, wq, wkv)))
    w_gu = in_hbm(w_gate_up)
    bounds = np.cumsum([0] + [hidden // LANES * n // 28 for n in GU_SHARES]).tolist()
    shares = list(zip(bounds, bounds[1:]))
    fetched = []

    chunks = max(2 * width // COPY_ROWS, 1)

    def block_of(share):
        return pltpu.VMEM((2 * width, (share[1] - share[0]) * LANES), BF16)

    def fetch(share, token, *keep):
        return pl.pallas_call(
            functools.partial(fetch_kernel, share[0]),
            out_shape=block_of(share),
            in_specs=[hbm(), hbm()] + [vmem()] * len(keep),
            out_specs=vmem(),
            scratch_shapes=[pltpu.SemaphoreType.DMA((chunks,))],
            compiler_params=params(docs, 2),
            cost_estimate=cost(0.3 * (share[1] - share[0])),
            name="fetch",
        )(token, w_gu, *keep)

    fetched.append(fetch(shares[0], table, cache))
    qkv_parts = exchange(qkv_parts, "tp", tp)[::-1]
    head_out, new_kv, w_ready = pl.pallas_call(
        functools.partial(attend_kernel, tp, heads, 512, shares[1][0]),
        out_shape=[
            jax.ShapeDtypeStruct((heads, LANES), BF16),
            jax.ShapeDtypeStruct((1, 2 * LANES), BF16),
            block_of(shares[1]),
        ],
        in_specs=[vmem(), vmem(), hbm()] + [vmem()] * tp + [hbm()] * len(fetched),
        out_specs=[vmem(), hbm(), vmem()],
        scratch_shapes=[
            pltpu.VMEM((heads, cache_len), F32),
            pltpu.VMEM((1, 2 * LANES), BF16),
            pltpu.SemaphoreType.DMA((chunks,)),
            pltpu.SemaphoreType.DMA((1,)),
        ],
        compiler_params=params(docs, 6),
        cost_estimate=cost(8),
        name="attend",
    )(table, cache, w_gu, *qkv_parts, *fetched)
    fetched.append(w_ready)

    fetched.append(fetch(shares[2], head_out))
    head_parts = exchange([head_out] * tp, "tp", tp)
    out_part = pl.pallas_call(
        functools.partial(out_kernel, tp),
        out_shape=jax.ShapeDtypeStruct((docs, width), BF16),
        in_specs=[vmem()] * (tp + 2) + [hbm()],
        out_specs=vmem(),
        scratch_shapes=[pltpu.VMEM((max(docs, 8), heads * LANES), F32)],
        compiler_params=params(docs, 6),
        cost_estimate=cost(6),
        name="attn_project",
    )(places, w_out, *head_parts, fetched[-1])

    fetched.append(fetch(shares[3], out_part, w_down))
    out_parts = exchange([out_part] * kv, "kv", kv)
    attn_out, gu_part = pl.pallas_call(
        functools.partial(gate_up_kernel, kv, len(fetched), shares[4][0]),
        out_shape=[
            jax.ShapeDtypeStruct((docs, width), BF16),
            jax.ShapeDtypeStruct((2 * docs, hidden + LANES), BF16),
        ],
        in_specs=[vmem(), vmem(), hbm()] + [vmem()] * (len(fetched) + kv),
        out_specs=[hbm(), vmem()],
        scratch_shapes=[
            *(block_of(share) for share in shares[4:]),
            pltpu.VMEM((4 * docs, 2 * width), BF16),
            pltpu.VMEM((docs, width), BF16),
            pltpu.SemaphoreType.DMA((len(shares) - 4, chunks)),
            pltpu.SemaphoreType.DMA((1,)),
        ],
        compiler_params=params(docs, 19),
        cost_estimate=cost(10),
        name="gate_up",
    )(states, norm_gains, w_gu, *fetched, *out_parts)

    gu_parts = exchange([gu_part] * tp, "tp", tp)
    ffn_part = pl.pallas_call(
        functools.partial(down_kernel, tp),
        out_shape=jax.ShapeDtypeStruct((docs, width), BF16),
        in_specs=[vmem()] * (1 + tp),
        out_specs=vmem(),
        compiler_params=params(docs, 6),
        cost_estimate=cost(5),
        name="down",
    )(w_down, *gu_parts)
    ffn_parts = exchange([ffn_part] * kv, "kv", kv)
    ffn_out = tree_sum([part.astype(F32) for part in ffn_parts]).astype(BF16)
    return attn_out, ffn_out, new_kv.reshape(1, 1, 2 * LANES)


def solution(mesh):
    return jax.shard_map(
        functools.partial(per_device, mesh.shape["tp"], mesh.shape["kv"]),
        mesh=mesh,
        in_specs=(
            P("grp", "tp"),
            P(None, "tp"),
            P("tp", "kv", None),
            P("tp", "kv", None),
            P("kv", "tp"),
            P("tp", None, "kv"),
            P("kv", "tp"),
            P(("grp", "tp"), None, "kv", None),
            P("grp"),
            P("grp"),
        ),
        out_specs=(P("grp", "tp"), P("grp", "tp"), P(("grp", "tp"), "kv", None)),
        check_vma=False,
    )
```

```python
import functools
import math

import jax
import jax.numpy as jnp
import numpy as np
from jax import lax
from jax.experimental import pallas as pl
from jax.experimental.pallas import tpu as pltpu
from jax.sharding import PartitionSpec as P

D = 8192
EPS = 1e-05
ROPE_BASE = 500000.0
LANES = 128
MIB = 1 << 20
COPY_ROWS = 4096
DOWN_ROWS = 1024
GU_SHARES = (4, 6, 4, 3, 4, 4, 3)
F32 = jnp.float32
BF16 = jnp.bfloat16
QUARTER = (1.5703125, 4.837512969970703125e-4, 7.549789948768648e-8)
SIN = (-1.9515295891e-4, 8.3321608736e-3, -1.6666654611e-1)
COS = (2.443315711809948e-5, -1.388731625493765e-3, 4.166664568298827e-2)


def vmem():
    return pl.BlockSpec(memory_space=pltpu.VMEM)


def hbm():
    return pl.BlockSpec(memory_space=pltpu.HBM)


def in_hbm(array):
    return pltpu.with_memory_space_constraint(array, pltpu.HBM)


def exchange(arrays, axis, size):
    return [arrays[0]] + [
        lax.ppermute(arrays[s], axis, [(i, i ^ s) for i in range(size)])
        for s in range(1, size)
    ]


def tree_sum(parts):
    while len(parts) > 1:
        parts = [a + b for a, b in zip(parts[::2], parts[1::2])]
    return parts[0]


def two_parts(scaled):
    high = scaled.astype(BF16).astype(F32)
    return high, scaled - high


def spread(rows16, out_ref, docs):
    width = rows16.shape[1]
    pick = one_hot_spread(2)
    row = lax.broadcasted_iota(jnp.int32, (4 * docs, 2 * LANES), 0)
    lane = lax.broadcasted_iota(jnp.int32, (4 * docs, 2 * LANES), 1)
    keep = (lax.shift_right_logical(row, docs.bit_length() - 1) & 1) == (lane & 1)
    chunks = width // LANES
    stacked = jnp.concatenate(
        [rows16[:, c * LANES : (c + 1) * LANES] for c in range(chunks)], axis=0
    )
    doubled = jnp.dot(stacked, pick, preferred_element_type=F32)
    for c in range(chunks):
        piece = doubled[c * 4 * docs : (c + 1) * 4 * docs]
        out_ref[:, 2 * c * LANES : 2 * (c + 1) * LANES] = jnp.where(keep, piece, 0.0).astype(BF16)


def start_all(copies):
    for copy in copies:
        copy.start(priority=1)


def matrix_of(w):
    return w if len(w.shape) == 2 else w.reshape(w.shape[0] * w.shape[1], w.shape[2])


def block_copies(matrix, first, buf, sems):
    rows, columns = buf.shape
    chunk = min(rows, COPY_ROWS)
    return [
        pltpu.make_async_copy(
            matrix.at[pl.ds(start, chunk), pl.ds(first * LANES, columns)],
            buf.at[pl.ds(start, chunk)],
            sems.at[start // chunk],
        )
        for start in range(0, rows, chunk)
    ]


def pick_doc(value, doc, docs):
    axis = value.ndim - 2
    row = lax.broadcasted_iota(jnp.int32, value.shape, axis)
    return jnp.sum(jnp.where(row & (docs - 1) == doc, value, 0.0), axis=axis)


def sine_cosine(angle):
    turns = jnp.floor(angle * (2.0 / math.pi) + 0.5)
    rest = ((angle - turns * QUARTER[0]) - turns * QUARTER[1]) - turns * QUARTER[2]
    square = rest * rest
    sine = rest + rest * square * ((SIN[0] * square + SIN[1]) * square + SIN[2])
    cosine = 1.0 - 0.5 * square + square * square * (
        (COS[0] * square + COS[1]) * square + COS[2]
    )
    quadrant = turns - 4.0 * jnp.floor(turns * 0.25)
    odd = (quadrant == 1.0) | (quadrant == 3.0)
    sine, cosine = jnp.where(odd, cosine, sine), jnp.where(odd, sine, cosine)
    return (
        jnp.where(quadrant >= 2.0, -sine, sine),
        jnp.where((quadrant == 1.0) | (quadrant == 2.0), -cosine, cosine),
    )


def rope_rows(length, frequency):
    sine, cosine = sine_cosine(length * frequency)
    lane = lax.broadcasted_iota(jnp.int32, (1, LANES), 1)
    return cosine, jnp.where(lane < LANES // 2, -sine, sine)


def one_hot_spread(fold):
    source = lax.broadcasted_iota(jnp.int32, (LANES, fold * LANES), 0)
    target = lax.broadcasted_iota(jnp.int32, (LANES, fold * LANES), 1)
    return (lax.shift_right_logical(target, fold.bit_length() - 1) == source).astype(F32).astype(BF16)


def spread_heads(rows, out_ref, heads):
    count, width = rows.shape
    chunks = width // LANES
    stacked = jnp.concatenate([rows[:, c * LANES : (c + 1) * LANES] for c in range(chunks)], axis=0)
    wide = jnp.dot(stacked.astype(BF16), one_hot_spread(heads), preferred_element_type=F32)
    columns = heads * LANES
    lane = lax.broadcasted_iota(jnp.int32, (count, columns), 1) & (heads - 1)
    for c in range(chunks):
        piece = wide[c * count : (c + 1) * count]
        for h in range(0, heads, 2):
            pair = [jnp.where(lane == h + i, piece, 0.0) for i in range(2)]
            out_ref[h * count : (h + 2) * count, c * columns : (c + 1) * columns] = (
                jnp.concatenate(pair, axis=0).astype(BF16)
            )


def qkv_kernel(tp, owner_hbm, lengths_hbm, frequency_hbm, states_hbm, gains_hbm, wq, wkv, *rest):
    outs = rest[:tp]
    table, places = rest[tp : tp + 2]
    owner, lengths, frequency, states, gains = rest[tp + 2 : tp + 7]
    wq_buf, wkv_buf, spread_buf, sems, small_sems = rest[tp + 7 :]
    docs, width = states.shape
    heads = wq.shape[0] // width
    parts = wq_buf.shape[0]
    rows = wq_buf.shape[1]
    small = [
        pltpu.make_async_copy(source, target, small_sems.at[i])
        for i, (source, target) in enumerate(
            [
                (states_hbm, states),
                (gains_hbm, gains),
                (owner_hbm, owner),
                (lengths_hbm, lengths),
                (frequency_hbm, frequency),
            ]
        )
    ]
    copies = [
        pltpu.make_async_copy(wq.at[pl.ds(c * rows, rows)], wq_buf.at[c], sems.at[c])
        for c in range(parts)
    ]
    kv_copy = pltpu.make_async_copy(wkv, wkv_buf, sems.at[parts])
    for copy in small:
        copy.start()
    start_all([kv_copy] + copies)
    for copy in small:
        copy.wait()
    me = lax.axis_index("tp")
    x = states[...].astype(F32)
    squares = jnp.broadcast_to(jnp.sum(x * x, axis=1, keepdims=True), (docs, LANES))
    both = jnp.concatenate(two_parts(x * gains[0:1, :]), axis=0)
    kv_copy.wait()
    kv_total = jnp.dot(both.astype(BF16), wkv_buf[...], preferred_element_type=F32)
    spread_heads(both, spread_buf, heads)
    length = lengths[owner[me]].astype(F32)
    cosine, sine = rope_rows(length, frequency[...])
    table[0:1, :] = cosine
    table[1:2, :] = sine
    table[2:3, :] = jnp.full((1, LANES), length, F32)
    table[3:, :] = jnp.zeros((table.shape[0] - 3, LANES), F32)
    for s in range(tp):
        places[s : s + 1, :] = jnp.full((1, LANES), owner[me ^ s], jnp.int32)
    total = jnp.zeros((heads * 2 * docs, LANES), F32)
    for c in range(parts):
        copies[c].wait()
        total = total + jnp.dot(
            spread_buf[:, c * rows : (c + 1) * rows], wq_buf[c], preferred_element_type=F32
        )
    total = total.reshape(heads, 2 * docs, LANES)
    for s in range(tp):
        doc = owner[me ^ s]
        out = outs[s]
        out[:heads, :] = pick_doc(total, doc, docs)
        kv_row = pick_doc(kv_total, doc, docs)[None]
        out[heads : heads + 1, :] = kv_row[:, :LANES]
        out[heads + 1 : heads + 2, :] = kv_row[:, LANES:]
        out[heads + 2 : heads + 3, :] = pick_doc(squares, doc, docs)[None]
        out[heads + 3 :, :] = jnp.zeros((out.shape[0] - heads - 3, LANES), F32)


def attend_kernel(tp, heads, rows, first, table, cache, w, *rest):
    parts = rest[:tp]
    heads_out, new_kv_out, w_ready, scores, new_kv, w_sems, out_sem = rest[-7:]
    w_copies = block_copies(matrix_of(w), first, w_ready, w_sems)
    start_all(w_copies)
    blocks = cache.shape[0] // rows
    sums = tree_sum([part[...] for part in parts])
    sums = sums * lax.rsqrt(sums[heads + 2 : heads + 3, :] / D + EPS)
    rotated = sums * table[0:1, :] + pltpu.roll(sums, LANES // 2, 1) * table[1:2, :]
    query = rotated[:heads].astype(BF16)
    key = rotated[heads : heads + 1].astype(BF16)
    value = sums[heads + 1 : heads + 2].astype(BF16)
    new_kv[:, :LANES] = key
    new_kv[:, LANES:] = value
    out_copy = pltpu.make_async_copy(new_kv, new_kv_out, out_sem.at[0])
    out_copy.start()
    key = key.astype(F32)
    value = value.astype(F32)
    scale = LANES ** (-0.5)
    own = jnp.sum(query.astype(F32) * key, axis=1, keepdims=True) * scale
    column = lax.broadcasted_iota(jnp.int32, (heads, LANES), 1).astype(F32)
    length = table[2:3, :]
    tops = jnp.full((heads, LANES), -jnp.inf, F32)
    for b in range(blocks):
        block = lax.dot_general(
            query,
            cache[b * rows : (b + 1) * rows, :LANES],
            (((1,), (1,)), ((), ())),
            preferred_element_type=F32,
        )
        for start in range(0, rows, LANES):
            at = b * rows + start
            piece = block[:, start : start + LANES] * scale
            piece = jnp.where(column < length - at, piece, -jnp.inf)
            tops = jnp.maximum(tops, piece)
            scores[:, at : at + LANES] = piece
    top = jnp.maximum(jnp.max(tops, axis=1, keepdims=True), own)
    own = jnp.exp(own - top)
    sums_by_lane = jnp.zeros((heads, LANES), F32)
    acc = own.astype(BF16).astype(F32) * value
    for b in range(blocks):
        weights = jnp.exp(scores[:, b * rows : (b + 1) * rows] - top)
        for start in range(0, rows, LANES):
            sums_by_lane = sums_by_lane + weights[:, start : start + LANES]
        acc = acc + jnp.dot(
            weights.astype(BF16),
            cache[b * rows : (b + 1) * rows, LANES:],
            preferred_element_type=F32,
        )
    total = own + jnp.sum(sums_by_lane, axis=1, keepdims=True)
    heads_out[...] = (acc / total).astype(BF16)
    for copy in w_copies:
        copy.wait()
    out_copy.wait()


def out_kernel(tp, places, w_out, *rest):
    parts = rest[:tp]
    out, left = rest[-2:]
    docs = out.shape[0]
    row = lax.broadcasted_iota(jnp.int32, (left.shape[0], LANES), 0)
    own = [parts[s][...].astype(F32) for s in range(tp)]
    for h in range(own[0].shape[0]):
        piece = jnp.zeros((left.shape[0], LANES), F32)
        for s in range(tp):
            piece = jnp.where(row == places[s : s + 1, :], own[s][h : h + 1, :], piece)
        left[:, h * LANES : (h + 1) * LANES] = piece
    terms = jnp.dot(left[...].astype(BF16), w_out[...], preferred_element_type=F32)
    out[...] = terms[:docs].astype(BF16)


def fetch_kernel(first, token, w, *rest):
    out, sems = rest[-2:]
    copies = block_copies(matrix_of(w), first, out, sems)
    start_all(copies)
    for copy in copies:
        copy.wait()


def gate_up_kernel(kv, groups, first, states, gains, w, *rest):
    ready, parts = rest[:groups], rest[groups : groups + kv]
    attn_out, partial_out, *blocks, spread_buf, attn_buf, w_sems, out_sem = rest[groups + kv :]
    docs, width = states.shape
    hidden = w.shape[2]
    w_matrix = matrix_of(w)
    copies = []
    for i, block in enumerate(blocks):
        copies.append(block_copies(w_matrix, first, block, w_sems.at[i]))
        first += block.shape[1] // LANES
        start_all(copies[-1])
    attn = tree_sum([part[...].astype(F32) for part in parts]).astype(BF16)
    attn_buf[...] = attn
    out_copy = pltpu.make_async_copy(attn_buf, attn_out, out_sem.at[0])
    out_copy.start()
    resid = (states[...].astype(F32) + attn.astype(F32)).astype(BF16).astype(F32)
    squares = jnp.sum(resid * resid, axis=1, keepdims=True)
    high, low = two_parts(resid * gains[1:2, :])
    spread(jnp.concatenate([high, high, low, low], axis=0).astype(BF16), spread_buf, docs)

    lane = lax.broadcasted_iota(jnp.int32, (docs, LANES), 1)
    first = squares.astype(BF16).astype(F32)
    second = (squares - first).astype(BF16).astype(F32)
    third = squares - first - second
    terms = jnp.where(lane == 0, first, jnp.where(lane == 1, second, jnp.where(lane == 2, third, 0.0)))
    partial_out[:, hidden:] = jnp.concatenate([terms, terms], axis=0).astype(BF16)
    at = 0
    for i, block in enumerate([*ready, *blocks]):
        if i >= groups:
            for copy in copies[i - groups]:
                copy.wait()
        product = jnp.dot(spread_buf[...], block[...], preferred_element_type=F32)
        columns = slice(at, at + block.shape[1])
        partial_out[:, columns] = (product[: 2 * docs] + product[2 * docs :]).astype(BF16)
        at += block.shape[1]
    out_copy.wait()


def down_kernel(tp, w_down, *rest):
    parts, out = rest[:tp], rest[tp]
    docs, width = out.shape
    hidden = w_down.shape[0]

    def summed(start, size):
        return tree_sum([part[:, start : start + size].astype(F32) for part in parts])

    squares = jnp.sum(summed(hidden, LANES)[:docs], axis=1, keepdims=True)
    inverse = lax.rsqrt(squares / D + EPS)
    total = jnp.zeros((docs, width), F32)
    for start in range(0, hidden, DOWN_ROWS):
        size = min(DOWN_ROWS, hidden - start)
        both = summed(start, size)
        gate = both[:docs] * inverse
        up = both[docs:] * inverse
        act = (gate / (1.0 + jnp.exp(-gate)) * up).astype(BF16)
        total = total + jnp.dot(
            act, w_down[start : start + size, :], preferred_element_type=F32
        )
    out[...] = total.astype(BF16)


def cost(micros):
    return pl.CostEstimate(flops=0, bytes_accessed=int(micros * 3.69e6), transcendentals=0)


def params(docs, mib):
    return pltpu.CompilerParams(vmem_limit_bytes=(mib if docs <= 8 else mib + 24) * MIB)


def per_device(
    tp, kv,
    states, norm_gains, w_query, w_keyval, w_out, w_gate_up, w_down, kv_cache, lengths, owner_rows
):
    docs, width = states.shape
    heads = w_query.shape[1]
    cache_len = kv_cache.shape[1]
    hidden = w_gate_up.shape[2]
    wq = w_query.reshape(width * heads, LANES)
    wkv = w_keyval.reshape(width, 2 * LANES)
    cache = kv_cache.reshape(cache_len, 2 * LANES)
    packed = 2 * heads
    wq_parts = 8

    half = LANES // 2
    freq = ROPE_BASE ** (-(np.arange(half, dtype=np.float64) * 2.0 / LANES))
    freq = jnp.asarray(np.concatenate([freq, freq]).astype(np.float32)[None, :])
    *qkv_parts, table, places = pl.pallas_call(
        functools.partial(qkv_kernel, tp),
        out_shape=[jax.ShapeDtypeStruct((packed, LANES), F32)] * tp
        + [
            jax.ShapeDtypeStruct((8, LANES), F32),
            jax.ShapeDtypeStruct((max(tp, 8), LANES), jnp.int32),
        ],
        in_specs=[hbm()] * 7,
        out_specs=[vmem()] * (tp + 2),
        scratch_shapes=[
            pltpu.SMEM((docs,), jnp.int32),
            pltpu.SMEM((docs,), jnp.int32),
            pltpu.VMEM((1, LANES), F32),
            pltpu.VMEM((docs, width), BF16),
            pltpu.VMEM((2, width), F32),
            pltpu.VMEM((wq_parts, width * heads // wq_parts, LANES), BF16),
            pltpu.VMEM((width, 2 * LANES), BF16),
            pltpu.VMEM((heads * 2 * docs, width * heads), BF16),
            pltpu.SemaphoreType.DMA((wq_parts + 1,)),
            pltpu.SemaphoreType.DMA((5,)),
        ],
        compiler_params=params(docs, 10),
        cost_estimate=cost(8),
        name="qkv",
    )(*(in_hbm(a) for a in (owner_rows, lengths, freq, states, norm_gains, wq, wkv)))
    w_gu = in_hbm(w_gate_up)
    bounds = np.cumsum([0] + [hidden // LANES * n // 28 for n in GU_SHARES]).tolist()
    shares = list(zip(bounds, bounds[1:]))
    fetched = []

    chunks = max(2 * width // COPY_ROWS, 1)

    def block_of(share):
        return pltpu.VMEM((2 * width, (share[1] - share[0]) * LANES), BF16)

    def fetch(share, token, *keep):
        return pl.pallas_call(
            functools.partial(fetch_kernel, share[0]),
            out_shape=block_of(share),
            in_specs=[hbm(), hbm()] + [vmem()] * len(keep),
            out_specs=vmem(),
            scratch_shapes=[pltpu.SemaphoreType.DMA((chunks,))],
            compiler_params=params(docs, 2),
            cost_estimate=cost(0.3 * (share[1] - share[0])),
            name="fetch",
        )(token, w_gu, *keep)

    fetched.append(fetch(shares[0], table, cache))
    qkv_parts = exchange(qkv_parts, "tp", tp)[::-1]
    head_out, new_kv, w_ready = pl.pallas_call(
        functools.partial(attend_kernel, tp, heads, 512, shares[1][0]),
        out_shape=[
            jax.ShapeDtypeStruct((heads, LANES), BF16),
            jax.ShapeDtypeStruct((1, 2 * LANES), BF16),
            block_of(shares[1]),
        ],
        in_specs=[vmem(), vmem(), hbm()] + [vmem()] * tp + [hbm()] * len(fetched),
        out_specs=[vmem(), hbm(), vmem()],
        scratch_shapes=[
            pltpu.VMEM((heads, cache_len), F32),
            pltpu.VMEM((1, 2 * LANES), BF16),
            pltpu.SemaphoreType.DMA((chunks,)),
            pltpu.SemaphoreType.DMA((1,)),
        ],
        compiler_params=params(docs, 6),
        cost_estimate=cost(8),
        name="attend",
    )(table, cache, w_gu, *qkv_parts, *fetched)
    fetched.append(w_ready)

    fetched.append(fetch(shares[2], head_out))
    head_parts = exchange([head_out] * tp, "tp", tp)
    out_part = pl.pallas_call(
        functools.partial(out_kernel, tp),
        out_shape=jax.ShapeDtypeStruct((docs, width), BF16),
        in_specs=[vmem()] * (tp + 2) + [hbm()],
        out_specs=vmem(),
        scratch_shapes=[pltpu.VMEM((max(docs, 8), heads * LANES), F32)],
        compiler_params=params(docs, 6),
        cost_estimate=cost(6),
        name="attn_project",
    )(places, w_out, *head_parts, fetched[-1])

    fetched.append(fetch(shares[3], out_part, w_down))
    out_parts = exchange([out_part] * kv, "kv", kv)
    attn_out, gu_part = pl.pallas_call(
        functools.partial(gate_up_kernel, kv, len(fetched), shares[4][0]),
        out_shape=[
            jax.ShapeDtypeStruct((docs, width), BF16),
            jax.ShapeDtypeStruct((2 * docs, hidden + LANES), BF16),
        ],
        in_specs=[vmem(), vmem(), hbm()] + [vmem()] * (len(fetched) + kv),
        out_specs=[hbm(), vmem()],
        scratch_shapes=[
            *(block_of(share) for share in shares[4:]),
            pltpu.VMEM((4 * docs, 2 * width), BF16),
            pltpu.VMEM((docs, width), BF16),
            pltpu.SemaphoreType.DMA((len(shares) - 4, chunks)),
            pltpu.SemaphoreType.DMA((1,)),
        ],
        compiler_params=params(docs, 19),
        cost_estimate=cost(10),
        name="gate_up",
    )(states, norm_gains, w_gu, *fetched, *out_parts)

    gu_parts = exchange([gu_part] * tp, "tp", tp)
    ffn_part = pl.pallas_call(
        functools.partial(down_kernel, tp),
        out_shape=jax.ShapeDtypeStruct((docs, width), BF16),
        in_specs=[vmem()] * (1 + tp),
        out_specs=vmem(),
        compiler_params=params(docs, 6),
        cost_estimate=cost(5),
        name="down",
    )(w_down, *gu_parts)
    ffn_parts = exchange([ffn_part] * kv, "kv", kv)
    ffn_out = tree_sum([part.astype(F32) for part in ffn_parts]).astype(BF16)
    return attn_out, ffn_out, new_kv.reshape(1, 1, 2 * LANES)


def solution(mesh):
    return jax.shard_map(
        functools.partial(per_device, mesh.shape["tp"], mesh.shape["kv"]),
        mesh=mesh,
        in_specs=(
            P("grp", "tp"),
            P(None, "tp"),
            P("tp", "kv", None),
            P("tp", "kv", None),
            P("kv", "tp"),
            P("tp", None, "kv"),
            P("kv", "tp"),
            P(("grp", "tp"), None, "kv", None),
            P("grp"),
            P("grp"),
        ),
        out_specs=(P("grp", "tp"), P("grp", "tp"), P(("grp", "tp"), "kv", None)),
        check_vma=False,
    )
```
